32 devices in a mesh: dp: 2 (over core), seq: 16 (over z, y, x).
Axes of the slice: x: 2, y: 2, z: 4, core: 2. Of those that a mesh axis runs over, the one named last changes fastest.
Arguments:
- hidden_in: bfloat16 [2, 2048, 960], P('dp', 'seq'), may hold values from -6 to 6
- segment_ids: int32 [2, 2048], P('dp', 'seq'), may hold values from 0 to 7, never falling along the last dimension, each value on 1 to 1536 neighbouring positions
- route_mask: int32 [2, 2048], P('dp', 'seq'), may hold values 0 or 1
- valid_mask: int32 [2, 2048], P('dp', 'seq'), may hold values from 0 to 1, as said below
- teacher: bfloat16 [2, 2048, 960], P('dp', 'seq'), may hold values from -24 to 24
- norm_gain: bfloat16 [960], P('seq'), may hold values from 0.5 to 1.5
- w_query: bfloat16 [960, 960], P('seq', 'dp'), may hold values from -0.1875 to 0.1875
- w_key: bfloat16 [960, 320], P('seq', 'dp'), may hold values from -0.1875 to 0.1875
- w_value: bfloat16 [960, 320], P('seq', 'dp'), may hold values from -0.1875 to 0.1875
- w_out: bfloat16 [960, 960], P('seq', 'dp'), may hold values from -0.75 to 0.75
- ffn_gain: bfloat16 [960], P('seq'), may hold values from 0.5 to 1.5
- w_gate: bfloat16 [960, 2560], P('seq', 'dp'), may hold values from -0.1875 to 0.1875
- w_up: bfloat16 [960, 2560], P('seq', 'dp'), may hold values from -0.1875 to 0.1875
- w_down: bfloat16 [2560, 960], P('seq', 'dp'), may hold values from -0.125 to 0.125
- router_weight: bfloat16 [960], P('seq'), may hold values from -0.1875 to 0.1875
Outputs:
- outputs: bfloat16 [2, 2048, 960], P('dp', 'seq')
- loss: float32 [], replicated
- grad_input: bfloat16 [2, 2048, 960], P('dp', 'seq')
- grad_norm_gain: float32 [960], P('seq')
- grad_query: float32 [960, 960], P('seq', 'dp')
- grad_key: float32 [960, 320], P('seq', 'dp')
- grad_value: float32 [960, 320], P('seq', 'dp')
- grad_out: float32 [960, 960], P('seq', 'dp')
- grad_ffn_gain: float32 [960], P('seq')
- grad_gate: float32 [960, 2560], P('seq', 'dp')
- grad_up: float32 [960, 2560], P('seq', 'dp')
- grad_down: float32 [2560, 960], P('seq', 'dp')
- grad_router: float32 [960], P('seq')
The draws below stay inside these ranges and needn't reach their ends.
Inputs may be any that keep to these rules, and one draw needn't show every extreme that they name: `segment_ids`: within a sequence segment numbers never fall; each of the 8 documents holds 1 to 1536 tokens. `valid_mask`: in each sequence the valid tokens form a prefix of 1024 tokens or more.
All inputs are finite; a program needn't handle non-finite values. No bound on the sum of `route_mask` on one device may be relied on, other than what follows from the above.
Results may differ from the reference program's by a relative error of at most 0.018.
Values may be sent and summed in bfloat16 or wider, within the bound.
A program may use at most 256 MiB of HBM per device.

```python
import math
import jax
import jax.numpy as jnp
import numpy as np
from jax import lax

D = 960
FF = 2560
HEADS = 15
KV_HEADS = 5
HEAD_DIM = 64
LENGTH = 2048
SEQS_ALL = 2
DOCS = 8
DOC_MOST = 1536


def draw_valid_mask(key, part):
    fill_to = jax.random.randint(key, (SEQS_ALL, 1), LENGTH // 2, LENGTH + 1, dtype=jnp.int32)
    places = jnp.arange(LENGTH, dtype=jnp.int32)[None, :]
    return (places < fill_to).astype(jnp.int32)


def draw_teacher(key, part):
    places = jnp.arange(LENGTH, dtype=jnp.float32) / LENGTH
    growth = 1.0 + 2.0 * places
    sample = jnp.clip(jax.random.normal(key, (SEQS_ALL, LENGTH, D), jnp.float32), -8.0, 8.0)
    return (sample * growth[None, :, None]).astype(jnp.bfloat16)


def set_ends(values, own_key, low, largest):
    longest = values.shape.index(max(values.shape))
    spots = []
    for shift in (0, 1):
        where = [jax.random.randint(jax.random.fold_in(own_key, axis), (), 0, length) for axis, length in enumerate(values.shape)]
        where[longest] = (where[longest] + shift) % values.shape[longest]
        spots.append(tuple(where))
    return values.at[spots[0]].set(low).at[spots[1]].set(largest)


def shard_levels(own_key, extent, shards, smallest, largest):
    gain, own = 1.0, jax.random.fold_in(own_key, 6)
    for position, parts in shards:
        steps = jnp.exp(jax.random.uniform(jax.random.fold_in(own, position), (parts,), jnp.float32, smallest / len(shards), largest / len(shards)))
        gain = gain * jnp.repeat(steps, extent[position] // parts).reshape([-1 if axis == position else 1 for axis in range(len(extent))])
    return gain


def length_profile(number_of, total, most, slope):
    portions = [(1 << 20) // math.isqrt(grade ** slope) + 1 for grade in range(2, number_of + 1)]
    spare, counts = total - most - (number_of - 1), [1] * (number_of - 1)
    while spare > 0:
        candidates = [i for i in range(number_of - 1) if counts[i] < most]
        pool, budget = sum([portions[i] for i in candidates]), spare
        for i in candidates:
            addition = min(most - counts[i], max(1, budget * portions[i] // pool), spare)
            counts[i] = counts[i] + addition
            spare = spare - addition
    return np.array([most] + counts)


def ragged(own_key, number_of, total, reach, lean):
    if number_of == 2:
        one = jax.random.randint(own_key, (), max(1, total - reach), min(reach, total - 1) + 1)
        return jnp.stack([one, total - one])
    sizes = jnp.asarray(length_profile(number_of, total, reach, lean), jnp.int32)
    pairs = (number_of - 1) // 2
    source_of, sink = sizes[1:1 + 2 * pairs:2], sizes[2:2 + 2 * pairs:2]
    room = jnp.minimum(source_of - 1, reach - sink)
    shifted = jax.random.randint(jax.random.fold_in(own_key, 1), (pairs,), 0, 1 << 20) % (room + 1)
    sizes = sizes.at[1:1 + 2 * pairs:2].set(source_of - shifted).at[2:2 + 2 * pairs:2].set(sink + shifted)
    return sizes[jax.random.permutation(jax.random.fold_in(own_key, 2), number_of)]


def noise(rng, dims, deviation, limit, shards=(), kind=jnp.bfloat16):
    values = jax.random.normal(rng, dims, jnp.float32) * deviation
    if len(shards) > 0:
        values = shard_levels(rng, dims, shards, -0.22, 0.18) * values
    return jnp.clip(values, min=-limit, max=limit).astype(kind)


def setup_inputs(seed: int = 0) -> dict:
    key_list = jax.random.split(jax.random.key(seed), 16)
    return {
        "hidden_in": noise(key_list[0], (SEQS_ALL, LENGTH, D), 1.0, 6.0, ((0, 2), (1, 16))),
        "segment_ids": jax.vmap(lambda own: jnp.searchsorted(jnp.cumsum(ragged(own, DOCS, LENGTH, DOC_MOST, 2)), jnp.arange(LENGTH), side="right"))(jax.random.split(key_list[1], SEQS_ALL)).reshape((SEQS_ALL, LENGTH)).astype(jnp.int32),
        "route_mask": set_ends((jax.random.randint(key_list[2], (SEQS_ALL, LENGTH), 0, 3) < 2).astype(jnp.int32), jax.random.fold_in(key_list[2], 1), 0, 1),
        "valid_mask": draw_valid_mask(jax.random.fold_in(key_list[15], 71), 0),
        "teacher": draw_teacher(jax.random.fold_in(key_list[15], 71), 0),
        "norm_gain": jnp.clip(1.0 + 0.1 * jax.random.normal(key_list[5], (D,), jnp.float32), 0.5, 1.5).astype(jnp.bfloat16),
        "w_query": noise(key_list[6], (D, HEADS * HEAD_DIM), D ** -0.5, 0.1875, ((0, 16), (1, 2))),
        "w_key": noise(key_list[7], (D, KV_HEADS * HEAD_DIM), D ** -0.5, 0.1875, ((0, 16), (1, 2))),
        "w_value": noise(key_list[8], (D, KV_HEADS * HEAD_DIM), D ** -0.5, 0.1875, ((0, 16), (1, 2))),
        "w_out": noise(key_list[9], (HEADS * HEAD_DIM, D), (HEADS * HEAD_DIM // 16) ** -0.5, 0.75, ((0, 16), (1, 2))),
        "ffn_gain": jnp.clip(1.0 + 0.1 * jax.random.normal(key_list[10], (D,), jnp.float32), 0.5, 1.5).astype(jnp.bfloat16),
        "w_gate": noise(key_list[11], (D, FF), D ** -0.5, 0.1875, ((0, 16), (1, 2))),
        "w_up": noise(key_list[12], (D, FF), D ** -0.5, 0.1875, ((0, 16), (1, 2))),
        "w_down": noise(key_list[13], (FF, D), FF ** -0.5, 0.125, ((0, 16), (1, 2))),
        "router_weight": noise(key_list[14], (D,), D ** -0.5, 0.1875, ((0, 16),)),
    }


norm_eps = 1e-05
masked_score = -1e+30
highest = lax.Precision.HIGHEST

@jax.custom_vjp
def low(v):
    return lax.optimization_barrier(v.astype(jnp.bfloat16)).astype(jnp.float32)

@jax.custom_vjp
def low_back(v):
    return v

def low_keep(v):
    return (low(v), None)

def low_pass(kept, grad):
    return (grad,)

def back_keep(v):
    return (v, None)

def back_low(kept, grad):
    return (low(grad),)
low.defvjp(low_keep, low_pass)
low_back.defvjp(back_keep, back_low)

def rotary_tables(places, head_dim):
    half_dim = head_dim // 2
    inv_freq = jnp.exp(jnp.arange(half_dim, dtype=jnp.float32) * (-math.log(10000.0) / half_dim))
    angles = places[:, None] * inv_freq[None, :]
    return (jnp.cos(angles), jnp.sin(angles))

def rotate(tensor, cosine, sine_tab):
    half_dim = tensor.shape[-1] // 2
    first_half = tensor[..., :half_dim]
    second = tensor[..., half_dim:]
    cos_wide = cosine[:, None, :]
    sin_wide = sine_tab[:, None, :]
    return jnp.concatenate([first_half * cos_wide - second * sin_wide, second * cos_wide + first_half * sin_wide], axis=-1)

def matmul(left, right):
    return jnp.dot(left, right, precision=highest, preferred_element_type=jnp.float32)

def rms_scale(tensor):
    return lax.rsqrt(lax.optimization_barrier(jnp.mean(tensor * tensor, axis=-1, keepdims=True)) + norm_eps)

def attention(queries, key_rows, value_rows, segment, route_row):
    length = queries.shape[0]
    key_block = min(512, length)
    blocks = length // key_block
    places = jnp.arange(length, dtype=jnp.int32)
    grouped = queries.reshape(blocks, key_block, KV_HEADS, HEADS // KV_HEADS, HEAD_DIM)
    starts = jnp.arange(blocks, dtype=jnp.int32) * key_block

    def one_block(items):
        query_block, first_row = items
        rowpos = first_row + jnp.arange(key_block, dtype=jnp.int32)
        rowseg = lax.dynamic_slice_in_dim(segment, first_row, key_block)
        raw_scores = jnp.einsum('qkgd,pkd->kgqp', query_block, key_rows, precision=highest) * HEAD_DIM ** (-0.5)
        raw_scores = low_back(raw_scores)
        allowed = (rowseg[:, None] == segment[None, :]) & (places[None, :] <= rowpos[:, None]) & ((route_row[None, :] == 1) | (places[None, :] == rowpos[:, None]))
        scores = jnp.where(allowed[None, None], raw_scores, masked_score)
        softmax_w = jax.nn.softmax(scores, axis=-1)
        mixed_out = jnp.einsum('kgqp,pkd->qkgd', low(softmax_w), value_rows, precision=highest)
        return mixed_out.reshape(key_block, HEADS * HEAD_DIM)
    outcome = lax.map(jax.checkpoint(one_block), (grouped, starts))
    return outcome.reshape(length, HEADS * HEAD_DIM)

def block_forward(params, hidden, segment, route_row, cosine, sine_tab):
    gain_one, wq_full, wk_full, wv_full, wo_full, gain_two, wg_full, wu_full, wd_full, router_full = params
    length = hidden.shape[0]
    normed = low(hidden * rms_scale(hidden) * gain_one)
    q_pre = low_back(matmul(normed, wq_full)).reshape(length, HEADS, HEAD_DIM)
    queries = low(rotate(q_pre, cosine, sine_tab))
    k_pre = low_back(matmul(normed, wk_full)).reshape(length, KV_HEADS, HEAD_DIM)
    key_rows = low(rotate(k_pre, cosine, sine_tab))
    value_rows = low(low_back(matmul(normed, wv_full))).reshape(length, KV_HEADS, HEAD_DIM)
    context = low_back(low(attention(queries, key_rows, value_rows, segment, route_row)))
    attn_out = low_back(matmul(context, wo_full))
    residual = hidden + attn_out
    normed2 = low(residual * rms_scale(residual) * gain_two)
    gate_pre = low_back(matmul(normed2, wg_full))
    up_pre = low_back(matmul(normed2, wu_full))
    activated = low(jax.nn.silu(gate_pre) * up_pre)
    ffn_out = low_back(matmul(activated, wd_full))
    logit = jnp.dot(hidden, router_full, precision=highest)
    mix_rate = route_row.astype(jnp.float32) * jax.nn.sigmoid(logit)
    return hidden + mix_rate[:, None] * (attn_out + ffn_out)

def reference(hidden_in, segment_ids, route_mask, valid_mask, teacher, norm_gain, w_query, w_key, w_value, w_out, ffn_gain, w_gate, w_up, w_down, router_weight):
    params = tuple((weight.astype(jnp.float32) for weight in (norm_gain, w_query, w_key, w_value, w_out, ffn_gain, w_gate, w_up, w_down, router_weight)))
    tok_count = jnp.sum(valid_mask.astype(jnp.float32))
    places = jnp.arange(LENGTH, dtype=jnp.float32)
    cosine, sine_tab = rotary_tables(places, HEAD_DIM)

    def per_sequence(running, items):
        hidden, segment, route_row, valid_row, target = items
        hidden = hidden.astype(jnp.float32)
        target = target.astype(jnp.float32)

        def objective(hidden_val, param_val):
            state = block_forward(param_val, hidden_val, segment, route_row, cosine, sine_tab)
            sq_error = jnp.sum(valid_row.astype(jnp.float32)[:, None] * (state - target) ** 2) / (D * tok_count)
            return (sq_error, state)
        sq_error, pullback, state = jax.vjp(objective, hidden, params, has_aux=True)
        grad_hidden, grad_params = pullback(jnp.ones_like(sq_error))
        loss_sum, grad_sums = running
        grad_sums = jax.tree.map(jnp.add, grad_sums, grad_params)
        return ((loss_sum + sq_error, grad_sums), (state.astype(jnp.bfloat16), grad_hidden.astype(jnp.bfloat16)))
    zero_sums = jax.tree.map(jnp.zeros_like, params)
    (loss_value, grad_sums), (outputs, grad_in) = lax.scan(per_sequence, (jnp.zeros((), jnp.float32), zero_sums), (hidden_in, segment_ids, route_mask, valid_mask, teacher))
    return (outputs, loss_value, grad_in, grad_sums[0], grad_sums[1], grad_sums[2], grad_sums[3], grad_sums[4], grad_sums[5], grad_sums[6], grad_sums[7], grad_sums[8], grad_sums[9])
```

```python
import functools
import math

import jax
import jax.numpy as jnp
from jax import lax
from jax.experimental import pallas as pl
from jax.experimental.pallas import tpu as pltpu
from jax.sharding import PartitionSpec as P

HEADS = 15
KV_HEADS = 5
HEAD_DIM = 64
GROUPS = HEADS // KV_HEADS
LANES = 128

norm_eps = 1e-05
masked_score = -1e30

MESH = pl.DeviceIdType.MESH
VMEM_LIMIT = 62 * 2**20

ORDERS = {"A": (2, 0, 1), "B": (1, 0, 2), "C": (0, 2, 1), "D": (0, 1, 2)}


def round_up(value, unit):
    return (value + unit - 1) // unit * unit


class Sizes:
    def __init__(self, chips, hidden_block, gate_block, down_block):
        self.chips = chips
        _, self.tokens, self.width = hidden_block
        self.side = math.isqrt(chips // 4)
        self.grid = (4, self.side, self.side)
        self.keys = self.tokens * chips
        self.rows, _ = gate_block
        self.rows_p = round_up(self.rows, 16)
        self.wide = chips * self.rows_p
        self.half = self.wide // 2
        self.ffn_rows = down_block[0]
        self.ffn_rows_p = round_up(self.ffn_rows, 16)
        self.ffn_half = chips * self.ffn_rows_p // 2
        self.q_cols = HEADS * HEAD_DIM // 2
        self.k_cols = KV_HEADS * HEAD_DIM // 2
        self.cols = self.q_cols + 2 * self.k_cols
        self.pack = round_up(self.cols, LANES)
        self.ffn_cols = gate_block[1]
        self.gain_lane = 3 * self.tokens
        assert self.rows < self.rows_p and self.gain_lane + 3 * self.rows <= self.pack
        self.step_heads = GROUPS if self.keys <= 4096 else 1
        self.steps = HEADS // self.step_heads
        self.steps_per_kv = GROUPS // self.step_heads
        self.step_rows = self.step_heads * self.tokens
        self.kv_wide = KV_HEADS * LANES
        self.slots = 2 if self.keys <= 4096 else 1
        self.row_parts = 1 if self.keys <= 4096 else 4
        self.bias_type = jnp.float32 if self.keys <= 4096 else jnp.bfloat16


class Place:
    def __init__(self, chips, count_only=False):
        side = math.isqrt(chips // 4)
        self.sizes = (4, side, side)
        self.strides = (side * side, side, 1)
        if count_only:
            self.core, self.chip, self.pos = 0, 0, (0, 0, 0)
            return
        self.core = lax.axis_index("dp")
        self.chip = lax.axis_index("seq")
        self.pos = (
            self.chip // (side * side),
            lax.rem(self.chip // side, side),
            lax.rem(self.chip, side),
        )

    def step(self, axis, k):
        size = self.sizes[axis]
        if size == 2:
            return 1 - self.pos[axis]
        return lax.rem(self.pos[axis] + (k + size) % size, size)

    def at(self, axis, other):
        return (self.core, self.chip + (other - self.pos[axis]) * self.strides[axis])

    def peer(self):
        return (1 - self.core, self.chip)

    def greet(self):
        barrier = pltpu.get_barrier_semaphore()
        devices = [self.peer()]
        for axis, size in enumerate(self.sizes):
            devices += [self.at(axis, self.step(axis, k)) for k in range(1, size)]
        for dev in devices:
            pl.semaphore_signal(barrier, inc=1, device_id=dev, device_id_type=MESH)
        pl.semaphore_wait(barrier, len(devices))


class Sems:
    def __init__(self, send=None, recv=None):
        self.send, self.recv, self.used = send, recv, 0

    def take(self):
        self.used += 1
        return self.used - 1


class Copy:
    def __init__(self, sems, src, dst, dev, come):
        self.i, self.sems = sems.take(), sems
        self.src, self.dst, self.dev, self.come = src, dst, dev, come

    def _make(self, src, dst):
        return pltpu.make_async_remote_copy(
            src_ref=src(),
            dst_ref=dst(),
            send_sem=self.sems.send.at[self.i],
            recv_sem=self.sems.recv.at[self.i],
            device_id=self.dev,
            device_id_type=MESH,
        )

    def start(self):
        self._make(self.src, self.dst).start()

    def sent(self):
        self._make(self.src, self.dst).wait_send()

    def came(self):
        self._make(self.come, self.come).wait_recv()


class Gather:
    def __init__(self, place, sems, view, order, twin=None):
        self.place, self.view, self.twin, self.order = place, view, twin, order
        a, b, c = order
        size, pos = place.sizes, place.pos
        self.all = []
        self.first = [
            self._line(sems, a, k, lambda j: self._ref(j, pos[b], pos[c]))
            for k in range(1, size[a])
        ]
        self.second = [
            self._line(sems, b, k, lambda j: self._ref(None, j, pos[c]))
            for k in range(1, size[b])
        ]
        self.third, self.cross = [], []
        for m in range(size[b]):
            jb = pos[b] if m == 0 else place.step(b, -m)
            self.third.append(
                [
                    self._line(sems, c, k, lambda j, jb=jb: self._ref(None, jb, j))
                    for k in range(1, size[c])
                ]
            )
            self.cross.append(
                [
                    self._cross(sems, jb, pos[c] if k == 0 else place.step(c, -k))
                    for k in range(size[c])
                ]
            )

    def _ref(self, ia, ib, ic, twin=False):
        idx = [None] * 3
        for axis, i in zip(self.order, (ia, ib, ic)):
            idx[axis] = slice(None) if i is None else i
        return (self.twin if twin else self.view)(*idx)

    def _line(self, sems, axis, k, unit):
        mine = lambda: unit(self.place.pos[axis])
        dev = self.place.at(axis, self.place.step(axis, k))
        c = Copy(sems, mine, mine, dev, lambda: unit(self.place.step(axis, -k)))
        self.all.append(c)
        return c

    def _cross(self, sems, jb, jc):
        if self.twin is None:
            return None
        here = lambda: self._ref(None, jb, jc)
        c = Copy(sems, here, here, self.place.peer(), lambda: self._ref(None, jb, jc, True))
        self.all.append(c)
        return c

    def _spread(self, m):
        for c in self.third[m]:
            c.start()
        if self.twin is not None:
            self.cross[m][0].start()

    def run(self, r):
        if r == 0:
            for c in self.first:
                c.start()
        elif r == 1:
            for c in self.first:
                c.came()
            for c in self.second:
                c.start()
            self._spread(0)
        elif r == 2:
            for m, c in enumerate(self.second):
                c.came()
                self._spread(m + 1)
        elif r == 3:
            for line, cross in zip(self.third, self.cross):
                for k, c in enumerate(line):
                    c.came()
                    if self.twin is not None:
                        cross[k + 1].start()
        elif r == 4:
            if self.twin is not None:
                for cross in self.cross:
                    for c in cross:
                        c.came()
        else:
            for c in self.all:
                c.sent()


class Scatter:
    def __init__(self, place, sems, view, order, lands):
        self.place, self.view, self.order = place, view, order
        self.lands = lands
        a, b, c = order
        size, pos = place.sizes, place.pos
        self.all = []
        self.first, self.second, self.third = [], [], []
        land_c, land_b, land_a = lands if lands is not None else (None,) * 3
        for m in list(range(1, size[b])) + [0]:
            jb = pos[b] if m == 0 else place.step(b, m)
            self.first.append(
                (
                    m,
                    jb,
                    [
                        self._line(
                            sems, c, k, lambda j, jb=jb: self._ref(None, jb, j),
                            land_c, m * (size[c] - 1) + k - 1,
                        )
                        for k in range(1, size[c])
                    ],
                )
            )
        for m in range(1, size[b]):
            self.second.append(
                self._line(sems, b, m, lambda j: self._ref(None, j, pos[c]), land_b, m - 1)
            )
        for k in range(1, size[a]):
            self.third.append(
                self._line(sems, a, k, lambda j: self._ref(j, pos[b], pos[c]), land_a, k - 1)
            )

    def _ref(self, ia, ib, ic):
        idx = [None] * 3
        for axis, i in zip(self.order, (ia, ib, ic)):
            idx[axis] = slice(None) if i is None else i
        return self.view(*idx)

    def _line(self, sems, axis, k, unit, land, slot):
        to = self.place.step(axis, k)
        spot = lambda: land.at[slot]
        c = Copy(sems, lambda: unit(to), spot, self.place.at(axis, to), spot)
        self.all.append(c)
        return c

    def _add(self, ref, land, slots):
        total = ref[...].astype(jnp.float32)
        for s in slots:
            total = total + land[s].astype(jnp.float32)
        return total

    def run(self, r):
        a, b, c = self.order
        size, pos = self.place.sizes, self.place.pos
        if r == 0:
            for _, _, line in self.first:
                for cp in line:
                    cp.start()
        elif r == 1:
            for m, jb, line in self.first:
                for cp in line:
                    cp.came()
                unit = self._ref(None, jb, pos[c])
                slots = [m * (size[c] - 1) + k for k in range(size[c] - 1)]
                unit[...] = self._add(unit, self.lands[0], slots).astype(unit.dtype)
                if m > 0:
                    self.second[m - 1].start()
        elif r == 2:
            for cp in self.second:
                cp.came()
            unit = self._ref(None, pos[b], pos[c])
            unit[...] = self._add(unit, self.lands[1], range(size[b] - 1)).astype(unit.dtype)
            for cp in self.third:
                cp.start()
        elif r == 3:
            for cp in self.third:
                cp.came()
        else:
            for cp in self.all:
                cp.sent()

    def total(self):
        a, b, c = self.order
        unit = self._ref(*(self.place.pos[axis] for axis in self.order))
        return self._add(unit, self.lands[2], range(self.place.sizes[a] - 1))


def land_shapes(grid, order, rows, cols):
    a, b, c = (grid[axis] for axis in order)
    return [
        pltpu.VMEM((b * (c - 1), a, rows, cols), jnp.bfloat16),
        pltpu.VMEM((b - 1, a, rows, cols), jnp.bfloat16),
        pltpu.VMEM((a - 1, rows, cols), jnp.bfloat16),
    ]


def tiles(total, **shares):
    out, at = [], 0
    names = list(shares)
    for name in names:
        span = shares[name] if name != names[-1] else total // LANES - at
        out.append((name, at * LANES, span * LANES))
        at += span
    return out


def weight_flows(sz):
    out = []
    for tensor, total in (("g", sz.ffn_half), ("u", sz.ffn_half), ("o", sz.half), ("d", sz.half)):
        shares = dict(C=total // LANES // 2, D=0)
        out += [(tensor + name, tensor, first, span) for name, first, span in tiles(total, **shares)]
    return out


def pack_flows(sz):
    return [("q" + n, "q", f, s) for n, f, s in tiles(sz.pack, C=4, D=3)]


def kv_flows(sz):
    half = sz.tokens // 2
    return [("kC", 0, half, 0, sz.kv_wide), ("kD", half, half, 0, sz.kv_wide)]


FORWARD = (
    "qC0", "qD0", "others", "gC0", "qC1", "qD1", "qC2", "oD0", "gD0", "qD2", "uC0", "gC1", "oD1",
    "gD1", "qC3", "qD3", "dC0", "gC2", "oC0", "dD0", "qD4", "prep", "uC1", "qC4", "gD2", "qkv",
    "oC1", "gC3", "kC0", "dC1", "oC2", "kD0", "kC1", "oD2", "oC3", "oC4", "uD0", "kD1", "kC2",
    "gC4", "heads", "mask", "kD2", "uD1", "kD3", "kC3", "dD1", "atta", "oD3", "gD3", "uC2",
    "gD4", "attb", "uD2", "oD4", "dC2", "dD2", "attc", "attd", "atte", "uC3", "uC4", "uD3",
    "dC3", "out", "dC4", "uD4", "dD3", "gu", "dD4", "down",)

BACKWARD = (
    "ld", "lg", "lu", "uC0", "uD0", "lo", "atta", "attb", "attc", "attd", "atte", "kD0", "kC0",
    "dC0", "qs", "eC0", "uD1", "kC1", "uC1", "kD1", "oD0", "kC2", "uC2", "dC1", "gC0", "uD2",
    "dD0", "gD0", "oD1", "kD2", "kC3", "kD3", "dC2", "dD1", "oC0", "gC1", "oD2", "dD2", "gD1",
    "oC1", "kq", "eC1", "uC3", "qC0", "gC2", "qD0", "dC3", "gi", "eC2", "oC2", "gD2", "qC1",
    "gC3", "uD3", "qD1", "qC2", "gD3", "dD3", "oD3", "qD2", "qC3", "oC3", "qD3", "eC3", "fin",)


class Order:
    def __init__(self, flows, words):
        self.flows, self.words, self.at = flows, words, 0

    def until(self, mark):
        while self.words[self.at] != mark:
            word = self.words[self.at]
            self.flows[word[:-1]].run(int(word[-1]))
            self.at += 1
        self.at += 1


def dot(left, right):
    return jnp.dot(left, right, preferred_element_type=jnp.float32)


def dot_nt(left, right):
    return lax.dot_general(
        left, right, (((1,), (1,)), ((), ())), preferred_element_type=jnp.float32
    )


def dot_tn(left, right):
    return lax.dot_general(
        left, right, (((0,), (0,)), ((), ())), preferred_element_type=jnp.float32
    )


def blocks_padded(value, block, block_p):
    if block == block_p:
        return value
    zero = jnp.zeros((value.shape[0], block_p - block), value.dtype)
    pieces = []
    for j in range(value.shape[1] // block):
        pieces += [value[:, j * block : (j + 1) * block], zero]
    return jnp.concatenate(pieces, axis=1)


def blocks_cut(value, block, block_p):
    if block == block_p:
        return value
    return jnp.concatenate(
        [value[:, j * block_p : j * block_p + block] for j in range(value.shape[1] // block_p)],
        axis=1,
    )


def spread(sz, value):
    return blocks_padded(value, sz.rows, sz.rows_p)


def narrow(sz, value):
    return blocks_cut(value, sz.rows, sz.rows_p)


def tokens_in(sz, ref):
    value = ref[...].astype(jnp.float32)
    zero = jnp.zeros((sz.rows_p - sz.rows, sz.tokens), jnp.float32)
    pieces = []
    for j in range(sz.chips):
        pieces += [value[j * sz.rows : (j + 1) * sz.rows], zero]
    return jnp.concatenate(pieces, axis=0).T


def tokens_out(sz, value):
    value = value.T
    pieces = [value[j * sz.rows_p : j * sz.rows_p + sz.rows] for j in range(sz.chips)]
    return jnp.concatenate(pieces, axis=0).astype(jnp.bfloat16)


def rows_padded(value, rows):
    if value.shape[0] < rows:
        zero = jnp.zeros((rows - value.shape[0], value.shape[1]), value.dtype)
        value = jnp.concatenate([value, zero], axis=0)
    return value.astype(jnp.bfloat16)


def lane_index(shape):
    return lax.broadcasted_iota(jnp.int32, shape, len(shape) - 1)


def swap_halves(value):
    span = value.shape[1]
    first = lax.rem(lane_index(value.shape), HEAD_DIM) < HEAD_DIM // 2
    return jnp.where(
        first,
        pltpu.roll(value, span - HEAD_DIM // 2, 1),
        pltpu.roll(value, HEAD_DIM // 2, 1),
    )


def repeat_lanes(table, span):
    return jnp.concatenate([table] * (span // LANES), axis=1)


def chips_of(sz):
    return [(i, j, k) for i in range(sz.grid[0]) for j in range(sz.side) for k in range(sz.side)]


def gain_row(sz, wq, which):
    first = sz.gain_lane + which * sz.rows
    zero = jnp.zeros((1, sz.rows_p - sz.rows), jnp.float32)
    pieces = []
    for i, j, k in chips_of(sz):
        line = wq[0, i, j, k, sz.rows : sz.rows + 1, :].astype(jnp.float32)
        pieces += [line[:, first : first + sz.rows], zero]
    return jnp.concatenate(pieces, axis=1)


def rotary_tables(sz, place):
    lane = lane_index((sz.tokens, LANES))
    row = lax.broadcasted_iota(jnp.int32, (sz.tokens, LANES), 0)
    half = HEAD_DIM // 2
    place_of = (place.chip * sz.tokens + row).astype(jnp.float32)
    inv_freq = jnp.exp(lax.rem(lane, half).astype(jnp.float32) * (-math.log(10000.0) / half))
    angles = place_of * inv_freq
    sine = jnp.sin(angles)
    return jnp.cos(angles), jnp.where(lax.rem(lane, HEAD_DIM) < half, -sine, sine)


def forward_flows(sz, place, sems, full, kv):
    flows = {}
    for name, tensor, first, span in pack_flows(sz) + weight_flows(sz):

        def view(half, ref=full[tensor], first=first, span=span):
            return lambda i, j, k: ref.at[half, i, j, k, :, pl.ds(first, span)]

        core = place.core
        flows[name] = Gather(place, sems, view(core), ORDERS[name[1]], view(1 - core))
    for name, r0, rn, first, span in kv_flows(sz):

        def view(i, j, k, r0=r0, rn=rn, first=first, span=span):
            return kv.at[i, j, k, pl.ds(r0, rn), pl.ds(first, span)]

        flows[name] = Gather(place, sems, view, ORDERS[name[1]])
    return flows


def backward_flows(sz, place, sems, partial, kv, err, lands):
    flows, at = {}, 0
    for name, tensor, first, span in pack_flows(sz) + weight_flows(sz):

        def view(i, j, k, ref=partial[tensor], first=first, span=span):
            return ref.at[i, j, k, :, pl.ds(first, span)]

        land = None if lands is None else lands[at : at + 3]
        flows[name] = Scatter(place, sems, view, ORDERS[name[1]], land)
        at += 3
    for name, r0, rn, first, span in kv_flows(sz):

        def view(i, j, k, r0=r0, rn=rn, first=first, span=span):
            return kv.at[i, j, k, pl.ds(r0, rn), pl.ds(first, span)]

        land = None if lands is None else lands[at : at + 3]
        flows[name] = Scatter(place, sems, view, ORDERS[name[1]], land)
        at += 3
    flows["eC"] = Gather(place, sems, lambda i, j, k: err.at[i, j, k], ORDERS["C"])
    return flows


def forward_kernel(
    sz,
    q_in, k_in, v_in, out_in, gate_in, up_in, down_in, gains_in, seg_in, route_in, valid_in,
    hid_in, teach_in,
    state_out, dhid_out, small_out, wq_out, kv_out, prob_out, heads_out, dctx_out,
    cos_out, sin_out, pg_out, pu_out, po_out, pd_out,
    wq, wo, wg, wu, wd, kv, bias, prob, ctx_h, hid, normed2, act, gate_s, up_s, ctx2, datt2, dffn2,
    dgate2, dup2, stage_d, stage_h, col_in,
    send, recv, local,
):
    place = Place(sz.chips)
    sems = Sems(send, recv)
    core = place.core
    t, n, wide = sz.tokens, sz.chips, sz.wide
    full = {"q": wq, "o": wo, "g": wg, "u": wu, "d": wd}
    flows = forward_flows(sz, place, sems, full, kv)
    peer = place.peer()

    def to_peer(src, dst):
        return Copy(sems, lambda: src, lambda: dst, peer, lambda: dst)

    own, other = pl.ds(0, t), pl.ds(t, t)
    x_n2 = to_peer(normed2.at[own], normed2.at[other])
    x_act = to_peer(act.at[:, own], act.at[:, other])
    x_ctx = to_peer(ctx2.at[own], ctx2.at[other])
    x_dffn = to_peer(stage_d.at[0], dffn2.at[other])
    x_datt = to_peer(stage_d.at[1], datt2.at[other])
    x_dgate = to_peer(stage_h.at[0], dgate2.at[other])
    x_dup = to_peer(stage_h.at[1], dup2.at[other])
    used = [0]

    def bring(src, dst):
        used[0] += 1
        return pltpu.make_async_copy(src, dst, local.at[used[0] - 1])

    f32 = jnp.float32
    spot = (core,) + place.pos
    marks = [ref[...].astype(f32) for ref in (seg_in, route_in, valid_in)]
    rest = sz.pack - sz.gain_lane - 3 * sz.rows
    line = jnp.concatenate(marks + [gains_in[...].astype(f32), jnp.zeros((1, rest), f32)], axis=1)
    block = jnp.concatenate(
        [ref[...].astype(f32) for ref in (q_in, k_in, v_in)]
        + [jnp.zeros((sz.rows, sz.pack - sz.cols), f32)],
        axis=1,
    )
    wq[spot] = rows_padded(jnp.concatenate([block, line], axis=0), sz.rows_p)
    place.greet()
    order = Order(flows, FORWARD)
    order.until("others")
    wo[spot] = rows_padded(spread(sz, out_in[...].astype(f32)), sz.rows_p)
    for ref, own_in in ((wg, gate_in), (wu, up_in)):
        block = blocks_padded(own_in[...].astype(f32), sz.ffn_rows, sz.ffn_rows_p)
        ref[spot] = rows_padded(block, sz.rows_p)
    wd[spot] = rows_padded(spread(sz, down_in[...].astype(f32)), sz.ffn_rows_p)

    order.until("prep")
    hid[...] = tokens_in(sz, hid_in)
    hidden = hid[...]
    inv_first = lax.rsqrt(jnp.sum(hidden * hidden, axis=-1, keepdims=True) / sz.width + norm_eps)
    cos_out[...], sin_out[...] = rotary_tables(sz, place)
    col_in[...] = jnp.concatenate(marks + [jnp.zeros((5, t), f32)], axis=0).T
    cosine, sine = repeat_lanes(cos_out[...], 8 * LANES), repeat_lanes(sin_out[...], 8 * LANES)

    order.until("qkv")
    wq_full = [wq[h].reshape(wide, sz.pack) for h in (0, 1)]
    gain_one = gain_row(sz, wq, 0)
    normed = (hidden * inv_first * gain_one).astype(jnp.bfloat16)
    halves = [dot(normed, w) for w in wq_full]
    qc, kc = sz.q_cols, sz.k_cols
    q_pre = jnp.concatenate(
        [halves[0][:, :qc], halves[1][:, :qc], jnp.zeros((t, 8 * LANES - 2 * qc), jnp.float32)],
        axis=1,
    )
    pad_k = jnp.zeros((t, 3 * LANES - 2 * kc), jnp.float32)
    k_pre = jnp.concatenate(
        [halves[0][:, qc : qc + kc], halves[1][:, qc : qc + kc], pad_k], axis=1
    )
    v_pre = jnp.concatenate(
        [halves[0][:, qc + kc : qc + 2 * kc], halves[1][:, qc + kc : qc + 2 * kc]], axis=1
    )
    k_rot = k_pre * cosine[:, : 3 * LANES] + swap_halves(k_pre) * sine[:, : 3 * LANES]
    kv_own = jnp.concatenate(
        [
            piece[:, g * HEAD_DIM : (g + 1) * HEAD_DIM]
            for g in range(KV_HEADS)
            for piece in (k_rot, v_pre)
        ],
        axis=1,
    )
    kv[place.pos[0], place.pos[1], place.pos[2]] = kv_own.astype(jnp.bfloat16)
    order.until("heads")
    q_rot = q_pre * cosine + swap_halves(q_pre) * sine
    q_low = q_rot.astype(jnp.bfloat16).astype(jnp.float32) * HEAD_DIM ** (-0.5)
    blank = jnp.zeros((t, HEAD_DIM), jnp.float32)
    for h in range(HEADS):
        st, sub = h // sz.step_heads, h % sz.step_heads
        heads_out[st, pl.ds(sub * t, t)] = jnp.concatenate(
            [q_low[:, h * HEAD_DIM : (h + 1) * HEAD_DIM], blank], axis=1
        ).astype(jnp.bfloat16)
    order.until("mask")

    row_at = sz.rows
    seg_col, route_col, valid_col = col_in[:, 0:1], col_in[:, 1:2], col_in[:, 2:3]
    q_pos = place.chip * t + lax.broadcasted_iota(jnp.int32, (t, LANES), 0)
    count = jnp.zeros((1, LANES), jnp.float32)
    for m, (i, j, k) in enumerate(chips_of(sz)):
        line = wq[core, i, j, k, row_at : row_at + 1, : 2 * LANES].astype(jnp.float32)
        seg_row, route_row = line[:, :LANES], line[:, LANES:]
        k_pos = m * t + lane_index((t, LANES))
        allowed = (
            (seg_col == seg_row)
            & (k_pos <= q_pos)
            & ((route_row > 0.5) | (k_pos == q_pos))
        )
        bias[:, m * t : (m + 1) * t] = jnp.where(allowed, 0.0, masked_score).astype(bias.dtype)
        for h in (0, 1):
            count = count + wq[
                h, i, j, k, row_at : row_at + 1, 2 * LANES : 3 * LANES
            ].astype(jnp.float32)
    tok_count = jnp.sum(count, axis=-1, keepdims=True)
    small_out[...] = jnp.zeros(small_out.shape, f32)
    small_out[3:4] = jnp.broadcast_to(tok_count, (1, wide))
    small_out[4:5] = gain_one
    keep_wq = bring(wq, wq_out)
    keep_kv = bring(kv, kv_out)
    prob_sem = used[0]
    used[0] += sz.slots

    def attend(st):
        g = st // sz.steps_per_kv
        slot = lax.rem(st, sz.slots)
        lanes = pl.ds(pl.multiple_of(g * LANES, LANES), LANES)
        tile = kv[:, :, :, :, lanes].reshape(sz.keys, LANES)
        s = dot_nt(heads_out[st], tile).reshape(sz.step_heads, t, sz.keys) + bias[...].astype(jnp.float32)[None]
        s = s.reshape(sz.step_rows, sz.keys)
        e = jnp.exp(s - jnp.max(s, axis=-1, keepdims=True))
        p = (e * (1.0 / jnp.sum(e, axis=-1, keepdims=True))).astype(jnp.bfloat16)
        save = pltpu.make_async_copy(prob.at[slot], prob_out.at[st], local.at[prob_sem + slot])

        @pl.when(st >= sz.slots)
        def _():
            save.wait()

        prob[slot] = p
        save.start()
        ctx_h[st] = dot(p, tile).astype(jnp.bfloat16)

    for g in range(KV_HEADS):
        order.until("att%s" % "abcde"[g])
        if g == 0:
            keep_wq.start()
            keep_kv.start()
        pl.loop(g * sz.steps // KV_HEADS, (g + 1) * sz.steps // KV_HEADS)(attend)
    for slot in range(sz.slots):
        pltpu.make_async_copy(prob.at[slot], prob_out.at[slot], local.at[prob_sem + slot]).wait()

    ctx = jnp.concatenate(
        [
            ctx_h[h // sz.step_heads, pl.ds(h % sz.step_heads * t, t), HEAD_DIM:].astype(jnp.float32)
            for h in range(HEADS)
        ],
        axis=1,
    )
    ctx2[own] = spread(sz, ctx).astype(jnp.bfloat16)
    x_ctx.start()
    order.until("out")
    attn = jnp.concatenate([dot(ctx2[own], wo[q].reshape(wide, sz.half)) for q in (0, 1)], axis=1)
    hidden = hid[...]
    gain_two, router = gain_row(sz, wq, 1), gain_row(sz, wq, 2)
    residual = hidden + attn
    inv_second = lax.rsqrt(
        jnp.sum(residual * residual, axis=-1, keepdims=True) / sz.width + norm_eps
    )
    normed2[own] = (residual * inv_second * gain_two).astype(jnp.bfloat16)
    x_n2.start()
    order.until("gu")
    for h in (0, 1):
        gate_pre = dot(normed2[own], wg[h].reshape(wide, sz.ffn_half))
        up_pre = dot(normed2[own], wu[h].reshape(wide, sz.ffn_half))
        gate_s[h], up_s[h] = gate_pre, up_pre
        act[h, own] = (gate_pre * jax.nn.sigmoid(gate_pre) * up_pre).astype(jnp.bfloat16)
    x_act.start()
    order.until("down")
    two = sz.grid[0] // 2

    def down(q, h):
        return wd[q, pl.ds(h * two, two)].reshape(sz.ffn_half, sz.half)

    ffn = jnp.concatenate(
        [dot(act[0, own], down(q, 0)) + dot(act[1, own], down(q, 1)) for q in (0, 1)], axis=1
    )

    router_sig = jax.nn.sigmoid(jnp.sum(hidden * router, axis=-1, keepdims=True))
    mix = route_col * router_sig
    branch = attn + ffn
    state = hidden + mix * branch
    state_out[...] = tokens_out(sz, state)
    misfit = state - tokens_in(sz, teach_in)
    small_out[2:3] = jnp.sum(valid_col * misfit * misfit, axis=0, keepdims=True)
    d_state = 2.0 / (sz.width * tok_count) * valid_col * misfit
    d_branch = mix * d_state
    d_logit = (
        route_col
        * jnp.sum(d_state * branch, axis=-1, keepdims=True)
        * router_sig
        * (1.0 - router_sig)
    )
    small_out[1:2] = jnp.sum(d_logit * hidden, axis=0, keepdims=True)
    d_ffn = d_branch.astype(jnp.bfloat16)
    low, high = d_ffn[:, : sz.half], d_ffn[:, sz.half :]
    stage_d[0] = jnp.where(core == 0, high, low)
    x_dffn.start()
    dffn2[own] = jnp.where(core == 0, low, high)
    d_normed2 = jnp.zeros((t, wide), jnp.float32)
    for turn in (1, 0):
        h = core if turn == 0 else 1 - core
        d_act = dot_nt(low, down(0, h)) + dot_nt(high, down(1, h))
        gate_pre, up_pre = gate_s[h], up_s[h]
        sig = jax.nn.sigmoid(gate_pre)
        d_gate = (d_act * up_pre * sig * (1.0 + gate_pre * (1.0 - sig))).astype(jnp.bfloat16)
        d_up = (d_act * (gate_pre * sig)).astype(jnp.bfloat16)
        if turn == 1:
            stage_h[0], stage_h[1] = d_gate, d_up
            x_dgate.start()
            x_dup.start()
        else:
            dgate2[own], dup2[own] = d_gate, d_up
        d_normed2 = (
            d_normed2
            + dot_nt(d_gate, wg[h].reshape(wide, sz.ffn_half))
            + dot_nt(d_up, wu[h].reshape(wide, sz.ffn_half))
        )
    small_out[0:1] = jnp.sum(d_normed2 * residual * inv_second, axis=0, keepdims=True)
    scaled = gain_two * d_normed2
    d_mid = inv_second * scaled - residual * (
        inv_second**3 * (jnp.sum(scaled * residual, axis=-1, keepdims=True) / sz.width)
    )
    dhid_out[...] = d_state + d_logit * router + d_mid
    d_attn = (d_branch + d_mid).astype(jnp.bfloat16)
    low, high = d_attn[:, : sz.half], d_attn[:, sz.half :]
    stage_d[1] = jnp.where(core == 0, high, low)
    x_datt.start()
    datt2[own] = jnp.where(core == 0, low, high)
    d_ctx = dot_nt(low, wo[0].reshape(wide, sz.half)) + dot_nt(high, wo[1].reshape(wide, sz.half))
    d_ctx = narrow(sz, d_ctx)
    for h in range(HEADS):
        st, sub = h // sz.step_heads, h % sz.step_heads
        dctx_out[st, pl.ds(sub * t, t)] = jnp.concatenate(
            [blank, d_ctx[:, h * HEAD_DIM : (h + 1) * HEAD_DIM]], axis=1
        ).astype(jnp.bfloat16)

    for cp in (x_n2, x_act, x_ctx, x_dffn, x_datt, x_dgate, x_dup):
        cp.came()
    for name, flow in flows.items():
        flow.run(5)
    pd, pg, pu, po = wd.at[0], wg.at[0], wu.at[0], wo.at[0]
    shape = (sz.side, sz.side)
    for h in (0, 1):
        for i in range(two):
            part = sz.ffn_half // two
            pd[h * two + i] = (
                dot_tn(act[h, :, pl.ds(i * part, part)], dffn2[...])
                .astype(jnp.bfloat16)
                .reshape(shape + (sz.ffn_rows_p, sz.half))
            )
    keep = [bring(pd, pd_out)]
    keep[-1].start()
    part = wide // sz.grid[0]
    for left, right, ref, out in (
        (normed2, dgate2, pg, pg_out),
        (normed2, dup2, pu, pu_out),
        (ctx2, datt2, po, po_out),
    ):
        for i in range(sz.grid[0]):
            ref[i] = (
                dot_tn(left[:, pl.ds(i * part, part)], right[...])
                .astype(jnp.bfloat16)
                .reshape(shape + (sz.rows_p, right.shape[1]))
            )
        keep.append(bring(ref, out))
        keep[-1].start()
    for cp in keep + [keep_wq, keep_kv]:
        cp.wait()
    for cp in (x_n2, x_act, x_ctx, x_dffn, x_datt, x_dgate, x_dup):
        cp.sent()


def backward_kernel(
    sz,
    wq_in, kv_in, prob_in, heads, dctx, pg_in, pu_in, po_in, pd_in, hid_in, dhid, small_in,
    cos_in, sin_in,
    ghid_out, gq_out, gk_out, gv_out, go_out, gg_out, gu_out, gd_out, gain1_out, gain2_out,
    router_out, loss_out,
    wq, kv, prob, dq_h, normed2, dpack2, stage, pg, pu, po, pd, small2, err,
    lands, send, recv, local,
):
    place = Place(sz.chips)
    sems = Sems(send, recv)
    core = place.core
    t, wide = sz.tokens, sz.wide
    pq = wq.at[0]
    partial = {"q": pq, "o": po, "g": pg, "u": pu, "d": pd}
    flows = backward_flows(sz, place, sems, partial, kv, err, lands)
    peer = place.peer()

    def to_peer(src, dst):
        return Copy(sems, lambda: src, lambda: dst, peer, lambda: dst)

    own, other = pl.ds(0, t), pl.ds(t, t)
    x_n = to_peer(normed2.at[own], normed2.at[other])
    x_pack = to_peer(stage, dpack2.at[other])
    x_small = to_peer(small2.at[0], small2.at[1])
    x_err = to_peer(small2.at[2], small2.at[3])
    used = [0]

    def bring(src, dst):
        used[0] += 1
        return pltpu.make_async_copy(src, dst, local.at[used[0] - 1])

    get_kv, get_wq = bring(kv_in, kv), bring(wq_in, wq)
    get_p = [bring(src, ref) for src, ref in ((pd_in, pd), (pg_in, pg), (pu_in, pu), (po_in, po))]
    prob_sem = used[0]

    part_rows = sz.step_rows // sz.row_parts

    def fetch(st, slot):
        rows = pl.ds(lax.rem(st, sz.row_parts) * part_rows, part_rows)
        return pltpu.make_async_copy(
            prob_in.at[st // sz.row_parts, rows], prob.at[slot], local.at[prob_sem + slot]
        )

    fetch(0, 0).start()
    for cp in get_p + [get_kv, get_wq]:
        cp.start()
    small2[2] = small_in[...]
    place.greet()
    x_err.start()
    order = Order(flows, BACKWARD)
    for name, cp in zip("dguo", get_p):
        order.until("l" + name)
        cp.wait()
    get_kv.wait()

    def attend(i, total):
        st = i // sz.row_parts
        slot = lax.rem(i, 2)
        fetch(i, slot).wait()

        @pl.when(i + 1 < sz.steps * sz.row_parts)
        def _():
            fetch(i + 1, 1 - slot).start()

        lanes = pl.ds(pl.multiple_of(st // sz.steps_per_kv * LANES, LANES), LANES)
        tile = kv[:, :, :, :, lanes].reshape(sz.keys, LANES)
        rows = pl.ds(pl.multiple_of(lax.rem(i, sz.row_parts) * part_rows, part_rows), part_rows)
        p_low = prob[slot]
        p = p_low.astype(jnp.float32)
        d_w = dot_nt(dctx[st, rows], tile)
        terms = p * d_w
        delta = jnp.sum(terms, axis=-1, keepdims=True)
        d_s = (terms - p * delta).astype(jnp.bfloat16)
        dq_h[st, rows] = dot(d_s, tile)
        more = dot_tn(heads[st, rows], d_s) + dot_tn(dctx[st, rows], p_low)
        return more if total is None else total + more

    for g in range(KV_HEADS):
        order.until("att%s" % "abcde"[g])
        each = sz.steps_per_kv * sz.row_parts
        if each == 1:
            total = attend(jnp.int32(g), None)
        else:
            total = jnp.zeros((LANES, sz.keys), jnp.float32)
            total = lax.fori_loop(g * each, (g + 1) * each, attend, total)
        kv[:, :, :, :, pl.ds(g * LANES, LANES)] = (
            total.astype(jnp.bfloat16).T.reshape(sz.grid + (t, LANES))
        )
    order.until("qs")

    get_wq.wait()
    wq_full = [wq[h].reshape(wide, sz.pack) for h in (0, 1)]
    gain_one = small_in[4:5]
    hidden = tokens_in(sz, hid_in)
    inv_first = lax.rsqrt(jnp.sum(hidden * hidden, axis=-1, keepdims=True) / sz.width + norm_eps)
    normed2[own] = (hidden * inv_first * gain_one).astype(jnp.bfloat16)
    x_n.start()
    cosine, sine = cos_in[...], sin_in[...]
    scale = HEAD_DIM ** (-0.5)
    dq = jnp.concatenate(
        [
            dq_h[h // sz.step_heads, pl.ds(h % sz.step_heads * t, t), :HEAD_DIM]
            for h in range(HEADS)
        ]
        + [jnp.zeros((t, HEAD_DIM), jnp.float32)],
        axis=1,
    ) * scale
    dq = dq * repeat_lanes(cosine, 8 * LANES) - swap_halves(dq) * repeat_lanes(sine, 8 * LANES)
    d_q = dq.astype(jnp.bfloat16).astype(jnp.float32)

    x_err.came()
    both_err = jnp.sum(small2[2][2:3] + small2[3][2:3], axis=-1, keepdims=True)
    err[place.pos[0], place.pos[1], place.pos[2]] = jnp.broadcast_to(both_err, (8, LANES))
    order.until("kq")
    d_kv = jnp.concatenate([flows["kC"].total(), flows["kD"].total()], axis=0)
    in_key = lax.rem(lane_index(d_kv.shape), LANES) < HEAD_DIM
    cos_kv = jnp.where(in_key, repeat_lanes(cosine, sz.kv_wide), 1.0)
    sin_kv = jnp.where(in_key, repeat_lanes(sine, sz.kv_wide), 0.0)
    d_kv = d_kv * cos_kv - swap_halves(d_kv) * sin_kv
    d_kv = d_kv.astype(jnp.bfloat16).astype(jnp.float32)
    d_k = jnp.concatenate(
        [d_kv[:, g * LANES : g * LANES + HEAD_DIM] for g in range(KV_HEADS)], axis=1
    )
    d_v = jnp.concatenate(
        [d_kv[:, g * LANES + HEAD_DIM : (g + 1) * LANES] for g in range(KV_HEADS)], axis=1
    )
    qc, kc = sz.q_cols, sz.k_cols
    blank = jnp.zeros((t, sz.pack - sz.cols), jnp.float32)
    d_pack = [
        jnp.concatenate(
            [
                d_q[:, h * qc : (h + 1) * qc],
                d_k[:, h * kc : (h + 1) * kc],
                d_v[:, h * kc : (h + 1) * kc],
                blank,
            ],
            axis=1,
        ).astype(jnp.bfloat16)
        for h in (0, 1)
    ]
    stage[...] = jnp.where(core == 0, d_pack[1], d_pack[0])
    x_pack.start()
    dpack2[own] = jnp.where(core == 0, d_pack[0], d_pack[1])
    d_normed = dot_nt(d_pack[0], wq_full[0]) + dot_nt(d_pack[1], wq_full[1])
    small2[0] = small_in[...]
    small2[0, 2:3] = jnp.sum(d_normed * hidden * inv_first, axis=0, keepdims=True)
    x_small.start()
    x_n.came()
    x_pack.came()
    x_small.came()
    rows = small2[0] + small2[1]
    part = wide // sz.grid[0]
    shape = (sz.side, sz.side)
    for i in range(sz.grid[0]):
        grad = dot_tn(normed2[:, pl.ds(i * part, part)], dpack2[...])
        for b in range(part // sz.rows_p):
            first = i * part + b * sz.rows_p
            line = jnp.concatenate(
                [jnp.zeros((1, sz.gain_lane), jnp.float32)]
                + [rows[r : r + 1, first : first + sz.rows] for r in (2, 0, 1)]
                + [jnp.zeros((1, sz.pack - sz.gain_lane - 3 * sz.rows), jnp.float32)],
                axis=1,
            )
            block = grad[b * sz.rows_p : (b + 1) * sz.rows_p]
            is_line = lax.broadcasted_iota(jnp.int32, block.shape, 0) == sz.rows
            block = jnp.where(is_line, line, block).astype(jnp.bfloat16)
            pq[i, b // sz.side, b % sz.side] = block
    order.until("gi")
    scaled = gain_one * d_normed
    d_hid = (
        dhid[...]
        + inv_first * scaled
        - hidden * (inv_first**3 * (jnp.sum(scaled * hidden, axis=-1, keepdims=True) / sz.width))
    )
    ghid_out[...] = tokens_out(sz, d_hid)
    order.until("fin")

    def whole(tensor):
        return jnp.concatenate(
            [flows[name].total() for name in flows if name[0] == tensor], axis=1
        )

    gd_out[...] = narrow(sz, whole("d"))[: sz.ffn_rows]
    gg_out[...] = blocks_cut(whole("g"), sz.ffn_rows, sz.ffn_rows_p)[: sz.rows]
    gu_out[...] = blocks_cut(whole("u"), sz.ffn_rows, sz.ffn_rows_p)[: sz.rows]
    go_out[...] = narrow(sz, whole("o"))[: sz.rows]
    grad = whole("q")
    gq_out[...] = grad[: sz.rows, :qc]
    gk_out[...] = grad[: sz.rows, qc : qc + kc]
    gv_out[...] = grad[: sz.rows, qc + kc : qc + 2 * kc]
    for r, ref in enumerate((gain1_out, gain2_out, router_out)):
        first = sz.gain_lane + r * sz.rows
        ref[...] = grad[sz.rows : sz.rows + 1, first : first + sz.rows]
    total = jnp.zeros((8, LANES), jnp.float32)
    for i, j, k in chips_of(sz):
        total = total + err[i, j, k]
    loss_out[...] = total / (sz.width * small_in[3:4, :LANES])
    for flow in flows.values():
        flow.run(5)
    for cp in (x_n, x_pack, x_small, x_err):
        cp.sent()


def count_copies(sz, flows_of, more):
    sems = Sems()
    tensors = dict.fromkeys("qogud")
    flows_of(sz, Place(sz.chips, True), sems, tensors)
    return sems.used + more


def deliver_kernel(*refs):
    half = len(refs) // 2
    for source, target in zip(refs[: half - 1], refs[half:-1]):
        target[...] = source[...]
    refs[-1][0, 0] = refs[half - 1][0, 0]


def body(chips, hidden_in, segment_ids, route_mask, valid_mask, teacher, norm_gain, w_query, w_key,
         w_value, w_out, ffn_gain, w_gate, w_up, w_down, router_weight):
    sz = Sizes(chips, hidden_in.shape, w_gate.shape, w_down.shape)
    t = sz.tokens
    gains = jnp.concatenate([norm_gain, ffn_gain, router_weight])[None]
    low, f32 = jnp.bfloat16, jnp.float32
    grid = sz.grid
    any_spec, vmem_spec = pl.BlockSpec(memory_space=pl.ANY), pl.BlockSpec(memory_space=pltpu.VMEM)
    shape = jax.ShapeDtypeStruct
    gate_shape = grid + (sz.rows_p, sz.ffn_half)
    out_shape = grid + (sz.rows_p, sz.half)
    down_shape = grid + (sz.ffn_rows_p, sz.half)
    pack_shape = grid + (sz.rows_p, sz.pack)
    kv_shape = grid + (t, sz.kv_wide)
    head_shape = (sz.steps, sz.step_rows, LANES)
    prob_shape = (sz.steps, sz.step_rows, sz.keys)
    copies = count_copies(sz, lambda *a: forward_flows(*a, None), 7)
    outs = pl.pallas_call(
        functools.partial(forward_kernel, sz),
        out_shape=[
            shape((sz.width, t), low),
            shape((t, sz.wide), f32),
            shape((8, sz.wide), f32),
            shape((2,) + pack_shape, low),
            shape(kv_shape, low),
            shape(prob_shape, low),
            shape(head_shape, low),
            shape(head_shape, low),
            shape((t, LANES), f32),
            shape((t, LANES), f32),
            shape(gate_shape, low),
            shape(gate_shape, low),
            shape(out_shape, low),
            shape(down_shape, low),
        ],
        in_specs=[vmem_spec] * 13,
        out_specs=[vmem_spec] * 3 + [any_spec] * 3 + [vmem_spec] * 4 + [any_spec] * 4,
        scratch_shapes=[
            pltpu.VMEM((2,) + pack_shape, low),
            pltpu.VMEM((2,) + out_shape, low),
            pltpu.VMEM((2,) + gate_shape, low),
            pltpu.VMEM((2,) + gate_shape, low),
            pltpu.VMEM((2,) + down_shape, low),
            pltpu.VMEM(kv_shape, low),
            pltpu.VMEM((t, sz.keys), sz.bias_type),
            pltpu.VMEM((sz.slots, sz.step_rows, sz.keys), low),
            pltpu.VMEM(head_shape, low),
            pltpu.VMEM((t, sz.wide), f32),
            pltpu.VMEM((2 * t, sz.wide), low),
            pltpu.VMEM((2, 2 * t, sz.ffn_half), low),
            pltpu.VMEM((2, t, sz.ffn_half), f32),
            pltpu.VMEM((2, t, sz.ffn_half), f32),
            pltpu.VMEM((2 * t, sz.wide), low),
            pltpu.VMEM((2 * t, sz.half), low),
            pltpu.VMEM((2 * t, sz.half), low),
            pltpu.VMEM((2 * t, sz.ffn_half), low),
            pltpu.VMEM((2 * t, sz.ffn_half), low),
            pltpu.VMEM((2, t, sz.half), low),
            pltpu.VMEM((2, t, sz.ffn_half), low),
            pltpu.VMEM((t, 8), f32),
            pltpu.SemaphoreType.DMA((copies,)),
            pltpu.SemaphoreType.DMA((copies,)),
            pltpu.SemaphoreType.DMA((16,)),
        ],
        compiler_params=pltpu.CompilerParams(
            collective_id=0, has_side_effects=True, vmem_limit_bytes=VMEM_LIMIT
        ),
        name="forward",
    )(
        w_query, w_key, w_value, w_out, w_gate, w_up, w_down, gains,
        segment_ids, route_mask, valid_mask, hidden_in[0].T, teacher[0].T,
    )
    state, dhid, small, wq_all, kv_all, prob, heads, dctx, cosine, sine, pg, pu, po, pd = outs

    lands = []
    for name, tensor, first, span in pack_flows(sz) + weight_flows(sz):
        rows = sz.ffn_rows_p if tensor == "d" else sz.rows_p
        lands += land_shapes(grid, ORDERS[name[1]], rows, span)
    for name, r0, rn, first, span in kv_flows(sz):
        lands += land_shapes(grid, ORDERS[name[1]], rn, span)
    copies = count_copies(sz, lambda *a: backward_flows(*a, None, None, None), 4)
    outs = pl.pallas_call(
        functools.partial(backward_kernel, sz),
        out_shape=[
            shape((sz.width, t), low),
            shape((sz.rows, sz.q_cols), f32),
            shape((sz.rows, sz.k_cols), f32),
            shape((sz.rows, sz.k_cols), f32),
            shape((sz.rows, sz.width // 2), f32),
            shape((sz.rows, sz.ffn_cols), f32),
            shape((sz.rows, sz.ffn_cols), f32),
            shape((sz.ffn_rows, sz.width // 2), f32),
            shape((1, sz.rows), f32),
            shape((1, sz.rows), f32),
            shape((1, sz.rows), f32),
            shape((8, LANES), f32),
        ],
        in_specs=[any_spec] * 3 + [vmem_spec] * 2 + [any_spec] * 4 + [vmem_spec] * 5,
        out_specs=[vmem_spec] * 12,
        scratch_shapes=[
            pltpu.VMEM((2,) + pack_shape, low),
            pltpu.VMEM(kv_shape, low),
            pltpu.VMEM((2, sz.step_rows // sz.row_parts, sz.keys), low),
            pltpu.VMEM(head_shape, f32),
            pltpu.VMEM((2 * t, sz.wide), low),
            pltpu.VMEM((2 * t, sz.pack), low),
            pltpu.VMEM((t, sz.pack), low),
            pltpu.VMEM(gate_shape, low),
            pltpu.VMEM(gate_shape, low),
            pltpu.VMEM(out_shape, low),
            pltpu.VMEM(down_shape, low),
            pltpu.VMEM((4, 8, sz.wide), f32),
            pltpu.VMEM(grid + (8, LANES), f32),
            lands,
            pltpu.SemaphoreType.DMA((copies,)),
            pltpu.SemaphoreType.DMA((copies,)),
            pltpu.SemaphoreType.DMA((16,)),
        ],
        compiler_params=pltpu.CompilerParams(
            collective_id=1, has_side_effects=True, vmem_limit_bytes=VMEM_LIMIT
        ),
        name="backward",
    )(wq_all, kv_all, prob, heads, dctx, pg, pu, po, pd, hidden_in[0].T, dhid, small, cosine, sine)
    outs = [state] + list(outs)
    last = len(outs) - 1
    state, ghid, gq, gk, gv, go, gg, gu, gd, gain1, gain2, router, loss = pl.pallas_call(
        deliver_kernel,
        out_shape=[shape(o.shape, o.dtype) for o in outs[:-1]] + [shape((1, 1), f32)],
        in_specs=[vmem_spec] * (last + 1),
        out_specs=[vmem_spec] * last + [pl.BlockSpec(memory_space=pltpu.SMEM)],
        name="deliver",
    )(*outs)
    return (
        state.T[None],
        loss.reshape(()),
        ghid.T[None],
        gain1.reshape(-1),
        gq,
        gk,
        gv,
        go,
        gain2.reshape(-1),
        gg,
        gu,
        gd,
        router.reshape(-1),
    )


def solution(mesh):
    tokens, rows, blocks = P("dp", "seq", None), P("dp", "seq"), P("seq", "dp")
    vector = P("seq")
    return jax.shard_map(
        functools.partial(body, mesh.shape["seq"]),
        mesh=mesh,
        in_specs=(
            tokens, rows, rows, rows, tokens, vector, blocks, blocks, blocks, blocks, vector,
            blocks, blocks, blocks, vector,
        ),
        out_specs=(
            tokens, P(), tokens, vector, blocks, blocks, blocks, blocks, vector, blocks, blocks,
            blocks, vector,
        ),
        check_vma=False,
    )
```

```python
import functools
import math

import jax
import jax.numpy as jnp
from jax import lax
from jax.experimental import pallas as pl
from jax.experimental.pallas import tpu as pltpu
from jax.sharding import PartitionSpec as P

HEADS = 15
KV_HEADS = 5
HEAD_DIM = 64
GROUPS = HEADS // KV_HEADS
LANES = 128

norm_eps = 1e-05
masked_score = -1e30

MESH = pl.DeviceIdType.MESH
VMEM_LIMIT = 62 * 2**20

ORDERS = {"A": (2, 0, 1), "B": (1, 0, 2), "C": (0, 2, 1), "D": (0, 1, 2)}


def round_up(value, unit):
    return (value + unit - 1) // unit * unit


class Sizes:
    def __init__(self, chips, hidden_block, gate_block, down_block):
        self.chips = chips
        _, self.tokens, self.width = hidden_block
        self.side = math.isqrt(chips // 4)
        self.grid = (4, self.side, self.side)
        self.keys = self.tokens * chips
        self.rows, _ = gate_block
        self.rows_p = round_up(self.rows, 16)
        self.wide = chips * self.rows_p
        self.half = self.wide // 2
        self.ffn_rows = down_block[0]
        self.ffn_rows_p = round_up(self.ffn_rows, 16)
        self.ffn_half = chips * self.ffn_rows_p // 2
        self.q_cols = HEADS * HEAD_DIM // 2
        self.k_cols = KV_HEADS * HEAD_DIM // 2
        self.cols = self.q_cols + 2 * self.k_cols
        self.pack = round_up(self.cols, LANES)
        self.ffn_cols = gate_block[1]
        self.gain_lane = 3 * self.tokens
        assert self.rows < self.rows_p and self.gain_lane + 3 * self.rows <= self.pack
        self.step_heads = GROUPS if self.keys <= 4096 else 1
        self.steps = HEADS // self.step_heads
        self.steps_per_kv = GROUPS // self.step_heads
        self.step_rows = self.step_heads * self.tokens
        self.kv_wide = KV_HEADS * LANES
        self.slots = 2 if self.keys <= 4096 else 1
        self.row_parts = 1 if self.keys <= 4096 else 4
        self.bias_type = jnp.float32 if self.keys <= 4096 else jnp.bfloat16


class Place:
    def __init__(self, chips, count_only=False):
        side = math.isqrt(chips // 4)
        self.sizes = (4, side, side)
        self.strides = (side * side, side, 1)
        if count_only:
            self.core, self.chip, self.pos = 0, 0, (0, 0, 0)
            return
        self.core = lax.axis_index("dp")
        self.chip = lax.axis_index("seq")
        self.pos = (
            self.chip // (side * side),
            lax.rem(self.chip // side, side),
            lax.rem(self.chip, side),
        )

    def step(self, axis, k):
        size = self.sizes[axis]
        if size == 2:
            return 1 - self.pos[axis]
        return lax.rem(self.pos[axis] + (k + size) % size, size)

    def at(self, axis, other):
        return (self.core, self.chip + (other - self.pos[axis]) * self.strides[axis])

    def peer(self):
        return (1 - self.core, self.chip)

    def greet(self):
        barrier = pltpu.get_barrier_semaphore()
        devices = [self.peer()]
        for axis, size in enumerate(self.sizes):
            devices += [self.at(axis, self.step(axis, k)) for k in range(1, size)]
        for dev in devices:
            pl.semaphore_signal(barrier, inc=1, device_id=dev, device_id_type=MESH)
        pl.semaphore_wait(barrier, len(devices))


class Sems:
    def __init__(self, send=None, recv=None):
        self.send, self.recv, self.used = send, recv, 0

    def take(self):
        self.used += 1
        return self.used - 1


class Copy:
    def __init__(self, sems, src, dst, dev, come):
        self.i, self.sems = sems.take(), sems
        self.src, self.dst, self.dev, self.come = src, dst, dev, come

    def _make(self, src, dst):
        return pltpu.make_async_remote_copy(
            src_ref=src(),
            dst_ref=dst(),
            send_sem=self.sems.send.at[self.i],
            recv_sem=self.sems.recv.at[self.i],
            device_id=self.dev,
            device_id_type=MESH,
        )

    def start(self):
        self._make(self.src, self.dst).start()

    def sent(self):
        self._make(self.src, self.dst).wait_send()

    def came(self):
        self._make(self.come, self.come).wait_recv()


class Gather:
    def __init__(self, place, sems, view, order, twin=None):
        self.place, self.view, self.twin, self.order = place, view, twin, order
        a, b, c = order
        size, pos = place.sizes, place.pos
        self.all = []
        self.first = [
            self._line(sems, a, k, lambda j: self._ref(j, pos[b], pos[c]))
            for k in range(1, size[a])
        ]
        self.second = [
            self._line(sems, b, k, lambda j: self._ref(None, j, pos[c]))
            for k in range(1, size[b])
        ]
        self.third, self.cross = [], []
        for m in range(size[b]):
            jb = pos[b] if m == 0 else place.step(b, -m)
            self.third.append(
                [
                    self._line(sems, c, k, lambda j, jb=jb: self._ref(None, jb, j))
                    for k in range(1, size[c])
                ]
            )
            self.cross.append(
                [
                    self._cross(sems, jb, pos[c] if k == 0 else place.step(c, -k))
                    for k in range(size[c])
                ]
            )

    def _ref(self, ia, ib, ic, twin=False):
        idx = [None] * 3
        for axis, i in zip(self.order, (ia, ib, ic)):
            idx[axis] = slice(None) if i is None else i
        return (self.twin if twin else self.view)(*idx)

    def _line(self, sems, axis, k, unit):
        mine = lambda: unit(self.place.pos[axis])
        dev = self.place.at(axis, self.place.step(axis, k))
        c = Copy(sems, mine, mine, dev, lambda: unit(self.place.step(axis, -k)))
        self.all.append(c)
        return c

    def _cross(self, sems, jb, jc):
        if self.twin is None:
            return None
        here = lambda: self._ref(None, jb, jc)
        c = Copy(sems, here, here, self.place.peer(), lambda: self._ref(None, jb, jc, True))
        self.all.append(c)
        return c

    def _spread(self, m):
        for c in self.third[m]:
            c.start()
        if self.twin is not None:
            self.cross[m][0].start()

    def run(self, r):
        if r == 0:
            for c in self.first:
                c.start()
        elif r == 1:
            for c in self.first:
                c.came()
            for c in self.second:
                c.start()
            self._spread(0)
        elif r == 2:
            for m, c in enumerate(self.second):
                c.came()
                self._spread(m + 1)
        elif r == 3:
            for line, cross in zip(self.third, self.cross):
                for k, c in enumerate(line):
                    c.came()
                    if self.twin is not None:
                        cross[k + 1].start()
        elif r == 4:
            if self.twin is not None:
                for cross in self.cross:
                    for c in cross:
                        c.came()
        else:
            for c in self.all:
                c.sent()


class Scatter:
    def __init__(self, place, sems, view, order, lands):
        self.place, self.view, self.order = place, view, order
        self.lands = lands
        a, b, c = order
        size, pos = place.sizes, place.pos
        self.all = []
        self.first, self.second, self.third = [], [], []
        land_c, land_b, land_a = lands if lands is not None else (None,) * 3
        for m in list(range(1, size[b])) + [0]:
            jb = pos[b] if m == 0 else place.step(b, m)
            self.first.append(
                (
                    m,
                    jb,
                    [
                        self._line(
                            sems, c, k, lambda j, jb=jb: self._ref(None, jb, j),
                            land_c, m * (size[c] - 1) + k - 1,
                        )
                        for k in range(1, size[c])
                    ],
                )
            )
        for m in range(1, size[b]):
            self.second.append(
                self._line(sems, b, m, lambda j: self._ref(None, j, pos[c]), land_b, m - 1)
            )
        for k in range(1, size[a]):
            self.third.append(
                self._line(sems, a, k, lambda j: self._ref(j, pos[b], pos[c]), land_a, k - 1)
            )

    def _ref(self, ia, ib, ic):
        idx = [None] * 3
        for axis, i in zip(self.order, (ia, ib, ic)):
            idx[axis] = slice(None) if i is None else i
        return self.view(*idx)

    def _line(self, sems, axis, k, unit, land, slot):
        to = self.place.step(axis, k)
        spot = lambda: land.at[slot]
        c = Copy(sems, lambda: unit(to), spot, self.place.at(axis, to), spot)
        self.all.append(c)
        return c

    def _add(self, ref, land, slots):
        total = ref[...].astype(jnp.float32)
        for s in slots:
            total = total + land[s].astype(jnp.float32)
        return total

    def run(self, r):
        a, b, c = self.order
        size, pos = self.place.sizes, self.place.pos
        if r == 0:
            for _, _, line in self.first:
                for cp in line:
                    cp.start()
        elif r == 1:
            for m, jb, line in self.first:
                for cp in line:
                    cp.came()
                unit = self._ref(None, jb, pos[c])
                slots = [m * (size[c] - 1) + k for k in range(size[c] - 1)]
                unit[...] = self._add(unit, self.lands[0], slots).astype(unit.dtype)
                if m > 0:
                    self.second[m - 1].start()
        elif r == 2:
            for cp in self.second:
                cp.came()
            unit = self._ref(None, pos[b], pos[c])
            unit[...] = self._add(unit, self.lands[1], range(size[b] - 1)).astype(unit.dtype)
            for cp in self.third:
                cp.start()
        elif r == 3:
            for cp in self.third:
                cp.came()
        else:
            for cp in self.all:
                cp.sent()

    def total(self):
        a, b, c = self.order
        unit = self._ref(*(self.place.pos[axis] for axis in self.order))
        return self._add(unit, self.lands[2], range(self.place.sizes[a] - 1))


def land_shapes(grid, order, rows, cols):
    a, b, c = (grid[axis] for axis in order)
    return [
        pltpu.VMEM((b * (c - 1), a, rows, cols), jnp.bfloat16),
        pltpu.VMEM((b - 1, a, rows, cols), jnp.bfloat16),
        pltpu.VMEM((a - 1, rows, cols), jnp.bfloat16),
    ]


def tiles(total, **shares):
    out, at = [], 0
    names = list(shares)
    for name in names:
        span = shares[name] if name != names[-1] else total // LANES - at
        out.append((name, at * LANES, span * LANES))
        at += span
    return out


def weight_flows(sz):
    out = []
    for tensor, total, shares in (
        ("g", sz.ffn_half, dict(A=6, D=4)),
        ("u", sz.ffn_half, dict(B=6, C=4)),
        ("o", sz.half, dict(C=2, D=2)),
        ("d", sz.half, dict(C=2, D=2)),
    ):
        out += [(tensor + name, tensor, first, span) for name, first, span in tiles(total, **shares)]
    return out


def pack_flows(sz):
    return [("q" + n, "q", f, s) for n, f, s in tiles(sz.pack, C=4, D=3)]


def kv_flows(sz):
    half = sz.tokens // 2
    return [("kC", 0, half, 0, sz.kv_wide), ("kD", half, half, 0, sz.kv_wide)]


ORDER = (
    "qD0", "qC0", "others", "uB0", "oD0", "gA0", "qD1", "qC1", "gD0", "oC0", "qD2", "dD0", "oD1",
    "qC2", "gD1", "qD3", "qC3", "qD4", "prep", "dC0", "oC1", "qC4", "oD2", "dD1", "qkv", "kC0",
    "dC1", "dD2", "oC2", "uC0", "oD3", "kC1", "kD0", "gA1", "dD3", "kD1", "oC3", "uB1", "kC2",
    "kD2", "gD2", "heads", "mask", "gA2", "kC3", "kD3", "atta", "uC1", "dC2", "attb", "gD3",
    "gD4", "gA3", "uB2", "uC2", "oC4", "attc", "dD4", "attd", "dC3", "oD4", "atte", "uB3", "uC3",
    "out", "gA4", "uC4", "dC4", "uB4", "gu", "down", "bwd", "pd", "pg", "GD0", "GA0", "pu", "po",
    "UB0", "DC0", "batta", "battb", "battc", "GA1", "battd", "batte", "OD0", "KC0", "UB1", "DC1",
    "OD1", "GD1", "KC1", "DC2", "KD0", "DD0", "OC0", "KC2", "KD1", "UC0", "OD2", "KC3", "KD2",
    "OC1", "GD2", "qs", "EC0", "DD1", "UC1", "KD3", "kq", "EC1", "OC2", "QD0", "QC0", "OD3",
    "UC2", "DD2", "DC3", "UB2", "QC1", "QD1", "QC2", "GD3", "QD2", "GA2", "GA3", "OC3", "UC3",
    "DD3", "UB3", "gi", "EC2", "QC3", "QD3", "EC3", "fin",
)


class Order:
    def __init__(self, flows, words):
        self.flows, self.words, self.at = flows, words, 0

    def until(self, mark):
        while self.words[self.at] != mark:
            word = self.words[self.at]
            self.flows[word[:-1]].run(int(word[-1]))
            self.at += 1
        self.at += 1


class Link:
    def __init__(self, sz, words, send, recv, local):
        self.place, self.sems, self.local = Place(sz.chips), Sems(send, recv), local
        self.flows, self.used = {}, 0
        self.order = Order(self.flows, words)

    def slot(self, count=1):
        self.used += count
        return self.used - count

    def bring(self, src, dst):
        return pltpu.make_async_copy(src, dst, self.local.at[self.slot()])

    def to_peer(self, src, dst):
        return Copy(self.sems, lambda: src, lambda: dst, self.place.peer(), lambda: dst)


def dot(left, right):
    return jnp.dot(left, right, preferred_element_type=jnp.float32)


def dot_nt(left, right):
    return lax.dot_general(
        left, right, (((1,), (1,)), ((), ())), preferred_element_type=jnp.float32
    )


def dot_tn(left, right):
    return lax.dot_general(
        left, right, (((0,), (0,)), ((), ())), preferred_element_type=jnp.float32
    )


def blocks_padded(value, block, block_p):
    if block == block_p:
        return value
    zero = jnp.zeros((value.shape[0], block_p - block), value.dtype)
    pieces = []
    for j in range(value.shape[1] // block):
        pieces += [value[:, j * block : (j + 1) * block], zero]
    return jnp.concatenate(pieces, axis=1)


def blocks_cut(value, block, block_p):
    if block == block_p:
        return value
    return jnp.concatenate(
        [value[:, j * block_p : j * block_p + block] for j in range(value.shape[1] // block_p)],
        axis=1,
    )


def spread(sz, value):
    return blocks_padded(value, sz.rows, sz.rows_p)


def narrow(sz, value):
    return blocks_cut(value, sz.rows, sz.rows_p)


def tokens_in(sz, ref):
    value = ref[...].astype(jnp.float32)
    zero = jnp.zeros((sz.rows_p - sz.rows, sz.tokens), jnp.float32)
    pieces = []
    for j in range(sz.chips):
        pieces += [value[j * sz.rows : (j + 1) * sz.rows], zero]
    return jnp.concatenate(pieces, axis=0).T


def tokens_out(sz, value):
    value = value.T
    pieces = [value[j * sz.rows_p : j * sz.rows_p + sz.rows] for j in range(sz.chips)]
    return jnp.concatenate(pieces, axis=0).astype(jnp.bfloat16)


def rows_padded(value, rows):
    if value.shape[0] < rows:
        zero = jnp.zeros((rows - value.shape[0], value.shape[1]), value.dtype)
        value = jnp.concatenate([value, zero], axis=0)
    return value.astype(jnp.bfloat16)


def lane_index(shape):
    return lax.broadcasted_iota(jnp.int32, shape, len(shape) - 1)


def swap_halves(value):
    span = value.shape[1]
    first = lax.rem(lane_index(value.shape), HEAD_DIM) < HEAD_DIM // 2
    return jnp.where(
        first,
        pltpu.roll(value, span - HEAD_DIM // 2, 1),
        pltpu.roll(value, HEAD_DIM // 2, 1),
    )


def repeat_lanes(table, span):
    return jnp.concatenate([table] * (span // LANES), axis=1)


def chips_of(sz):
    return [(i, j, k) for i in range(sz.grid[0]) for j in range(sz.side) for k in range(sz.side)]


def gain_row(sz, wq, which):
    first = sz.gain_lane + which * sz.rows
    zero = jnp.zeros((1, sz.rows_p - sz.rows), jnp.float32)
    pieces = []
    for i, j, k in chips_of(sz):
        line = wq[0, i, j, k, sz.rows : sz.rows + 1, :].astype(jnp.float32)
        pieces += [line[:, first : first + sz.rows], zero]
    return jnp.concatenate(pieces, axis=1)


def rotary_tables(sz, place):
    lane = lane_index((sz.tokens, LANES))
    row = lax.broadcasted_iota(jnp.int32, (sz.tokens, LANES), 0)
    half = HEAD_DIM // 2
    place_of = (place.chip * sz.tokens + row).astype(jnp.float32)
    inv_freq = jnp.exp(lax.rem(lane, half).astype(jnp.float32) * (-math.log(10000.0) / half))
    angles = place_of * inv_freq
    sine = jnp.sin(angles)
    return jnp.cos(angles), jnp.where(lax.rem(lane, HEAD_DIM) < half, -sine, sine)


def forward_flows(sz, place, sems, full, kv):
    flows = {}
    for name, tensor, first, span in pack_flows(sz) + weight_flows(sz):

        def view(half, ref=full[tensor], first=first, span=span):
            return lambda i, j, k: ref.at[half, i, j, k, :, pl.ds(first, span)]

        core = place.core
        flows[name] = Gather(place, sems, view(core), ORDERS[name[1].upper()], view(1 - core))
    for name, r0, rn, first, span in kv_flows(sz):

        def view(i, j, k, r0=r0, rn=rn, first=first, span=span):
            return kv.at[i, j, k, pl.ds(r0, rn), pl.ds(first, span)]

        flows[name] = Gather(place, sems, view, ORDERS[name[1].upper()])
    return flows


def backward_flows(sz, place, sems, partial, kv, err, lands):
    flows, at = {}, 0
    for name, tensor, first, span in pack_flows(sz) + weight_flows(sz):

        def view(i, j, k, ref=partial[tensor], first=first, span=span):
            return ref.at[i, j, k, :, pl.ds(first, span)]

        land = None if lands is None else lands[at : at + 3]
        flows[name[0].upper() + name[1:]] = Scatter(place, sems, view, ORDERS[name[1].upper()], land)
        at += 3
    for name, r0, rn, first, span in kv_flows(sz):

        def view(i, j, k, r0=r0, rn=rn, first=first, span=span):
            return kv.at[i, j, k, pl.ds(r0, rn), pl.ds(first, span)]

        land = None if lands is None else lands[at : at + 3]
        flows[name[0].upper() + name[1:]] = Scatter(place, sems, view, ORDERS[name[1].upper()], land)
        at += 3
    flows["EC"] = Gather(place, sems, lambda i, j, k: err.at[i, j, k], ORDERS["C"])
    return flows


def forward_part(
    sz, link,
    q_in, k_in, v_in, out_in, gate_in, up_in, down_in, gains_in, seg_in, route_in, valid_in,
    hid_in, teach_in,
    state_out, dhid_out, small_out, prob_out, heads_out, dctx_out, cos_out, sin_out,
    wq, wo, wg, wu, wd, kv, bias, prob, ctx_h, hid, normed2, act, gate_s, up_s, ctx2, datt2, dffn2,
    dgate2, dup2, stage_d, stage_h, col_in, keep, fused,
):
    place, sems, order, local = link.place, link.sems, link.order, link.local
    core = place.core
    t, n, wide = sz.tokens, sz.chips, sz.wide
    full = {"q": wq, "o": wo, "g": wg, "u": wu, "d": wd}
    flows = forward_flows(sz, place, sems, full, kv)
    link.flows.update(flows)
    own, other = pl.ds(0, t), pl.ds(t, t)
    x_n2 = link.to_peer(normed2.at[own], normed2.at[other])
    x_act = link.to_peer(act.at[:, own], act.at[:, other])
    x_ctx = link.to_peer(ctx2.at[own], ctx2.at[other])
    x_dffn = link.to_peer(stage_d.at[0], dffn2.at[other])
    x_datt = link.to_peer(stage_d.at[1], datt2.at[other])
    x_dgate = link.to_peer(stage_h.at[0], dgate2.at[other])
    x_dup = link.to_peer(stage_h.at[1], dup2.at[other])

    f32 = jnp.float32
    spot = (core,) + place.pos
    marks = [ref[...].astype(f32) for ref in (seg_in, route_in, valid_in)]
    rest = sz.pack - sz.gain_lane - 3 * sz.rows
    line = jnp.concatenate(marks + [gains_in[...].astype(f32), jnp.zeros((1, rest), f32)], axis=1)
    block = jnp.concatenate(
        [ref[...].astype(f32) for ref in (q_in, k_in, v_in)]
        + [jnp.zeros((sz.rows, sz.pack - sz.cols), f32)],
        axis=1,
    )
    wq[spot] = rows_padded(jnp.concatenate([block, line], axis=0), sz.rows_p)
    place.greet()
    order.until("others")
    wo[spot] = rows_padded(spread(sz, out_in[...].astype(f32)), sz.rows_p)
    for ref, own_in in ((wg, gate_in), (wu, up_in)):
        block = blocks_padded(own_in[...].astype(f32), sz.ffn_rows, sz.ffn_rows_p)
        ref[spot] = rows_padded(block, sz.rows_p)
    wd[spot] = rows_padded(spread(sz, down_in[...].astype(f32)), sz.ffn_rows_p)

    order.until("prep")
    hid[...] = tokens_in(sz, hid_in)
    hidden = hid[...]
    inv_first = lax.rsqrt(jnp.sum(hidden * hidden, axis=-1, keepdims=True) / sz.width + norm_eps)
    cos_out[...], sin_out[...] = rotary_tables(sz, place)
    col_in[...] = jnp.concatenate(marks + [jnp.zeros((5, t), f32)], axis=0).T
    cosine, sine = repeat_lanes(cos_out[...], 8 * LANES), repeat_lanes(sin_out[...], 8 * LANES)

    order.until("qkv")
    wq_full = [wq[h].reshape(wide, sz.pack) for h in (0, 1)]
    gain_one = gain_row(sz, wq, 0)
    normed = (hidden * inv_first * gain_one).astype(jnp.bfloat16)
    halves = [dot(normed, w) for w in wq_full]
    qc, kc = sz.q_cols, sz.k_cols
    q_pre = jnp.concatenate(
        [halves[0][:, :qc], halves[1][:, :qc], jnp.zeros((t, 8 * LANES - 2 * qc), jnp.float32)],
        axis=1,
    )
    pad_k = jnp.zeros((t, 3 * LANES - 2 * kc), jnp.float32)
    k_pre = jnp.concatenate(
        [halves[0][:, qc : qc + kc], halves[1][:, qc : qc + kc], pad_k], axis=1
    )
    v_pre = jnp.concatenate(
        [halves[0][:, qc + kc : qc + 2 * kc], halves[1][:, qc + kc : qc + 2 * kc]], axis=1
    )
    k_rot = k_pre * cosine[:, : 3 * LANES] + swap_halves(k_pre) * sine[:, : 3 * LANES]
    kv_own = jnp.concatenate(
        [
            piece[:, g * HEAD_DIM : (g + 1) * HEAD_DIM]
            for g in range(KV_HEADS)
            for piece in (k_rot, v_pre)
        ],
        axis=1,
    )
    kv[place.pos[0], place.pos[1], place.pos[2]] = kv_own.astype(jnp.bfloat16)
    order.until("heads")
    q_rot = q_pre * cosine + swap_halves(q_pre) * sine
    q_low = q_rot.astype(jnp.bfloat16).astype(jnp.float32) * HEAD_DIM ** (-0.5)
    blank = jnp.zeros((t, HEAD_DIM), jnp.float32)
    for h in range(HEADS):
        st, sub = h // sz.step_heads, h % sz.step_heads
        heads_out[st, pl.ds(sub * t, t)] = jnp.concatenate(
            [q_low[:, h * HEAD_DIM : (h + 1) * HEAD_DIM], blank], axis=1
        ).astype(jnp.bfloat16)
    order.until("mask")

    row_at = sz.rows
    seg_col, route_col, valid_col = col_in[:, 0:1], col_in[:, 1:2], col_in[:, 2:3]
    q_pos = place.chip * t + lax.broadcasted_iota(jnp.int32, (t, LANES), 0)
    count = jnp.zeros((1, LANES), jnp.float32)
    for m, (i, j, k) in enumerate(chips_of(sz)):
        line = wq[core, i, j, k, row_at : row_at + 1, : 2 * LANES].astype(jnp.float32)
        seg_row, route_row = line[:, :LANES], line[:, LANES:]
        k_pos = m * t + lane_index((t, LANES))
        allowed = (
            (seg_col == seg_row)
            & (k_pos <= q_pos)
            & ((route_row > 0.5) | (k_pos == q_pos))
        )
        bias[:, m * t : (m + 1) * t] = jnp.where(allowed, 0.0, masked_score).astype(bias.dtype)
        for h in (0, 1):
            count = count + wq[
                h, i, j, k, row_at : row_at + 1, 2 * LANES : 3 * LANES
            ].astype(jnp.float32)
    tok_count = jnp.sum(count, axis=-1, keepdims=True)
    small_out[...] = jnp.zeros(small_out.shape, f32)
    small_out[3:4] = jnp.broadcast_to(tok_count, (1, wide))
    small_out[4:5] = gain_one
    kept = []
    prob_sem = link.slot(sz.slots)

    def attend(st):
        g = st // sz.steps_per_kv
        slot = lax.rem(st, sz.slots)
        lanes = pl.ds(pl.multiple_of(g * LANES, LANES), LANES)
        tile = kv[:, :, :, :, lanes].reshape(sz.keys, LANES)
        s = dot_nt(heads_out[st], tile).reshape(sz.step_heads, t, sz.keys) + bias[...].astype(jnp.float32)[None]
        s = s.reshape(sz.step_rows, sz.keys)
        e = jnp.exp(s - jnp.max(s, axis=-1, keepdims=True))
        p = (e * (1.0 / jnp.sum(e, axis=-1, keepdims=True))).astype(jnp.bfloat16)
        save = pltpu.make_async_copy(prob.at[slot], prob_out.at[st], local.at[prob_sem + slot])

        @pl.when(st >= sz.slots)
        def _():
            save.wait()

        prob[slot] = p
        save.start()
        ctx_h[st] = dot(p, tile).astype(jnp.bfloat16)

    for g in range(KV_HEADS):
        order.until("att%s" % "abcde"[g])
        if g == 0:
            kept += [link.bring(ref, keep[x]) for x, ref in (("q", wq), ("k", kv)) if x in keep]
            for cp in kept:
                cp.start()
        pl.loop(g * sz.steps // KV_HEADS, (g + 1) * sz.steps // KV_HEADS)(attend)
    for slot in range(sz.slots):
        pltpu.make_async_copy(prob.at[slot], prob_out.at[slot], local.at[prob_sem + slot]).wait()

    ctx = jnp.concatenate(
        [
            ctx_h[h // sz.step_heads, pl.ds(h % sz.step_heads * t, t), HEAD_DIM:].astype(jnp.float32)
            for h in range(HEADS)
        ],
        axis=1,
    )
    ctx2[own] = spread(sz, ctx).astype(jnp.bfloat16)
    x_ctx.start()
    order.until("out")
    attn = jnp.concatenate([dot(ctx2[own], wo[q].reshape(wide, sz.half)) for q in (0, 1)], axis=1)
    hidden = hid[...]
    gain_two, router = gain_row(sz, wq, 1), gain_row(sz, wq, 2)
    residual = hidden + attn
    inv_second = lax.rsqrt(
        jnp.sum(residual * residual, axis=-1, keepdims=True) / sz.width + norm_eps
    )
    normed2[own] = (residual * inv_second * gain_two).astype(jnp.bfloat16)
    x_n2.start()
    order.until("gu")
    for h in (0, 1):
        gate_pre = dot(normed2[own], wg[h].reshape(wide, sz.ffn_half))
        up_pre = dot(normed2[own], wu[h].reshape(wide, sz.ffn_half))
        gate_s[h], up_s[h] = gate_pre, up_pre
        act[h, own] = (gate_pre * jax.nn.sigmoid(gate_pre) * up_pre).astype(jnp.bfloat16)
    x_act.start()
    order.until("down")
    two = sz.grid[0] // 2

    def down(q, h):
        return wd[q, pl.ds(h * two, two)].reshape(sz.ffn_half, sz.half)

    ffn = jnp.concatenate(
        [dot(act[0, own], down(q, 0)) + dot(act[1, own], down(q, 1)) for q in (0, 1)], axis=1
    )

    router_sig = jax.nn.sigmoid(jnp.sum(hidden * router, axis=-1, keepdims=True))
    mix = route_col * router_sig
    branch = attn + ffn
    state = hidden + mix * branch
    state_out[...] = tokens_out(sz, state)
    misfit = state - tokens_in(sz, teach_in)
    small_out[2:3] = jnp.sum(valid_col * misfit * misfit, axis=0, keepdims=True)
    d_state = 2.0 / (sz.width * tok_count) * valid_col * misfit
    d_branch = mix * d_state
    d_logit = (
        route_col
        * jnp.sum(d_state * branch, axis=-1, keepdims=True)
        * router_sig
        * (1.0 - router_sig)
    )
    small_out[1:2] = jnp.sum(d_logit * hidden, axis=0, keepdims=True)
    d_ffn = d_branch.astype(jnp.bfloat16)
    low, high = d_ffn[:, : sz.half], d_ffn[:, sz.half :]
    stage_d[0] = jnp.where(core == 0, high, low)
    x_dffn.start()
    dffn2[own] = jnp.where(core == 0, low, high)
    order.until("bwd")
    d_normed2 = jnp.zeros((t, wide), jnp.float32)
    for turn in (1, 0):
        h = core if turn == 0 else 1 - core
        d_act = dot_nt(low, down(0, h)) + dot_nt(high, down(1, h))
        gate_pre, up_pre = gate_s[h], up_s[h]
        sig = jax.nn.sigmoid(gate_pre)
        d_gate = (d_act * up_pre * sig * (1.0 + gate_pre * (1.0 - sig))).astype(jnp.bfloat16)
        d_up = (d_act * (gate_pre * sig)).astype(jnp.bfloat16)
        if turn == 1:
            stage_h[0], stage_h[1] = d_gate, d_up
            x_dgate.start()
            x_dup.start()
        else:
            dgate2[own], dup2[own] = d_gate, d_up
        d_normed2 = (
            d_normed2
            + dot_nt(d_gate, wg[h].reshape(wide, sz.ffn_half))
            + dot_nt(d_up, wu[h].reshape(wide, sz.ffn_half))
        )
    small_out[0:1] = jnp.sum(d_normed2 * residual * inv_second, axis=0, keepdims=True)
    scaled = gain_two * d_normed2
    d_mid = inv_second * scaled - residual * (
        inv_second**3 * (jnp.sum(scaled * residual, axis=-1, keepdims=True) / sz.width)
    )
    dhid_out[...] = d_state + d_logit * router + d_mid
    d_attn = (d_branch + d_mid).astype(jnp.bfloat16)
    low, high = d_attn[:, : sz.half], d_attn[:, sz.half :]
    stage_d[1] = jnp.where(core == 0, high, low)
    x_datt.start()
    datt2[own] = jnp.where(core == 0, low, high)
    d_ctx = dot_nt(low, wo[0].reshape(wide, sz.half)) + dot_nt(high, wo[1].reshape(wide, sz.half))
    d_ctx = narrow(sz, d_ctx)
    for h in range(HEADS):
        st, sub = h // sz.step_heads, h % sz.step_heads
        dctx_out[st, pl.ds(sub * t, t)] = jnp.concatenate(
            [blank, d_ctx[:, h * HEAD_DIM : (h + 1) * HEAD_DIM]], axis=1
        ).astype(jnp.bfloat16)

    for cp in (x_n2, x_act, x_ctx, x_dffn, x_datt, x_dgate, x_dup):
        cp.came()
    for flow in flows.values():
        flow.run(5)
    shape = (sz.side, sz.side)
    pd = wd.at[0]
    if fused:
        order.until("pd")
    for h in (0, 1):
        for i in range(two):
            part = sz.ffn_half // two
            pd[h * two + i] = (
                dot_tn(act[h, :, pl.ds(i * part, part)], dffn2[...])
                .astype(jnp.bfloat16)
                .reshape(shape + (sz.ffn_rows_p, sz.half))
            )
    part = wide // sz.grid[0]
    for name, left, right, ref in (
        ("g", normed2, dgate2, wg.at[0]),
        ("u", normed2, dup2, wu.at[0]),
        ("o", ctx2, datt2, wo.at[0]),
    ):
        if fused:
            order.until("p" + name)
        for i in range(sz.grid[0]):
            ref[i] = (
                dot_tn(left[:, pl.ds(i * part, part)], right[...])
                .astype(jnp.bfloat16)
                .reshape(shape + (sz.rows_p, right.shape[1]))
            )
    for name, ref in (("d", wd), ("g", wg), ("u", wu), ("o", wo)):
        if name in keep:
            kept.append(link.bring(ref.at[0], keep[name]))
            kept[-1].start()
    for cp in kept:
        cp.wait()
    for cp in (x_n2, x_act, x_ctx, x_dffn, x_datt, x_dgate, x_dup):
        cp.sent()


def backward_part(
    sz, link,
    prob_in, heads, dctx, hid_in, dhid, small_in, cos_in, sin_in,
    ghid_out, gq_out, gk_out, gv_out, go_out, gg_out, gu_out, gd_out, gain1_out, gain2_out,
    router_out, loss_out,
    wq, kv, prob, dq_h, normed2, dpack2, stage, small2, fused,
):
    place, order, local = link.place, link.order, link.local
    core = place.core
    t, wide = sz.tokens, sz.wide
    flows, pq = link.back_flows, wq.at[0]
    own, other = pl.ds(0, t), pl.ds(t, t)
    x_n = link.to_peer(normed2.at[own], normed2.at[other])
    x_pack = link.to_peer(stage, dpack2.at[other])
    x_small = link.to_peer(small2.at[0], small2.at[1])
    x_err = link.to_peer(small2.at[2], small2.at[3])
    prob_sem = link.slot(2)
    part_rows = sz.step_rows // sz.row_parts

    def fetch(st, slot):
        rows = pl.ds(lax.rem(st, sz.row_parts) * part_rows, part_rows)
        return pltpu.make_async_copy(
            prob_in.at[st // sz.row_parts, rows], prob.at[slot], local.at[prob_sem + slot]
        )

    fetch(0, 0).start()
    small2[2] = small_in[...]
    if not fused:
        place.greet()
    x_err.start()
    if not fused:
        for name in "dguokq":
            if name in link.gets:
                if name != "k" and name != "q":
                    order.until("p" + name)
                link.gets[name].wait()

    def attend(i, total):
        st = i // sz.row_parts
        slot = lax.rem(i, 2)
        fetch(i, slot).wait()

        @pl.when(i + 1 < sz.steps * sz.row_parts)
        def _():
            fetch(i + 1, 1 - slot).start()

        lanes = pl.ds(pl.multiple_of(st // sz.steps_per_kv * LANES, LANES), LANES)
        tile = kv[:, :, :, :, lanes].reshape(sz.keys, LANES)
        rows = pl.ds(pl.multiple_of(lax.rem(i, sz.row_parts) * part_rows, part_rows), part_rows)
        p_low = prob[slot]
        p = p_low.astype(jnp.float32)
        d_w = dot_nt(dctx[st, rows], tile)
        terms = p * d_w
        delta = jnp.sum(terms, axis=-1, keepdims=True)
        d_s = (terms - p * delta).astype(jnp.bfloat16)
        dq_h[st, rows] = dot(d_s, tile)
        more = dot_tn(heads[st, rows], d_s) + dot_tn(dctx[st, rows], p_low)
        return more if total is None else total + more

    for g in range(KV_HEADS):
        order.until("batt%s" % "abcde"[g])
        each = sz.steps_per_kv * sz.row_parts
        if each == 1:
            total = attend(jnp.int32(g), None)
        else:
            total = jnp.zeros((LANES, sz.keys), jnp.float32)
            total = lax.fori_loop(g * each, (g + 1) * each, attend, total)
        kv[:, :, :, :, pl.ds(g * LANES, LANES)] = (
            total.astype(jnp.bfloat16).T.reshape(sz.grid + (t, LANES))
        )
    order.until("qs")

    wq_full = [wq[h].reshape(wide, sz.pack) for h in (0, 1)]
    gain_one = small_in[4:5]
    hidden = tokens_in(sz, hid_in)
    inv_first = lax.rsqrt(jnp.sum(hidden * hidden, axis=-1, keepdims=True) / sz.width + norm_eps)
    normed2[own] = (hidden * inv_first * gain_one).astype(jnp.bfloat16)
    x_n.start()
    cosine, sine = cos_in[...], sin_in[...]
    scale = HEAD_DIM ** (-0.5)
    dq = jnp.concatenate(
        [
            dq_h[h // sz.step_heads, pl.ds(h % sz.step_heads * t, t), :HEAD_DIM]
            for h in range(HEADS)
        ]
        + [jnp.zeros((t, HEAD_DIM), jnp.float32)],
        axis=1,
    ) * scale
    dq = dq * repeat_lanes(cosine, 8 * LANES) - swap_halves(dq) * repeat_lanes(sine, 8 * LANES)
    d_q = dq.astype(jnp.bfloat16).astype(jnp.float32)

    x_err.came()
    both_err = jnp.sum(small2[2][2:3] + small2[3][2:3], axis=-1, keepdims=True)
    link.err[place.pos[0], place.pos[1], place.pos[2]] = jnp.broadcast_to(both_err, (8, LANES))
    order.until("kq")
    d_kv = jnp.concatenate([flows["KC"].total(), flows["KD"].total()], axis=0)
    in_key = lax.rem(lane_index(d_kv.shape), LANES) < HEAD_DIM
    cos_kv = jnp.where(in_key, repeat_lanes(cosine, sz.kv_wide), 1.0)
    sin_kv = jnp.where(in_key, repeat_lanes(sine, sz.kv_wide), 0.0)
    d_kv = d_kv * cos_kv - swap_halves(d_kv) * sin_kv
    d_kv = d_kv.astype(jnp.bfloat16).astype(jnp.float32)
    d_k = jnp.concatenate(
        [d_kv[:, g * LANES : g * LANES + HEAD_DIM] for g in range(KV_HEADS)], axis=1
    )
    d_v = jnp.concatenate(
        [d_kv[:, g * LANES + HEAD_DIM : (g + 1) * LANES] for g in range(KV_HEADS)], axis=1
    )
    qc, kc = sz.q_cols, sz.k_cols
    blank = jnp.zeros((t, sz.pack - sz.cols), jnp.float32)
    d_pack = [
        jnp.concatenate(
            [
                d_q[:, h * qc : (h + 1) * qc],
                d_k[:, h * kc : (h + 1) * kc],
                d_v[:, h * kc : (h + 1) * kc],
                blank,
            ],
            axis=1,
        ).astype(jnp.bfloat16)
        for h in (0, 1)
    ]
    stage[...] = jnp.where(core == 0, d_pack[1], d_pack[0])
    x_pack.start()
    dpack2[own] = jnp.where(core == 0, d_pack[0], d_pack[1])
    d_normed = dot_nt(d_pack[0], wq_full[0]) + dot_nt(d_pack[1], wq_full[1])
    small2[0] = small_in[...]
    small2[0, 2:3] = jnp.sum(d_normed * hidden * inv_first, axis=0, keepdims=True)
    x_small.start()
    x_n.came()
    x_pack.came()
    x_small.came()
    rows = small2[0] + small2[1]
    part = wide // sz.grid[0]
    shape = (sz.side, sz.side)
    for i in range(sz.grid[0]):
        grad = dot_tn(normed2[:, pl.ds(i * part, part)], dpack2[...])
        for b in range(part // sz.rows_p):
            first = i * part + b * sz.rows_p
            line = jnp.concatenate(
                [jnp.zeros((1, sz.gain_lane), jnp.float32)]
                + [rows[r : r + 1, first : first + sz.rows] for r in (2, 0, 1)]
                + [jnp.zeros((1, sz.pack - sz.gain_lane - 3 * sz.rows), jnp.float32)],
                axis=1,
            )
            block = grad[b * sz.rows_p : (b + 1) * sz.rows_p]
            is_line = lax.broadcasted_iota(jnp.int32, block.shape, 0) == sz.rows
            block = jnp.where(is_line, line, block).astype(jnp.bfloat16)
            pq[i, b // sz.side, b % sz.side] = block
    order.until("gi")
    scaled = gain_one * d_normed
    d_hid = (
        dhid[...]
        + inv_first * scaled
        - hidden * (inv_first**3 * (jnp.sum(scaled * hidden, axis=-1, keepdims=True) / sz.width))
    )
    ghid_out[...] = tokens_out(sz, d_hid)
    order.until("fin")

    def whole(tensor):
        return jnp.concatenate(
            [flows[name].total() for name in flows if name[0] == tensor], axis=1
        )

    gd_out[...] = narrow(sz, whole("D"))[: sz.ffn_rows]
    gg_out[...] = blocks_cut(whole("G"), sz.ffn_rows, sz.ffn_rows_p)[: sz.rows]
    gu_out[...] = blocks_cut(whole("U"), sz.ffn_rows, sz.ffn_rows_p)[: sz.rows]
    go_out[...] = narrow(sz, whole("O"))[: sz.rows]
    grad = whole("Q")
    gq_out[...] = grad[: sz.rows, :qc]
    gk_out[...] = grad[: sz.rows, qc : qc + kc]
    gv_out[...] = grad[: sz.rows, qc + kc : qc + 2 * kc]
    for r, ref in enumerate((gain1_out, gain2_out, router_out)):
        first = sz.gain_lane + r * sz.rows
        ref[...] = grad[sz.rows : sz.rows + 1, first : first + sz.rows]
    total = jnp.zeros((8, LANES), jnp.float32)
    for i, j, k in chips_of(sz):
        total = total + link.err[i, j, k]
    loss_out[...] = total / (sz.width * small_in[3:4, :LANES])
    for flow in flows.values():
        flow.run(5)
    for cp in (x_n, x_pack, x_small, x_err):
        cp.sent()


FORWARD_INS = 13


def set_back_flows(sz, link, partial, kv, err, lands):
    link.err = err
    link.back_flows = backward_flows(sz, link.place, link.sems, partial, kv, err, lands)
    link.flows.update(link.back_flows)


def whole_kernel(sz, *refs):
    at = FORWARD_INS
    ins = refs[:at]
    state, ghid, gq, gk, gv, go, gg, gu, gd, gain1, gain2, router, loss, prob_hbm = refs[at : at + 14]
    refs = refs[at + 14 :]
    dhid, small, heads, dctx, cosine, sine = refs[:6]
    first, refs = refs[6 : 6 + 22], refs[6 + 22 :]
    dq_h, normed2, dpack2, stage, small2, err, lands, send, recv, local = refs
    wq, wo, wg, wu, wd, kv, _, prob = first[:8]
    link = Link(sz, ORDER, send, recv, local)
    partial = {"q": wq, "o": wo, "g": wg, "u": wu, "d": wd}
    partial = {name: ref.at[0] for name, ref in partial.items()}
    set_back_flows(sz, link, partial, kv, err, lands)
    forward_part(
        sz, link, *ins, state, dhid, small, prob_hbm, heads, dctx, cosine, sine, *first, {}, True
    )
    backward_part(
        sz, link, prob_hbm, heads, dctx, ins[11], dhid, small, cosine, sine,
        ghid, gq, gk, gv, go, gg, gu, gd, gain1, gain2, router, loss,
        wq, kv, prob, dq_h, normed2, dpack2, stage, small2, True,
    )


def forward_kernel(sz, *refs):
    at = FORWARD_INS
    ins, refs = refs[:at], refs[at:]
    state, dhid, small, wq_out, kv_out, prob, heads, dctx, cosine, sine = refs[:10]
    keep = dict(zip("qkguod", (wq_out, kv_out) + refs[10:14]))
    first, (send, recv, local) = refs[14 : 14 + 22], refs[14 + 22 :]
    link = Link(sz, ORDER, send, recv, local)
    forward_part(
        sz, link, *ins, state, dhid, small, prob, heads, dctx, cosine, sine, *first, keep, False
    )


def backward_kernel(sz, *refs):
    wq_in, kv_in, prob_in, heads, dctx, pg_in, pu_in, po_in, pd_in, *more = refs[:14]
    outs, refs = refs[14 : 14 + 12], refs[14 + 12 :]
    wq, kv, prob, dq_h, normed2, dpack2, stage, pg, pu, po, pd, small2, err, lands = refs[:14]
    send, recv, local = refs[14:]
    link = Link(sz, ORDER[ORDER.index("bwd") + 1 :], send, recv, local)
    partial = {"q": wq.at[0], "o": po, "g": pg, "u": pu, "d": pd}
    set_back_flows(sz, link, partial, kv, err, lands)
    pairs = ((pd_in, pd), (pg_in, pg), (pu_in, pu), (po_in, po), (kv_in, kv), (wq_in, wq))
    link.gets = {name: link.bring(src, dst) for name, (src, dst) in zip("dguokq", pairs)}
    for cp in link.gets.values():
        cp.start()
    backward_part(
        sz, link, prob_in, heads, dctx, *more, *outs,
        wq, kv, prob, dq_h, normed2, dpack2, stage, small2, False,
    )


def count_copies(sz, flows_of, more):
    sems = Sems()
    tensors = dict.fromkeys("qogud")
    flows_of(sz, Place(sz.chips, True), sems, tensors)
    return sems.used + more


def deliver_kernel(*refs):
    half = len(refs) // 2
    for source, target in zip(refs[: half - 1], refs[half:-1]):
        target[...] = source[...]
    refs[-1][0, 0] = refs[half - 1][0, 0]


def body(chips, hidden_in, segment_ids, route_mask, valid_mask, teacher, norm_gain, w_query, w_key,
         w_value, w_out, ffn_gain, w_gate, w_up, w_down, router_weight):
    sz = Sizes(chips, hidden_in.shape, w_gate.shape, w_down.shape)
    t = sz.tokens
    gains = jnp.concatenate([norm_gain, ffn_gain, router_weight])[None]
    low, f32 = jnp.bfloat16, jnp.float32
    grid = sz.grid
    any_spec, vmem_spec = pl.BlockSpec(memory_space=pl.ANY), pl.BlockSpec(memory_space=pltpu.VMEM)
    shape = jax.ShapeDtypeStruct
    gate_shape = grid + (sz.rows_p, sz.ffn_half)
    out_shape = grid + (sz.rows_p, sz.half)
    down_shape = grid + (sz.ffn_rows_p, sz.half)
    pack_shape = grid + (sz.rows_p, sz.pack)
    kv_shape = grid + (t, sz.kv_wide)
    head_shape = (sz.steps, sz.step_rows, LANES)
    prob_shape = (sz.steps, sz.step_rows, sz.keys)
    copies_f = count_copies(sz, lambda *a: forward_flows(*a, None), 7)
    copies_b = count_copies(sz, lambda *a: backward_flows(*a, None, None, None), 4)
    first_scratch = [
        pltpu.VMEM((2,) + pack_shape, low),
        pltpu.VMEM((2,) + out_shape, low),
        pltpu.VMEM((2,) + gate_shape, low),
        pltpu.VMEM((2,) + gate_shape, low),
        pltpu.VMEM((2,) + down_shape, low),
        pltpu.VMEM(kv_shape, low),
        pltpu.VMEM((t, sz.keys), sz.bias_type),
        pltpu.VMEM((sz.slots, sz.step_rows, sz.keys), low),
        pltpu.VMEM(head_shape, low),
        pltpu.VMEM((t, sz.wide), f32),
        pltpu.VMEM((2 * t, sz.wide), low),
        pltpu.VMEM((2, 2 * t, sz.ffn_half), low),
        pltpu.VMEM((2, t, sz.ffn_half), f32),
        pltpu.VMEM((2, t, sz.ffn_half), f32),
        pltpu.VMEM((2 * t, sz.wide), low),
        pltpu.VMEM((2 * t, sz.half), low),
        pltpu.VMEM((2 * t, sz.half), low),
        pltpu.VMEM((2 * t, sz.ffn_half), low),
        pltpu.VMEM((2 * t, sz.ffn_half), low),
        pltpu.VMEM((2, t, sz.half), low),
        pltpu.VMEM((2, t, sz.ffn_half), low),
        pltpu.VMEM((t, 8), f32),
    ]
    lands = []
    for name, tensor, first, span in pack_flows(sz) + weight_flows(sz):
        rows = sz.ffn_rows_p if tensor == "d" else sz.rows_p
        lands += land_shapes(grid, ORDERS[name[1].upper()], rows, span)
    for name, r0, rn, first, span in kv_flows(sz):
        lands += land_shapes(grid, ORDERS[name[1].upper()], rn, span)
    second_scratch = [
        pltpu.VMEM(head_shape, f32),
        pltpu.VMEM((2 * t, sz.wide), low),
        pltpu.VMEM((2 * t, sz.pack), low),
        pltpu.VMEM((t, sz.pack), low),
    ]
    last_scratch = [pltpu.VMEM((4, 8, sz.wide), f32), pltpu.VMEM(grid + (8, LANES), f32), lands]
    results = [
        shape((sz.width, t), low),
        shape((sz.rows, sz.q_cols), f32),
        shape((sz.rows, sz.k_cols), f32),
        shape((sz.rows, sz.k_cols), f32),
        shape((sz.rows, sz.width // 2), f32),
        shape((sz.rows, sz.ffn_cols), f32),
        shape((sz.rows, sz.ffn_cols), f32),
        shape((sz.ffn_rows, sz.width // 2), f32),
        shape((1, sz.rows), f32),
        shape((1, sz.rows), f32),
        shape((1, sz.rows), f32),
        shape((8, LANES), f32),
    ]
    ins = (
        w_query, w_key, w_value, w_out, w_gate, w_up, w_down, gains,
        segment_ids, route_mask, valid_mask, hidden_in[0].T, teacher[0].T,
    )
    state_shape, dhid_shape = shape((sz.width, t), low), shape((t, sz.wide), f32)
    small_shape, table_shape = shape((8, sz.wide), f32), shape((t, LANES), f32)

    def sem_scratch(copies):
        return [pltpu.SemaphoreType.DMA((count,)) for count in (copies, copies, 16)]

    def params(number):
        return pltpu.CompilerParams(
            collective_id=number, has_side_effects=True, vmem_limit_bytes=VMEM_LIMIT
        )

    if sz.keys <= 4096:
        outs = pl.pallas_call(
            functools.partial(whole_kernel, sz),
            out_shape=[state_shape] + results + [shape(prob_shape, low)],
            in_specs=[vmem_spec] * FORWARD_INS,
            out_specs=[vmem_spec] * 13 + [any_spec],
            scratch_shapes=[
                pltpu.VMEM(dhid_shape.shape, f32),
                pltpu.VMEM(small_shape.shape, f32),
                pltpu.VMEM(head_shape, low),
                pltpu.VMEM(head_shape, low),
                pltpu.VMEM(table_shape.shape, f32),
                pltpu.VMEM(table_shape.shape, f32),
            ]
            + first_scratch
            + second_scratch
            + last_scratch
            + sem_scratch(copies_f + copies_b),
            compiler_params=params(0),
            name="whole",
        )(*ins)
        outs = outs[:-1]
    else:
        outs = pl.pallas_call(
            functools.partial(forward_kernel, sz),
            out_shape=[
                state_shape,
                dhid_shape,
                small_shape,
                shape((2,) + pack_shape, low),
                shape(kv_shape, low),
                shape(prob_shape, low),
                shape(head_shape, low),
                shape(head_shape, low),
                table_shape,
                table_shape,
                shape(gate_shape, low),
                shape(gate_shape, low),
                shape(out_shape, low),
                shape(down_shape, low),
            ],
            in_specs=[vmem_spec] * FORWARD_INS,
            out_specs=[vmem_spec] * 3 + [any_spec] * 3 + [vmem_spec] * 4 + [any_spec] * 4,
            scratch_shapes=first_scratch + sem_scratch(copies_f),
            compiler_params=params(1),
            name="forward",
        )(*ins)
        state, dhid, small, wq_all, kv_all, prob, heads, dctx, cosine, sine, pg, pu, po, pd = outs
        outs = pl.pallas_call(
            functools.partial(backward_kernel, sz),
            out_shape=results,
            in_specs=[any_spec] * 3 + [vmem_spec] * 2 + [any_spec] * 4 + [vmem_spec] * 5,
            out_specs=[vmem_spec] * 12,
            scratch_shapes=[
                pltpu.VMEM((2,) + pack_shape, low),
                pltpu.VMEM(kv_shape, low),
                pltpu.VMEM((2, sz.step_rows // sz.row_parts, sz.keys), low),
            ]
            + second_scratch
            + [
                pltpu.VMEM(gate_shape, low),
                pltpu.VMEM(gate_shape, low),
                pltpu.VMEM(out_shape, low),
                pltpu.VMEM(down_shape, low),
            ]
            + last_scratch
            + sem_scratch(copies_b),
            compiler_params=params(2),
            name="backward",
        )(wq_all, kv_all, prob, heads, dctx, pg, pu, po, pd, ins[11], dhid, small, cosine, sine)
        outs = [state] + list(outs)
    last = len(outs) - 1
    state, ghid, gq, gk, gv, go, gg, gu, gd, gain1, gain2, router, loss = pl.pallas_call(
        deliver_kernel,
        out_shape=[shape(o.shape, o.dtype) for o in outs[:-1]] + [shape((1, 1), f32)],
        in_specs=[vmem_spec] * (last + 1),
        out_specs=[vmem_spec] * last + [pl.BlockSpec(memory_space=pltpu.SMEM)],
        name="deliver",
    )(*outs)
    return (
        state.T[None],
        loss.reshape(()),
        ghid.T[None],
        gain1.reshape(-1),
        gq,
        gk,
        gv,
        go,
        gain2.reshape(-1),
        gg,
        gu,
        gd,
        router.reshape(-1),
    )


def solution(mesh):
    tokens, rows, blocks = P("dp", "seq", None), P("dp", "seq"), P("seq", "dp")
    vector = P("seq")
    return jax.shard_map(
        functools.partial(body, mesh.shape["seq"]),
        mesh=mesh,
        in_specs=(
            tokens, rows, rows, rows, tokens, vector, blocks, blocks, blocks, blocks, vector,
            blocks, blocks, blocks, vector,
        ),
        out_specs=(
            tokens, P(), tokens, vector, blocks, blocks, blocks, blocks, vector, blocks, blocks,
            blocks, vector,
        ),
        check_vma=False,
    )
```

```python
import functools
import math

import jax
import jax.numpy as jnp
from jax import lax
from jax.experimental import pallas as pl
from jax.experimental.pallas import tpu as pltpu
from jax.sharding import PartitionSpec as P

HEADS = 15
KV_HEADS = 5
HEAD_DIM = 64
GROUPS = HEADS // KV_HEADS
LANES = 128

norm_eps = 1e-05
masked_score = -1e30

MESH = pl.DeviceIdType.MESH
VMEM_LIMIT = 62 * 2**20

ORDERS = {"C": (0, 2, 1), "D": (0, 1, 2), "E": (2, 1, 0), "F": (1, 2, 0)}


def round_up(value, unit):
    return (value + unit - 1) // unit * unit


class Sizes:
    def __init__(self, chips, hidden_block, gate_block, down_block):
        self.chips = chips
        _, self.tokens, self.width = hidden_block
        self.side = math.isqrt(chips // 4)
        self.grid = (4, self.side, self.side)
        self.keys = self.tokens * chips
        self.rows, _ = gate_block
        self.rows_p = round_up(self.rows, 16)
        self.wide = chips * self.rows_p
        self.half = self.wide // 2
        self.ffn_rows = down_block[0]
        self.ffn_rows_p = round_up(self.ffn_rows, 16)
        self.ffn_half = chips * self.ffn_rows_p // 2
        self.q_cols = HEADS * HEAD_DIM // 2
        self.k_cols = KV_HEADS * HEAD_DIM // 2
        self.cols = self.q_cols + 2 * self.k_cols
        self.pack = round_up(self.cols, LANES)
        self.out_cols = self.width // 2
        self.full = round_up(self.cols + self.out_cols, LANES)
        self.win = self.cols // LANES * LANES
        self.skip = self.cols - self.win
        self.window = self.full - self.win
        self.ffn_cols = gate_block[1]
        self.gain_lane = 3 * self.tokens
        assert self.rows < self.rows_p and self.gain_lane + 3 * self.rows <= self.win
        self.step_heads = GROUPS if self.keys <= 4096 else 1
        self.steps = HEADS // self.step_heads
        self.steps_per_kv = GROUPS // self.step_heads
        self.step_rows = self.step_heads * self.tokens
        self.kv_wide = KV_HEADS * LANES
        self.slots = 2 if self.keys <= 4096 else 1
        self.row_parts = 1 if self.keys <= 4096 else 4
        self.bias_type = jnp.float32 if self.keys <= 4096 else jnp.bfloat16


class Place:
    def __init__(self, chips, count_only=False):
        side = math.isqrt(chips // 4)
        self.sizes = (4, side, side)
        self.strides = (side * side, side, 1)
        if count_only:
            self.core, self.chip, self.pos = 0, 0, (0, 0, 0)
            return
        self.core = lax.axis_index("dp")
        self.chip = lax.axis_index("seq")
        self.pos = (
            self.chip // (side * side),
            lax.rem(self.chip // side, side),
            lax.rem(self.chip, side),
        )

    def step(self, axis, k):
        size = self.sizes[axis]
        if size == 2:
            return 1 - self.pos[axis]
        return lax.rem(self.pos[axis] + (k + size) % size, size)

    def at(self, axis, other):
        return (self.core, self.chip + (other - self.pos[axis]) * self.strides[axis])

    def peer(self):
        return (1 - self.core, self.chip)

    def greet(self):
        barrier = pltpu.get_barrier_semaphore()
        devices = [self.peer()]
        for axis, size in enumerate(self.sizes):
            devices += [self.at(axis, self.step(axis, k)) for k in range(1, size)]
        for dev in devices:
            pl.semaphore_signal(barrier, inc=1, device_id=dev, device_id_type=MESH)
        pl.semaphore_wait(barrier, len(devices))


class Sems:
    def __init__(self, send=None, recv=None):
        self.send, self.recv, self.used = send, recv, 0

    def take(self):
        self.used += 1
        return self.used - 1


class Copy:
    def __init__(self, sems, src, dst, dev, come):
        self.i, self.sems = sems.take(), sems
        self.src, self.dst, self.dev, self.come = src, dst, dev, come

    def _make(self, src, dst):
        return pltpu.make_async_remote_copy(
            src_ref=src(),
            dst_ref=dst(),
            send_sem=self.sems.send.at[self.i],
            recv_sem=self.sems.recv.at[self.i],
            device_id=self.dev,
            device_id_type=MESH,
        )

    def start(self):
        self._make(self.src, self.dst).start()

    def sent(self):
        self._make(self.src, self.dst).wait_send()

    def came(self):
        self._make(self.come, self.come).wait_recv()


class Gather:
    def __init__(self, place, sems, view, order, twin=None):
        self.place, self.view, self.twin, self.order = place, view, twin, order
        a, b, c = order
        size, pos = place.sizes, place.pos
        self.all = []
        self.first = [
            self._line(sems, a, k, lambda j: self._ref(j, pos[b], pos[c]))
            for k in range(1, size[a])
        ]
        self.second = [
            self._line(sems, b, k, lambda j: self._ref(None, j, pos[c]))
            for k in range(1, size[b])
        ]
        self.third, self.cross = [], []
        for m in range(size[b]):
            jb = pos[b] if m == 0 else place.step(b, -m)
            self.third.append(
                [
                    self._line(sems, c, k, lambda j, jb=jb: self._ref(None, jb, j))
                    for k in range(1, size[c])
                ]
            )
            self.cross.append(
                [
                    self._cross(sems, jb, pos[c] if k == 0 else place.step(c, -k))
                    for k in range(size[c])
                ]
            )

    def _ref(self, ia, ib, ic, twin=False):
        idx = [None] * 3
        for axis, i in zip(self.order, (ia, ib, ic)):
            idx[axis] = slice(None) if i is None else i
        return (self.twin if twin else self.view)(*idx)

    def _line(self, sems, axis, k, unit):
        mine = lambda: unit(self.place.pos[axis])
        dev = self.place.at(axis, self.place.step(axis, k))
        c = Copy(sems, mine, mine, dev, lambda: unit(self.place.step(axis, -k)))
        self.all.append(c)
        return c

    def _cross(self, sems, jb, jc):
        if self.twin is None:
            return None
        here = lambda: self._ref(None, jb, jc)
        c = Copy(sems, here, here, self.place.peer(), lambda: self._ref(None, jb, jc, True))
        self.all.append(c)
        return c

    def _spread(self, m):
        for c in self.third[m]:
            c.start()
        if self.twin is not None:
            self.cross[m][0].start()

    def run(self, r):
        if r == 0:
            for c in self.first:
                c.start()
        elif r == 1:
            for c in self.first:
                c.came()
            for c in self.second:
                c.start()
            self._spread(0)
        elif r == 2:
            for m, c in enumerate(self.second):
                c.came()
                self._spread(m + 1)
        elif r == 3:
            for line, cross in zip(self.third, self.cross):
                for k, c in enumerate(line):
                    c.came()
                    if self.twin is not None:
                        cross[k + 1].start()
        elif r == 4:
            if self.twin is not None:
                for cross in self.cross:
                    for c in cross:
                        c.came()
        else:
            for c in self.all:
                c.sent()


class Scatter:
    def __init__(self, place, sems, view, order, lands):
        self.place, self.view, self.order = place, view, order
        self.lands = lands
        a, b, c = order
        size, pos = place.sizes, place.pos
        self.all = []
        self.first, self.second, self.third = [], [], []
        land_c, land_b, land_a = lands if lands is not None else (None,) * 3
        for m in list(range(1, size[b])) + [0]:
            jb = pos[b] if m == 0 else place.step(b, m)
            self.first.append(
                (
                    m,
                    jb,
                    [
                        self._line(
                            sems, c, k, lambda j, jb=jb: self._ref(None, jb, j),
                            land_c, m * (size[c] - 1) + k - 1,
                        )
                        for k in range(1, size[c])
                    ],
                )
            )
        for m in range(1, size[b]):
            self.second.append(
                self._line(sems, b, m, lambda j: self._ref(None, j, pos[c]), land_b, m - 1)
            )
        for k in range(1, size[a]):
            self.third.append(
                self._line(sems, a, k, lambda j: self._ref(j, pos[b], pos[c]), land_a, k - 1)
            )

    def _ref(self, ia, ib, ic):
        idx = [None] * 3
        for axis, i in zip(self.order, (ia, ib, ic)):
            idx[axis] = slice(None) if i is None else i
        return self.view(*idx)

    def _line(self, sems, axis, k, unit, land, slot):
        to = self.place.step(axis, k)
        spot = lambda: land.at[slot]
        c = Copy(sems, lambda: unit(to), spot, self.place.at(axis, to), spot)
        self.all.append(c)
        return c

    def _add(self, ref, land, slots):
        total = ref[...].astype(jnp.float32)
        for s in slots:
            total = total + land[s].astype(jnp.float32)
        return total

    def run(self, r):
        a, b, c = self.order
        size, pos = self.place.sizes, self.place.pos
        if r == 0:
            for _, _, line in self.first:
                for cp in line:
                    cp.start()
        elif r == 1:
            for m, jb, line in self.first:
                for cp in line:
                    cp.came()
                unit = self._ref(None, jb, pos[c])
                slots = [m * (size[c] - 1) + k for k in range(size[c] - 1)]
                unit[...] = self._add(unit, self.lands[0], slots).astype(unit.dtype)
                if m > 0:
                    self.second[m - 1].start()
        elif r == 2:
            for cp in self.second:
                cp.came()
            unit = self._ref(None, pos[b], pos[c])
            unit[...] = self._add(unit, self.lands[1], range(size[b] - 1)).astype(unit.dtype)
            for cp in self.third:
                cp.start()
        elif r == 3:
            for cp in self.third:
                cp.came()
        else:
            for cp in self.all:
                cp.sent()

    def total(self):
        a, b, c = self.order
        unit = self._ref(*(self.place.pos[axis] for axis in self.order))
        return self._add(unit, self.lands[2], range(self.place.sizes[a] - 1))


def land_shapes(grid, order, rows, cols):
    a, b, c = (grid[axis] for axis in order)
    return [
        pltpu.VMEM((b * (c - 1), a, rows, cols), jnp.bfloat16),
        pltpu.VMEM((b - 1, a, rows, cols), jnp.bfloat16),
        pltpu.VMEM((a - 1, rows, cols), jnp.bfloat16),
    ]


def tiles(total, **shares):
    out, at = [], 0
    names = list(shares)
    for name in names:
        span = shares[name] if name != names[-1] else total // LANES - at
        out.append((name, at * LANES, span * LANES))
        at += span
    return out


def weight_flows(sz):
    out = []
    for tensor, total, shares in (
        ("g", sz.ffn_half, dict(E=3, C=3, D=4)),
        ("u", sz.ffn_half, dict(F=3, C=4, D=3)),
        ("o", sz.full - sz.pack, dict(C=3)),
        ("d", sz.half, dict(C=2, D=2)),
    ):
        at = sz.pack if tensor == "o" else 0
        out += [(tensor + x, tensor, at + first, span) for x, first, span in tiles(total, **shares)]
    return out


def pack_flows(sz):
    return [("q" + n, "q", f, s) for n, f, s in tiles(sz.pack, C=4, D=3)]


def kv_flows(sz):
    half = sz.tokens // 2
    return [("kC", 0, half, 0, sz.kv_wide), ("kD", half, half, 0, sz.kv_wide)]


ORDER = (
    "qC0", "others", "uF0", "qD0", "qC1", "oC0", "qD1", "gC0", "prep", "uC0", "oC1", "gD0",
    "qC2", "qD2", "gE0", "gC1", "qD3", "qD4", "uC1", "uD0", "qC3", "qC4", "qkv", "gD1", "kD0",
    "kC0", "uD1", "kD1", "gD2", "gE1", "kD2", "uC2", "kC1", "gC2", "dD0", "dC0", "oC2", "heads",
    "kC2", "uF1", "dD1", "oC3", "gD3", "gD4", "uF2", "oC4", "mask", "dC1", "gC3", "gE2", "uC3",
    "uC4", "uD2", "kD3", "kC3", "atta", "attb", "dD2", "dC2", "attc", "attd", "uD3", "uF3",
    "gC4", "atte", "out", "uD4", "uF4", "gE3", "dD3", "dC3", "gE4", "gu", "dD4", "dC4", "down",
    "bwd", "pd", "DD0", "bwdb", "pg", "GE0", "DC0", "pu", "bwdc", "UF0", "UD0", "po", "batta",
    "battb", "battc", "DD1", "battd", "batte", "KD0", "KC0", "DC1", "GC0", "GD0", "KD1", "UC0",
    "DD2", "KC1", "DC2", "qs", "EC0", "KD2", "UF1", "GD1", "OC0", "GC1", "KC2", "UD1", "GC2",
    "KD3", "UC1", "KC3", "GD2", "kq", "EC1", "OC1", "gi", "EC2", "UC2", "QC0", "QD0", "GE1",
    "OC2", "UD2", "DC3", "QC1", "UF2", "QD1", "QC2", "UF3", "GD3", "GC3", "DD3", "GE2", "UD3",
    "OC3", "QD2", "QC3", "UC3", "GE3", "QD3", "EC3", "fin",
)


class Order:
    def __init__(self, flows, words):
        self.flows, self.words, self.at = flows, words, 0

    def until(self, mark):
        while self.words[self.at] != mark:
            word = self.words[self.at]
            if word[-1] in "01234":
                self.flows[word[:-1]].run(int(word[-1]))
            self.at += 1
        self.at += 1


class Link:
    def __init__(self, sz, words, send, recv, local):
        self.place, self.sems, self.local = Place(sz.chips), Sems(send, recv), local
        self.flows, self.used = {}, 0
        self.order = Order(self.flows, words)

    def slot(self, count=1):
        self.used += count
        return self.used - count

    def bring(self, src, dst):
        return pltpu.make_async_copy(src, dst, self.local.at[self.slot()])

    def to_peer(self, src, dst):
        return Copy(self.sems, lambda: src, lambda: dst, self.place.peer(), lambda: dst)


def dot(left, right):
    return jnp.dot(left, right, preferred_element_type=jnp.float32)


def dot_nt(left, right):
    return lax.dot_general(
        left, right, (((1,), (1,)), ((), ())), preferred_element_type=jnp.float32
    )


def dot_tn(left, right):
    return lax.dot_general(
        left, right, (((0,), (0,)), ((), ())), preferred_element_type=jnp.float32
    )


def blocks_padded(value, block, block_p):
    if block == block_p:
        return value
    zero = jnp.zeros((value.shape[0], block_p - block), value.dtype)
    pieces = []
    for j in range(value.shape[1] // block):
        pieces += [value[:, j * block : (j + 1) * block], zero]
    return jnp.concatenate(pieces, axis=1)


def blocks_cut(value, block, block_p):
    if block == block_p:
        return value
    return jnp.concatenate(
        [value[:, j * block_p : j * block_p + block] for j in range(value.shape[1] // block_p)],
        axis=1,
    )


def lanes_of(ref, which, first, span):
    value = ref[which, :, :, :, :, pl.ds(first, span)]
    return value.reshape(-1, span)


def beside(*pieces):
    return jnp.concatenate([p for p in pieces if p.shape[1] > 0], axis=1)


def spread(sz, value):
    return blocks_padded(value, sz.rows, sz.rows_p)


def narrow(sz, value):
    return blocks_cut(value, sz.rows, sz.rows_p)


def tokens_in(sz, ref):
    value = ref[...].astype(jnp.float32)
    zero = jnp.zeros((sz.rows_p - sz.rows, sz.tokens), jnp.float32)
    pieces = []
    for j in range(sz.chips):
        pieces += [value[j * sz.rows : (j + 1) * sz.rows], zero]
    return jnp.concatenate(pieces, axis=0).T


def tokens_out(sz, value):
    value = value.T
    pieces = [value[j * sz.rows_p : j * sz.rows_p + sz.rows] for j in range(sz.chips)]
    return jnp.concatenate(pieces, axis=0).astype(jnp.bfloat16)


def rows_padded(value, rows):
    if value.shape[0] < rows:
        zero = jnp.zeros((rows - value.shape[0], value.shape[1]), value.dtype)
        value = jnp.concatenate([value, zero], axis=0)
    return value.astype(jnp.bfloat16)


def lane_index(shape):
    return lax.broadcasted_iota(jnp.int32, shape, len(shape) - 1)


def swap_halves(value):
    span = value.shape[1]
    first = lax.rem(lane_index(value.shape), HEAD_DIM) < HEAD_DIM // 2
    return jnp.where(
        first,
        pltpu.roll(value, span - HEAD_DIM // 2, 1),
        pltpu.roll(value, HEAD_DIM // 2, 1),
    )


def repeat_lanes(table, span):
    return jnp.concatenate([table] * (span // LANES), axis=1)


def chips_of(sz):
    return [(i, j, k) for i in range(sz.grid[0]) for j in range(sz.side) for k in range(sz.side)]


def gain_row(sz, wq, which):
    first = sz.gain_lane + which * sz.rows
    zero = jnp.zeros((1, sz.rows_p - sz.rows), jnp.float32)
    pieces = []
    for i, j, k in chips_of(sz):
        line = wq[0, i, j, k, sz.rows : sz.rows + 1, : sz.win].astype(jnp.float32)
        pieces += [line[:, first : first + sz.rows], zero]
    return jnp.concatenate(pieces, axis=1)


def rotary_tables(sz, place):
    lane = lane_index((sz.tokens, LANES))
    row = lax.broadcasted_iota(jnp.int32, (sz.tokens, LANES), 0)
    half = HEAD_DIM // 2
    place_of = (place.chip * sz.tokens + row).astype(jnp.float32)
    inv_freq = jnp.exp(lax.rem(lane, half).astype(jnp.float32) * (-math.log(10000.0) / half))
    angles = place_of * inv_freq
    sine = jnp.sin(angles)
    return jnp.cos(angles), jnp.where(lax.rem(lane, HEAD_DIM) < half, -sine, sine)


def forward_flows(sz, place, sems, full, kv):
    flows = {}
    for name, tensor, first, span in pack_flows(sz) + weight_flows(sz):

        def view(half, ref=full[tensor], first=first, span=span):
            return lambda i, j, k: ref.at[half, i, j, k, :, pl.ds(first, span)]

        core = place.core
        flows[name] = Gather(place, sems, view(core), ORDERS[name[1].upper()], view(1 - core))
    for name, r0, rn, first, span in kv_flows(sz):

        def view(i, j, k, r0=r0, rn=rn, first=first, span=span):
            return kv.at[i, j, k, pl.ds(r0, rn), pl.ds(first, span)]

        flows[name] = Gather(place, sems, view, ORDERS[name[1].upper()])
    return flows


def backward_flows(sz, place, sems, partial, kv, err, lands):
    flows, at = {}, 0
    for name, tensor, first, span in pack_flows(sz) + weight_flows(sz):

        def view(i, j, k, ref=partial[tensor], first=first, span=span):
            return ref.at[i, j, k, :, pl.ds(first, span)]

        land = None if lands is None else lands[at : at + 3]
        flows[name[0].upper() + name[1:]] = Scatter(place, sems, view, ORDERS[name[1].upper()], land)
        at += 3
    for name, r0, rn, first, span in kv_flows(sz):

        def view(i, j, k, r0=r0, rn=rn, first=first, span=span):
            return kv.at[i, j, k, pl.ds(r0, rn), pl.ds(first, span)]

        land = None if lands is None else lands[at : at + 3]
        flows[name[0].upper() + name[1:]] = Scatter(place, sems, view, ORDERS[name[1].upper()], land)
        at += 3
    flows["EC"] = Gather(place, sems, lambda i, j, k: err.at[i, j, k], ORDERS["C"])
    return flows


def forward_part(
    sz, link,
    q_in, k_in, v_in, out_in, gate_in, up_in, down_in, gains_in, seg_in, route_in, valid_in,
    hid_in, teach_in,
    state_out, dhid_out, small_out, prob_out, heads_out, dctx_out, cos_out, sin_out,
    po6,
    wq, wg, wu, wd, kv, bias, prob, ctx_h, hid, normed2, act, gate_s, up_s, ctx2, datt2, dffn2,
    dgate2, dup2, stage_d, stage_o, stage_h, col_in, keep, fused,
):
    place, sems, order, local = link.place, link.sems, link.order, link.local
    core = place.core
    t, n, wide = sz.tokens, sz.chips, sz.wide
    full = {"q": wq, "o": wq, "g": wg, "u": wu, "d": wd}
    flows = forward_flows(sz, place, sems, full, kv)
    link.flows.update(flows)
    own, other = pl.ds(0, t), pl.ds(t, t)
    x_n2 = link.to_peer(normed2.at[own], normed2.at[other])
    x_act = link.to_peer(act.at[:, own], act.at[:, other])
    x_ctx = link.to_peer(ctx2.at[own], ctx2.at[other])
    x_dffn = link.to_peer(stage_d, dffn2.at[other])
    x_datt = link.to_peer(stage_o, datt2.at[other])
    x_dgate = link.to_peer(stage_h.at[0], dgate2.at[other])
    x_dup = link.to_peer(stage_h.at[1], dup2.at[other])

    f32 = jnp.float32
    spot = (core,) + place.pos
    marks = [ref[...].astype(f32) for ref in (seg_in, route_in, valid_in)]
    rest = sz.full - sz.gain_lane - 3 * sz.rows
    line = jnp.concatenate(marks + [gains_in[...].astype(f32), jnp.zeros((1, rest), f32)], axis=1)
    block = beside(
        *(ref[...].astype(f32) for ref in (q_in, k_in, v_in, out_in)),
        jnp.zeros((sz.rows, sz.full - sz.cols - sz.out_cols), f32),
    )
    wq[spot] = rows_padded(jnp.concatenate([block, line], axis=0), sz.rows_p)
    place.greet()
    order.until("others")
    for ref, own_in in ((wg, gate_in), (wu, up_in)):
        block = blocks_padded(own_in[...].astype(f32), sz.ffn_rows, sz.ffn_rows_p)
        ref[spot] = rows_padded(block, sz.rows_p)
    wd[spot] = rows_padded(spread(sz, down_in[...].astype(f32)), sz.ffn_rows_p)

    order.until("prep")
    hid[...] = tokens_in(sz, hid_in)
    hidden = hid[...]
    inv_first = lax.rsqrt(jnp.sum(hidden * hidden, axis=-1, keepdims=True) / sz.width + norm_eps)
    cos_out[...], sin_out[...] = rotary_tables(sz, place)
    col_in[...] = jnp.concatenate(marks + [jnp.zeros((5, t), f32)], axis=0).T
    cosine, sine = repeat_lanes(cos_out[...], 8 * LANES), repeat_lanes(sin_out[...], 8 * LANES)

    order.until("qkv")
    wq_full = [lanes_of(wq, h, 0, sz.pack) for h in (0, 1)]
    gain_one = gain_row(sz, wq, 0)
    normed = (hidden * inv_first * gain_one).astype(jnp.bfloat16)
    halves = [dot(normed, w) for w in wq_full]
    qc, kc = sz.q_cols, sz.k_cols
    q_pre = jnp.concatenate(
        [halves[0][:, :qc], halves[1][:, :qc], jnp.zeros((t, 8 * LANES - 2 * qc), jnp.float32)],
        axis=1,
    )
    pad_k = jnp.zeros((t, 3 * LANES - 2 * kc), jnp.float32)
    k_pre = jnp.concatenate(
        [halves[0][:, qc : qc + kc], halves[1][:, qc : qc + kc], pad_k], axis=1
    )
    v_pre = jnp.concatenate(
        [halves[0][:, qc + kc : qc + 2 * kc], halves[1][:, qc + kc : qc + 2 * kc]], axis=1
    )
    k_rot = k_pre * cosine[:, : 3 * LANES] + swap_halves(k_pre) * sine[:, : 3 * LANES]
    kv_own = jnp.concatenate(
        [
            piece[:, g * HEAD_DIM : (g + 1) * HEAD_DIM]
            for g in range(KV_HEADS)
            for piece in (k_rot, v_pre)
        ],
        axis=1,
    )
    kv[place.pos[0], place.pos[1], place.pos[2]] = kv_own.astype(jnp.bfloat16)
    order.until("heads")
    q_rot = q_pre * cosine + swap_halves(q_pre) * sine
    q_low = q_rot.astype(jnp.bfloat16).astype(jnp.float32) * HEAD_DIM ** (-0.5)
    blank = jnp.zeros((t, HEAD_DIM), jnp.float32)
    for h in range(HEADS):
        st, sub = h // sz.step_heads, h % sz.step_heads
        heads_out[st, pl.ds(sub * t, t)] = jnp.concatenate(
            [q_low[:, h * HEAD_DIM : (h + 1) * HEAD_DIM], blank], axis=1
        ).astype(jnp.bfloat16)
    order.until("mask")

    row_at = sz.rows
    seg_col, route_col, valid_col = col_in[:, 0:1], col_in[:, 1:2], col_in[:, 2:3]
    q_pos = place.chip * t + lax.broadcasted_iota(jnp.int32, (t, LANES), 0)
    count = jnp.zeros((1, LANES), jnp.float32)
    for m, (i, j, k) in enumerate(chips_of(sz)):
        line = wq[core, i, j, k, row_at : row_at + 1, : 2 * LANES].astype(jnp.float32)
        seg_row, route_row = line[:, :LANES], line[:, LANES:]
        k_pos = m * t + lane_index((t, LANES))
        allowed = (
            (seg_col == seg_row)
            & (k_pos <= q_pos)
            & ((route_row > 0.5) | (k_pos == q_pos))
        )
        bias[:, m * t : (m + 1) * t] = jnp.where(allowed, 0.0, masked_score).astype(bias.dtype)
        for h in (0, 1):
            count = count + wq[
                h, i, j, k, row_at : row_at + 1, 2 * LANES : 3 * LANES
            ].astype(jnp.float32)
    tok_count = jnp.sum(count, axis=-1, keepdims=True)
    small_out[...] = jnp.zeros(small_out.shape, f32)
    small_out[3:4] = jnp.broadcast_to(tok_count, (1, wide))
    small_out[4:5] = gain_one
    kept = []
    prob_sem = link.slot(sz.slots)

    def attend(st):
        g = st // sz.steps_per_kv
        slot = lax.rem(st, sz.slots)
        lanes = pl.ds(pl.multiple_of(g * LANES, LANES), LANES)
        tile = kv[:, :, :, :, lanes].reshape(sz.keys, LANES)
        s = dot_nt(heads_out[st], tile).reshape(sz.step_heads, t, sz.keys) + bias[...].astype(jnp.float32)[None]
        s = s.reshape(sz.step_rows, sz.keys)
        e = jnp.exp(s - jnp.max(s, axis=-1, keepdims=True))
        p = (e * (1.0 / jnp.sum(e, axis=-1, keepdims=True))).astype(jnp.bfloat16)
        save = pltpu.make_async_copy(prob.at[slot], prob_out.at[st], local.at[prob_sem + slot])

        @pl.when(st >= sz.slots)
        def _():
            save.wait()

        prob[slot] = p
        save.start()
        ctx_h[st] = dot(p, tile).astype(jnp.bfloat16)

    for g in range(KV_HEADS):
        order.until("att%s" % "abcde"[g])
        if g == 0:
            kept += [link.bring(ref, keep[x]) for x, ref in (("q", wq), ("k", kv)) if x in keep]
            for cp in kept:
                cp.start()
        pl.loop(g * sz.steps // KV_HEADS, (g + 1) * sz.steps // KV_HEADS)(attend)
    for slot in range(sz.slots):
        pltpu.make_async_copy(prob.at[slot], prob_out.at[slot], local.at[prob_sem + slot]).wait()

    ctx = jnp.concatenate(
        [
            ctx_h[h // sz.step_heads, pl.ds(h % sz.step_heads * t, t), HEAD_DIM:].astype(jnp.float32)
            for h in range(HEADS)
        ],
        axis=1,
    )
    ctx2[own] = spread(sz, ctx).astype(jnp.bfloat16)
    x_ctx.start()
    order.until("out")
    attn = [dot(ctx2[own], lanes_of(wq, q, sz.win, sz.window)) for q in (0, 1)]
    attn = [value[:, sz.skip : sz.skip + sz.out_cols] for value in attn]
    attn = spread(sz, jnp.concatenate(attn, axis=1))
    hidden = hid[...]
    gain_two, router = gain_row(sz, wq, 1), gain_row(sz, wq, 2)
    residual = hidden + attn
    inv_second = lax.rsqrt(
        jnp.sum(residual * residual, axis=-1, keepdims=True) / sz.width + norm_eps
    )
    normed2[own] = (residual * inv_second * gain_two).astype(jnp.bfloat16)
    x_n2.start()
    order.until("gu")
    for h in (0, 1):
        gate_pre = dot(normed2[own], wg[h].reshape(wide, sz.ffn_half))
        up_pre = dot(normed2[own], wu[h].reshape(wide, sz.ffn_half))
        gate_s[h], up_s[h] = gate_pre, up_pre
        act[h, own] = (gate_pre * jax.nn.sigmoid(gate_pre) * up_pre).astype(jnp.bfloat16)
    x_act.start()
    order.until("down")
    two = sz.grid[0] // 2

    def down(q, h):
        return wd[q, pl.ds(h * two, two)].reshape(sz.ffn_half, sz.half)

    ffn = jnp.concatenate(
        [dot(act[0, own], down(q, 0)) + dot(act[1, own], down(q, 1)) for q in (0, 1)], axis=1
    )

    router_sig = jax.nn.sigmoid(jnp.sum(hidden * router, axis=-1, keepdims=True))
    mix = route_col * router_sig
    branch = attn + ffn
    state = hidden + mix * branch
    state_out[...] = tokens_out(sz, state)
    misfit = state - tokens_in(sz, teach_in)
    small_out[2:3] = jnp.sum(valid_col * misfit * misfit, axis=0, keepdims=True)
    d_state = 2.0 / (sz.width * tok_count) * valid_col * misfit
    d_branch = mix * d_state
    d_logit = (
        route_col
        * jnp.sum(d_state * branch, axis=-1, keepdims=True)
        * router_sig
        * (1.0 - router_sig)
    )
    small_out[1:2] = jnp.sum(d_logit * hidden, axis=0, keepdims=True)
    d_ffn = d_branch.astype(jnp.bfloat16)
    low, high = d_ffn[:, : sz.half], d_ffn[:, sz.half :]
    stage_d[...] = jnp.where(core == 0, high, low)
    x_dffn.start()
    dffn2[own] = jnp.where(core == 0, low, high)
    order.until("bwd")
    for turn in (1, 0):
        h = core if turn == 0 else 1 - core
        d_act = dot_nt(low, down(0, h)) + dot_nt(high, down(1, h))
        gate_pre, up_pre = gate_s[h], up_s[h]
        sig = jax.nn.sigmoid(gate_pre)
        d_gate = (d_act * up_pre * sig * (1.0 + gate_pre * (1.0 - sig))).astype(jnp.bfloat16)
        d_up = (d_act * (gate_pre * sig)).astype(jnp.bfloat16)
        if turn == 1:
            stage_h[0], stage_h[1] = d_gate, d_up
            x_dgate.start()
            x_dup.start()
        else:
            dgate2[own], dup2[own] = d_gate, d_up

    def until(mark):
        if fused:
            order.until(mark)

    def copied(tensor):
        for name in flows:
            if name[0] == tensor:
                flows[name].run(5)

    shape, pd = (sz.side, sz.side), wd.at[0]
    until("pd")
    x_act.came()
    x_dffn.came()
    copied("d")
    for h in (0, 1):
        for i in range(two):
            part = sz.ffn_half // two
            pd[h * two + i] = (
                dot_tn(act[h, :, pl.ds(i * part, part)], dffn2[...])
                .astype(jnp.bfloat16)
                .reshape(shape + (sz.ffn_rows_p, sz.half))
            )
    until("bwdb")
    d_normed2 = jnp.zeros((t, wide), jnp.float32)
    for h, d_gate, d_up in (
        (1 - core, stage_h[0], stage_h[1]),
        (core, dgate2[own], dup2[own]),
    ):
        d_normed2 = (
            d_normed2
            + dot_nt(d_gate, wg[h].reshape(wide, sz.ffn_half))
            + dot_nt(d_up, wu[h].reshape(wide, sz.ffn_half))
        )
    x_n2.came()
    part = wide // sz.grid[0]
    for name, came, right, ref in (
        ("g", x_dgate, dgate2, wg.at[0]),
        ("u", x_dup, dup2, wu.at[0]),
    ):
        until("p" + name)
        came.came()
        copied(name)
        for i in range(sz.grid[0]):
            ref[i] = (
                dot_tn(normed2[:, pl.ds(i * part, part)], right[...])
                .astype(jnp.bfloat16)
                .reshape(shape + (sz.rows_p, sz.ffn_half))
            )
    until("bwdc")
    small_out[0:1] = jnp.sum(d_normed2 * residual * inv_second, axis=0, keepdims=True)
    scaled = gain_two * d_normed2
    d_mid = inv_second * scaled - residual * (
        inv_second**3 * (jnp.sum(scaled * residual, axis=-1, keepdims=True) / sz.width)
    )
    dhid_out[...] = d_state + d_logit * router + d_mid
    d_attn = narrow(sz, d_branch + d_mid)
    left = jnp.zeros((t, sz.skip), f32)
    right = jnp.zeros((t, sz.window - sz.skip - sz.out_cols), f32)
    low, high = (
        beside(left, value, right).astype(jnp.bfloat16)
        for value in (d_attn[:, : sz.out_cols], d_attn[:, sz.out_cols :])
    )
    stage_o[...] = jnp.where(core == 0, high, low)
    x_datt.start()
    datt2[own] = jnp.where(core == 0, low, high)
    d_ctx = dot_nt(low, lanes_of(wq, 0, sz.win, sz.window))
    d_ctx = narrow(sz, d_ctx + dot_nt(high, lanes_of(wq, 1, sz.win, sz.window)))
    for h in range(HEADS):
        st, sub = h // sz.step_heads, h % sz.step_heads
        dctx_out[st, pl.ds(sub * t, t)] = jnp.concatenate(
            [blank, d_ctx[:, h * HEAD_DIM : (h + 1) * HEAD_DIM]], axis=1
        ).astype(jnp.bfloat16)
    until("po")
    x_ctx.came()
    x_datt.came()
    for tensor in "oqk":
        copied(tensor)
    for cp in kept:
        cp.wait()
    kept = []
    out_lanes = pl.ds(sz.pack, sz.full - sz.pack)
    edge = sz.pack - sz.win
    for i in range(sz.grid[0]):
        grad = dot_tn(ctx2[:, pl.ds(i * part, part)], datt2[...]).astype(jnp.bfloat16)
        po6[i] = grad[:, :edge].reshape(shape + (sz.rows_p, edge))
        wq[0, i, :, :, :, out_lanes] = grad[:, edge:].reshape(
            shape + (sz.rows_p, sz.full - sz.pack)
        )
    for name, ref in (
        ("d", wd.at[0]),
        ("g", wg.at[0]),
        ("u", wu.at[0]),
        ("o", wq.at[0, :, :, :, :, out_lanes]),
    ):
        if name in keep:
            kept.append(link.bring(ref, keep[name]))
            kept[-1].start()
    for cp in kept:
        cp.wait()
    for cp in (x_n2, x_act, x_ctx, x_dffn, x_datt, x_dgate, x_dup):
        cp.sent()


def backward_part(
    sz, link,
    prob_in, heads, dctx, hid_in, dhid, small_in, cos_in, sin_in,
    po6,
    ghid_out, gq_out, gk_out, gv_out, go_out, gg_out, gu_out, gd_out, gain1_out, gain2_out,
    router_out, loss_out,
    wq, kv, prob, dq_h, normed2, dpack2, stage, small2, fused,
):
    place, order, local = link.place, link.order, link.local
    core = place.core
    t, wide = sz.tokens, sz.wide
    flows = link.back_flows
    own, other = pl.ds(0, t), pl.ds(t, t)
    x_n = link.to_peer(normed2.at[own], normed2.at[other])
    x_pack = link.to_peer(stage, dpack2.at[other])
    x_small = link.to_peer(small2.at[0], small2.at[1])
    x_err = link.to_peer(small2.at[2], small2.at[3])
    prob_sem = link.slot(2)
    part_rows = sz.step_rows // sz.row_parts

    def fetch(st, slot):
        rows = pl.ds(lax.rem(st, sz.row_parts) * part_rows, part_rows)
        return pltpu.make_async_copy(
            prob_in.at[st // sz.row_parts, rows], prob.at[slot], local.at[prob_sem + slot]
        )

    fetch(0, 0).start()
    small2[2] = small_in[...]
    if not fused:
        place.greet()
    x_err.start()
    if not fused:
        for name in "dgu":
            order.until("p" + name)
            link.gets[name].wait()
        link.gets["k"].wait()
        link.gets["q"].wait()
        order.until("po")
        link.gets["o"].start()
        link.gets["o"].wait()

    def attend(i, total):
        st = i // sz.row_parts
        slot = lax.rem(i, 2)
        fetch(i, slot).wait()

        @pl.when(i + 1 < sz.steps * sz.row_parts)
        def _():
            fetch(i + 1, 1 - slot).start()

        lanes = pl.ds(pl.multiple_of(st // sz.steps_per_kv * LANES, LANES), LANES)
        tile = kv[:, :, :, :, lanes].reshape(sz.keys, LANES)
        rows = pl.ds(pl.multiple_of(lax.rem(i, sz.row_parts) * part_rows, part_rows), part_rows)
        p_low = prob[slot]
        p = p_low.astype(jnp.float32)
        d_w = dot_nt(dctx[st, rows], tile)
        terms = p * d_w
        delta = jnp.sum(terms, axis=-1, keepdims=True)
        d_s = (terms - p * delta).astype(jnp.bfloat16)
        dq_h[st, rows] = dot(d_s, tile)
        more = dot_tn(heads[st, rows], d_s) + dot_tn(dctx[st, rows], p_low)
        return more if total is None else total + more

    for g in range(KV_HEADS):
        order.until("batt%s" % "abcde"[g])
        each = sz.steps_per_kv * sz.row_parts
        if each == 1:
            total = attend(jnp.int32(g), None)
        else:
            total = jnp.zeros((LANES, sz.keys), jnp.float32)
            total = lax.fori_loop(g * each, (g + 1) * each, attend, total)
        kv[:, :, :, :, pl.ds(g * LANES, LANES)] = (
            total.astype(jnp.bfloat16).T.reshape(sz.grid + (t, LANES))
        )
    order.until("qs")

    wq_full = [lanes_of(wq, h, 0, sz.pack) for h in (0, 1)]
    gain_one = small_in[4:5]
    hidden = tokens_in(sz, hid_in)
    inv_first = lax.rsqrt(jnp.sum(hidden * hidden, axis=-1, keepdims=True) / sz.width + norm_eps)
    normed2[own] = (hidden * inv_first * gain_one).astype(jnp.bfloat16)
    x_n.start()
    cosine, sine = cos_in[...], sin_in[...]
    scale = HEAD_DIM ** (-0.5)
    dq = jnp.concatenate(
        [
            dq_h[h // sz.step_heads, pl.ds(h % sz.step_heads * t, t), :HEAD_DIM]
            for h in range(HEADS)
        ]
        + [jnp.zeros((t, HEAD_DIM), jnp.float32)],
        axis=1,
    ) * scale
    dq = dq * repeat_lanes(cosine, 8 * LANES) - swap_halves(dq) * repeat_lanes(sine, 8 * LANES)
    d_q = dq.astype(jnp.bfloat16).astype(jnp.float32)

    x_err.came()
    both_err = jnp.sum(small2[2][2:3] + small2[3][2:3], axis=-1, keepdims=True)
    link.err[place.pos[0], place.pos[1], place.pos[2]] = jnp.broadcast_to(both_err, (8, LANES))
    order.until("kq")
    d_kv = jnp.concatenate([flows["KC"].total(), flows["KD"].total()], axis=0)
    in_key = lax.rem(lane_index(d_kv.shape), LANES) < HEAD_DIM
    cos_kv = jnp.where(in_key, repeat_lanes(cosine, sz.kv_wide), 1.0)
    sin_kv = jnp.where(in_key, repeat_lanes(sine, sz.kv_wide), 0.0)
    d_kv = d_kv * cos_kv - swap_halves(d_kv) * sin_kv
    d_kv = d_kv.astype(jnp.bfloat16).astype(jnp.float32)
    d_k = jnp.concatenate(
        [d_kv[:, g * LANES : g * LANES + HEAD_DIM] for g in range(KV_HEADS)], axis=1
    )
    d_v = jnp.concatenate(
        [d_kv[:, g * LANES + HEAD_DIM : (g + 1) * LANES] for g in range(KV_HEADS)], axis=1
    )
    qc, kc = sz.q_cols, sz.k_cols
    blank = jnp.zeros((t, sz.pack - sz.cols), jnp.float32)
    d_pack = [
        jnp.concatenate(
            [
                d_q[:, h * qc : (h + 1) * qc],
                d_k[:, h * kc : (h + 1) * kc],
                d_v[:, h * kc : (h + 1) * kc],
                blank,
            ],
            axis=1,
        ).astype(jnp.bfloat16)
        for h in (0, 1)
    ]
    stage[...] = jnp.where(core == 0, d_pack[1], d_pack[0])
    x_pack.start()
    dpack2[own] = jnp.where(core == 0, d_pack[0], d_pack[1])
    d_normed = dot_nt(d_pack[0], wq_full[0]) + dot_nt(d_pack[1], wq_full[1])
    small2[0] = small_in[...]
    small2[0, 2:3] = jnp.sum(d_normed * hidden * inv_first, axis=0, keepdims=True)
    x_small.start()
    x_n.came()
    x_pack.came()
    x_small.came()
    rows = small2[0] + small2[1]
    part = wide // sz.grid[0]
    shape = (sz.side, sz.side)
    for i in range(sz.grid[0]):
        grad = dot_tn(normed2[:, pl.ds(i * part, part)], dpack2[...])
        for b in range(part // sz.rows_p):
            first = i * part + b * sz.rows_p
            line = jnp.concatenate(
                [jnp.zeros((1, sz.gain_lane), jnp.float32)]
                + [rows[r : r + 1, first : first + sz.rows] for r in (2, 0, 1)]
                + [jnp.zeros((1, sz.pack - sz.gain_lane - 3 * sz.rows), jnp.float32)],
                axis=1,
            )
            block = grad[b * sz.rows_p : (b + 1) * sz.rows_p]
            is_line = lax.broadcasted_iota(jnp.int32, block.shape, 0) == sz.rows
            block = jnp.where(is_line, line, block)
            spot = (i, b // sz.side, b % sz.side)
            edge = block[:, sz.win :] + po6[spot].astype(jnp.float32)
            block = jnp.concatenate([block[:, : sz.win], edge], axis=1).astype(jnp.bfloat16)
            wq[(0,) + spot + (slice(None), pl.ds(0, sz.pack))] = block
    order.until("gi")
    scaled = gain_one * d_normed
    d_hid = (
        dhid[...]
        + inv_first * scaled
        - hidden * (inv_first**3 * (jnp.sum(scaled * hidden, axis=-1, keepdims=True) / sz.width))
    )
    ghid_out[...] = tokens_out(sz, d_hid)
    order.until("fin")

    def whole(tensor):
        return jnp.concatenate(
            [flows[name].total() for name in flows if name[0] == tensor], axis=1
        )

    gd_out[...] = narrow(sz, whole("D"))[: sz.ffn_rows]
    gg_out[...] = blocks_cut(whole("G"), sz.ffn_rows, sz.ffn_rows_p)[: sz.rows]
    gu_out[...] = blocks_cut(whole("U"), sz.ffn_rows, sz.ffn_rows_p)[: sz.rows]
    grad = whole("Q")
    grad_out = jnp.concatenate([grad[:, sz.cols :], whole("O")], axis=1)
    go_out[...] = grad_out[: sz.rows, : sz.out_cols]
    gq_out[...] = grad[: sz.rows, :qc]
    gk_out[...] = grad[: sz.rows, qc : qc + kc]
    gv_out[...] = grad[: sz.rows, qc + kc : qc + 2 * kc]
    for r, ref in enumerate((gain1_out, gain2_out, router_out)):
        first = sz.gain_lane + r * sz.rows
        ref[...] = grad[sz.rows : sz.rows + 1, first : first + sz.rows]
    total = jnp.zeros((8, LANES), jnp.float32)
    for i, j, k in chips_of(sz):
        total = total + link.err[i, j, k]
    loss_out[...] = total / (sz.width * small_in[3:4, :LANES])
    for flow in flows.values():
        flow.run(5)
    for cp in (x_n, x_pack, x_small, x_err):
        cp.sent()


FORWARD_INS = 13


def set_back_flows(sz, link, partial, kv, err, lands):
    link.err = err
    link.back_flows = backward_flows(sz, link.place, link.sems, partial, kv, err, lands)
    link.flows.update(link.back_flows)


def whole_kernel(sz, *refs):
    at = FORWARD_INS
    ins = refs[:at]
    state, ghid, gq, gk, gv, go, gg, gu, gd, gain1, gain2, router, loss, prob_hbm = refs[at : at + 14]
    refs = refs[at + 14 :]
    dhid, small, heads, dctx, cosine, sine, po6 = refs[:7]
    first, refs = refs[7 : 7 + 22], refs[7 + 22 :]
    dq_h, normed2, dpack2, stage, small2, err, lands, send, recv, local = refs
    wq, wg, wu, wd, kv, _, prob = first[:7]
    link = Link(sz, ORDER, send, recv, local)
    partial = {"q": wq, "o": wq, "g": wg, "u": wu, "d": wd}
    partial = {name: ref.at[0] for name, ref in partial.items()}
    set_back_flows(sz, link, partial, kv, err, lands)
    forward_part(
        sz, link, *ins, state, dhid, small, prob_hbm, heads, dctx, cosine, sine, po6, *first, {}, True
    )
    backward_part(
        sz, link, prob_hbm, heads, dctx, ins[11], dhid, small, cosine, sine, po6,
        ghid, gq, gk, gv, go, gg, gu, gd, gain1, gain2, router, loss,
        wq, kv, prob, dq_h, normed2, dpack2, stage, small2, True,
    )


def forward_kernel(sz, *refs):
    at = FORWARD_INS
    ins, refs = refs[:at], refs[at:]
    state, dhid, small, wq_out, kv_out, prob, heads, dctx, cosine, sine, po6 = refs[:11]
    keep = dict(zip("qkguod", (wq_out, kv_out) + refs[11:15]))
    first, (send, recv, local) = refs[15 : 15 + 22], refs[15 + 22 :]
    link = Link(sz, ORDER, send, recv, local)
    forward_part(
        sz, link, *ins, state, dhid, small, prob, heads, dctx, cosine, sine, po6, *first, keep, False
    )


def backward_kernel(sz, *refs):
    wq_in, kv_in, prob_in, heads, dctx, pg_in, pu_in, po_in, pd_in, *more = refs[:15]
    outs, refs = refs[15 : 15 + 12], refs[15 + 12 :]
    wq, kv, prob, dq_h, normed2, dpack2, stage, pg, pu, pd, small2, err, lands = refs[:13]
    send, recv, local = refs[13:]
    link = Link(sz, ORDER[ORDER.index("bwd") + 1 :], send, recv, local)
    partial = {"q": wq.at[0], "o": wq.at[0], "g": pg, "u": pu, "d": pd}
    set_back_flows(sz, link, partial, kv, err, lands)
    po = wq.at[0, :, :, :, :, pl.ds(sz.pack, sz.full - sz.pack)]
    pairs = ((pd_in, pd), (pg_in, pg), (pu_in, pu), (po_in, po), (kv_in, kv), (wq_in, wq))
    link.gets = {name: link.bring(src, dst) for name, (src, dst) in zip("dguokq", pairs)}
    for name, cp in link.gets.items():
        if name != "o":
            cp.start()
    backward_part(
        sz, link, prob_in, heads, dctx, *more, *outs,
        wq, kv, prob, dq_h, normed2, dpack2, stage, small2, False,
    )


def count_copies(sz, flows_of, more):
    sems = Sems()
    tensors = dict.fromkeys("qogud")
    flows_of(sz, Place(sz.chips, True), sems, tensors)
    return sems.used + more


def deliver_kernel(*refs):
    half = len(refs) // 2
    for source, target in zip(refs[: half - 1], refs[half:-1]):
        target[...] = source[...]
    refs[-1][0, 0] = refs[half - 1][0, 0]


def body(chips, hidden_in, segment_ids, route_mask, valid_mask, teacher, norm_gain, w_query, w_key,
         w_value, w_out, ffn_gain, w_gate, w_up, w_down, router_weight):
    sz = Sizes(chips, hidden_in.shape, w_gate.shape, w_down.shape)
    t = sz.tokens
    gains = jnp.concatenate([norm_gain, ffn_gain, router_weight])[None]
    low, f32 = jnp.bfloat16, jnp.float32
    grid = sz.grid
    any_spec, vmem_spec = pl.BlockSpec(memory_space=pl.ANY), pl.BlockSpec(memory_space=pltpu.VMEM)
    shape = jax.ShapeDtypeStruct
    gate_shape = grid + (sz.rows_p, sz.ffn_half)
    out_shape = grid + (sz.rows_p, sz.full - sz.pack)
    edge_shape = grid + (sz.rows_p, sz.pack - sz.win)
    down_shape = grid + (sz.ffn_rows_p, sz.half)
    pack_shape = grid + (sz.rows_p, sz.full)
    kv_shape = grid + (t, sz.kv_wide)
    head_shape = (sz.steps, sz.step_rows, LANES)
    prob_shape = (sz.steps, sz.step_rows, sz.keys)
    copies_f = count_copies(sz, lambda *a: forward_flows(*a, None), 7)
    copies_b = count_copies(sz, lambda *a: backward_flows(*a, None, None, None), 4)
    first_scratch = [
        pltpu.VMEM((2,) + pack_shape, low),
        pltpu.VMEM((2,) + gate_shape, low),
        pltpu.VMEM((2,) + gate_shape, low),
        pltpu.VMEM((2,) + down_shape, low),
        pltpu.VMEM(kv_shape, low),
        pltpu.VMEM((t, sz.keys), sz.bias_type),
        pltpu.VMEM((sz.slots, sz.step_rows, sz.keys), low),
        pltpu.VMEM(head_shape, low),
        pltpu.VMEM((t, sz.wide), f32),
        pltpu.VMEM((2 * t, sz.wide), low),
        pltpu.VMEM((2, 2 * t, sz.ffn_half), low),
        pltpu.VMEM((2, t, sz.ffn_half), f32),
        pltpu.VMEM((2, t, sz.ffn_half), f32),
        pltpu.VMEM((2 * t, sz.wide), low),
        pltpu.VMEM((2 * t, sz.window), low),
        pltpu.VMEM((2 * t, sz.half), low),
        pltpu.VMEM((2 * t, sz.ffn_half), low),
        pltpu.VMEM((2 * t, sz.ffn_half), low),
        pltpu.VMEM((t, sz.half), low),
        pltpu.VMEM((t, sz.window), low),
        pltpu.VMEM((2, t, sz.ffn_half), low),
        pltpu.VMEM((t, 8), f32),
    ]
    lands = []
    for name, tensor, first, span in pack_flows(sz) + weight_flows(sz):
        rows = sz.ffn_rows_p if tensor == "d" else sz.rows_p
        lands += land_shapes(grid, ORDERS[name[1].upper()], rows, span)
    for name, r0, rn, first, span in kv_flows(sz):
        lands += land_shapes(grid, ORDERS[name[1].upper()], rn, span)
    second_scratch = [
        pltpu.VMEM(head_shape, f32),
        pltpu.VMEM((2 * t, sz.wide), low),
        pltpu.VMEM((2 * t, sz.pack), low),
        pltpu.VMEM((t, sz.pack), low),
    ]
    last_scratch = [pltpu.VMEM((4, 8, sz.wide), f32), pltpu.VMEM(grid + (8, LANES), f32), lands]
    results = [
        shape((sz.width, t), low),
        shape((sz.rows, sz.q_cols), f32),
        shape((sz.rows, sz.k_cols), f32),
        shape((sz.rows, sz.k_cols), f32),
        shape((sz.rows, sz.width // 2), f32),
        shape((sz.rows, sz.ffn_cols), f32),
        shape((sz.rows, sz.ffn_cols), f32),
        shape((sz.ffn_rows, sz.width // 2), f32),
        shape((1, sz.rows), f32),
        shape((1, sz.rows), f32),
        shape((1, sz.rows), f32),
        shape((8, LANES), f32),
    ]
    ins = (
        w_query, w_key, w_value, w_out, w_gate, w_up, w_down, gains,
        segment_ids, route_mask, valid_mask, hidden_in[0].T, teacher[0].T,
    )
    state_shape, dhid_shape = shape((sz.width, t), low), shape((t, sz.wide), f32)
    small_shape, table_shape = shape((8, sz.wide), f32), shape((t, LANES), f32)

    def sem_scratch(copies):
        return [pltpu.SemaphoreType.DMA((count,)) for count in (copies, copies, 16)]

    def params(number):
        return pltpu.CompilerParams(
            collective_id=number, has_side_effects=True, vmem_limit_bytes=VMEM_LIMIT
        )

    if sz.keys <= 4096:
        outs = pl.pallas_call(
            functools.partial(whole_kernel, sz),
            out_shape=[state_shape] + results + [shape(prob_shape, low)],
            in_specs=[vmem_spec] * FORWARD_INS,
            out_specs=[vmem_spec] * 13 + [any_spec],
            scratch_shapes=[
                pltpu.VMEM(dhid_shape.shape, f32),
                pltpu.VMEM(small_shape.shape, f32),
                pltpu.VMEM(head_shape, low),
                pltpu.VMEM(head_shape, low),
                pltpu.VMEM(table_shape.shape, f32),
                pltpu.VMEM(table_shape.shape, f32),
                pltpu.VMEM(edge_shape, low),
            ]
            + first_scratch
            + second_scratch
            + last_scratch
            + sem_scratch(copies_f + copies_b),
            compiler_params=params(0),
            name="whole",
        )(*ins)
        outs = outs[:-1]
    else:
        outs = pl.pallas_call(
            functools.partial(forward_kernel, sz),
            out_shape=[
                state_shape,
                dhid_shape,
                small_shape,
                shape((2,) + pack_shape, low),
                shape(kv_shape, low),
                shape(prob_shape, low),
                shape(head_shape, low),
                shape(head_shape, low),
                table_shape,
                table_shape,
                shape(edge_shape, low),
                shape(gate_shape, low),
                shape(gate_shape, low),
                shape(out_shape, low),
                shape(down_shape, low),
            ],
            in_specs=[vmem_spec] * FORWARD_INS,
            out_specs=[vmem_spec] * 3 + [any_spec] * 3 + [vmem_spec] * 5 + [any_spec] * 4,
            scratch_shapes=first_scratch + sem_scratch(copies_f),
            compiler_params=params(1),
            name="forward",
        )(*ins)
        state, dhid, small, wq_all, kv_all, prob, heads, dctx, cosine, sine, edge, pg, pu, po, pd = outs
        outs = pl.pallas_call(
            functools.partial(backward_kernel, sz),
            out_shape=results,
            in_specs=[any_spec] * 3 + [vmem_spec] * 2 + [any_spec] * 4 + [vmem_spec] * 6,
            out_specs=[vmem_spec] * 12,
            scratch_shapes=[
                pltpu.VMEM((2,) + pack_shape, low),
                pltpu.VMEM(kv_shape, low),
                pltpu.VMEM((2, sz.step_rows // sz.row_parts, sz.keys), low),
            ]
            + second_scratch
            + [
                pltpu.VMEM(gate_shape, low),
                pltpu.VMEM(gate_shape, low),
                pltpu.VMEM(down_shape, low),
            ]
            + last_scratch
            + sem_scratch(copies_b),
            compiler_params=params(2),
            name="backward",
        )(
            wq_all, kv_all, prob, heads, dctx, pg, pu, po, pd,
            ins[11], dhid, small, cosine, sine, edge,
        )
        outs = [state] + list(outs)
    last = len(outs) - 1
    state, ghid, gq, gk, gv, go, gg, gu, gd, gain1, gain2, router, loss = pl.pallas_call(
        deliver_kernel,
        out_shape=[shape(o.shape, o.dtype) for o in outs[:-1]] + [shape((1, 1), f32)],
        in_specs=[vmem_spec] * (last + 1),
        out_specs=[vmem_spec] * last + [pl.BlockSpec(memory_space=pltpu.SMEM)],
        name="deliver",
    )(*outs)
    return (
        state.T[None],
        loss.reshape(()),
        ghid.T[None],
        gain1.reshape(-1),
        gq,
        gk,
        gv,
        go,
        gain2.reshape(-1),
        gg,
        gu,
        gd,
        router.reshape(-1),
    )


def solution(mesh):
    tokens, rows, blocks = P("dp", "seq", None), P("dp", "seq"), P("seq", "dp")
    vector = P("seq")
    return jax.shard_map(
        functools.partial(body, mesh.shape["seq"]),
        mesh=mesh,
        in_specs=(
            tokens, rows, rows, rows, tokens, vector, blocks, blocks, blocks, blocks, vector,
            blocks, blocks, blocks, vector,
        ),
        out_specs=(
            tokens, P(), tokens, vector, blocks, blocks, blocks, blocks, vector, blocks, blocks,
            blocks, vector,
        ),
        check_vma=False,
    )
```

```python
import functools
import math

import jax
import jax.numpy as jnp
from jax import lax
from jax.experimental import pallas as pl
from jax.experimental.pallas import tpu as pltpu
from jax.sharding import PartitionSpec as P

HEADS = 15
KV_HEADS = 5
HEAD_DIM = 64
GROUPS = HEADS // KV_HEADS
LANES = 128

norm_eps = 1e-05
masked_score = -1e30

MESH = pl.DeviceIdType.MESH
VMEM_LIMIT = 62 * 2**20

ORDERS = {"C": (0, 2, 1), "D": (0, 1, 2), "E": (2, 1, 0), "F": (1, 2, 0)}


def round_up(value, unit):
    return (value + unit - 1) // unit * unit


class Sizes:
    def __init__(self, chips, hidden_block, gate_block, down_block):
        self.chips = chips
        _, self.tokens, self.width = hidden_block
        self.side = math.isqrt(chips // 4)
        self.grid = (4, self.side, self.side)
        self.keys = self.tokens * chips
        self.rows, _ = gate_block
        self.rows_p = round_up(self.rows, 16)
        self.wide = chips * self.rows_p
        self.half = self.wide // 2
        self.ffn_rows = down_block[0]
        self.ffn_rows_p = round_up(self.ffn_rows, 16)
        self.ffn_half = chips * self.ffn_rows_p // 2
        self.q_cols = HEADS * HEAD_DIM // 2
        self.k_cols = KV_HEADS * HEAD_DIM // 2
        self.cols = self.q_cols + 2 * self.k_cols
        self.pack = round_up(self.cols, LANES)
        self.out_cols = self.width // 2
        self.full = round_up(self.cols + self.out_cols, LANES)
        self.win = self.cols // LANES * LANES
        self.skip = self.cols - self.win
        self.window = self.full - self.win
        self.ffn_cols = gate_block[1]
        self.gain_lane = 3 * self.tokens
        assert self.rows < self.rows_p and self.gain_lane + 3 * self.rows <= self.win
        self.step_heads = GROUPS if self.keys <= 4096 else 1
        self.steps = HEADS // self.step_heads
        self.steps_per_kv = GROUPS // self.step_heads
        self.step_rows = self.step_heads * self.tokens
        self.kv_wide = KV_HEADS * LANES
        self.slots = 2 if self.keys <= 4096 else 1
        self.row_parts = 1 if self.keys <= 4096 else 4
        self.bias_type = jnp.float32 if self.keys <= 4096 else jnp.bfloat16


def hands_on(grid):
    return grid[1] == 2


class Place:
    def __init__(self, chips, count_only=False):
        side = math.isqrt(chips // 4)
        self.sizes = (4, side, side)
        self.strides = (side * side, side, 1)
        self.count_only, self.hands_on = count_only, hands_on(self.sizes)
        if count_only:
            self.core, self.chip, self.pos = 0, 0, (0, 0, 0)
            return
        self.core = lax.axis_index("dp")
        self.chip = lax.axis_index("seq")
        self.pos = (
            self.chip // (side * side),
            lax.rem(self.chip // side, side),
            lax.rem(self.chip, side),
        )

    def near(self, axis):
        p = self.pos[axis]
        return p + 1 - 2 * lax.rem(p, 2) if not self.count_only else 1

    def far(self, axis):
        p = self.pos[axis]
        return lax.rem(p + 2, 4) if not self.count_only else 2

    def middle(self, axis):
        p = self.pos[axis]
        return jnp.logical_or(p == 1, p == 2) if not self.count_only else False

    def outer(self, axis):
        p = self.pos[axis]
        return jnp.logical_or(p == 0, p == 3) if not self.count_only else True

    def others(self, axis):
        p = self.pos[axis]
        return [1 - p] if self.sizes[axis] == 2 else [self.near(axis), self.far(axis), 3 - p]

    def back_order(self, axis):
        return self.others(axis)[::-1] + [self.pos[axis]]

    def at(self, axis, other):
        return (self.core, self.chip + (other - self.pos[axis]) * self.strides[axis])

    def peer(self):
        return (1 - self.core, self.chip)

    def greet(self):
        barrier = pltpu.get_barrier_semaphore()
        devices = [self.peer()]
        for axis, size in enumerate(self.sizes):
            devices += [self.at(axis, other) for other in self.others(axis)]
        for dev in devices:
            pl.semaphore_signal(barrier, inc=1, device_id=dev, device_id_type=MESH)
        pl.semaphore_wait(barrier, len(devices))


class Sems:
    def __init__(self, send=None, recv=None):
        self.send, self.recv, self.used = send, recv, 0

    def take(self):
        self.used += 1
        return self.used - 1


def when(cond, body):
    if cond is None:
        body()
    else:
        pl.when(cond)(body)


class Copy:
    def __init__(self, sems, src, dst, dev, come, send_if=None, recv_if=None):
        self.i, self.sems = sems.take(), sems
        self.src, self.dst, self.dev, self.come = src, dst, dev, come
        self.send_if, self.recv_if = send_if, recv_if

    def _make(self, src, dst):
        return pltpu.make_async_remote_copy(
            src_ref=src(),
            dst_ref=dst(),
            send_sem=self.sems.send.at[self.i],
            recv_sem=self.sems.recv.at[self.i],
            device_id=self.dev,
            device_id_type=MESH,
        )

    def start(self):
        when(self.send_if, lambda: self._make(self.src, self.dst).start())

    def sent(self):
        when(self.send_if, lambda: self._make(self.src, self.dst).wait_send())

    def came(self):
        when(self.recv_if, lambda: self._make(self.come, self.come).wait_recv())


class Line:
    def __init__(self, place, sems, axis, unit):
        self.size, p = place.sizes[axis], place.pos[axis]
        self.hands_on, self.slow = place.hands_on and axis == 0, axis == 0
        at = functools.partial(place.at, axis)

        def copy(block, to, come, send_if=None, recv_if=None):
            src = lambda: unit(block)
            return Copy(sems, src, src, at(to), lambda: unit(come), send_if, recv_if)

        if self.size == 2:
            self.near = copy(p, 1 - p, 1 - p)
            self.all = [self.near]
            self.others = [1 - p]
            return
        near, far, last = place.near(axis), place.far(axis), self.size - 1 - p
        self.near = copy(p, near, near)
        self.far = copy(p, far, far)
        self.others = [near, far, last]
        if self.hands_on:
            mid = place.middle(axis)
            self.across = copy(p, last, last, mid, mid)
            self.relayed = copy(far, near, last, mid, place.outer(axis))
            self.all = [self.near, self.far, self.across, self.relayed]
        else:
            self.across = copy(p, last, last)
            self.all = [self.near, self.far, self.across]

    def start(self):
        self.near.start()
        if self.size > 2:
            self.far.start()
            self.across.start()

    def relay(self):
        if not self.hands_on:
            return
        self.far.came()
        self.relayed.start()

    def arrivals(self, then):
        self.near.came()
        then(0)
        if self.size > 2:
            if not self.hands_on:
                self.far.came()
            then(1)
            self.across.came()
            if self.hands_on:
                self.relayed.came()
            then(2)


class Gather:
    def __init__(self, place, sems, view, order, twin=None):
        self.view, self.twin, self.order = view, twin, order
        a, b, c = order
        pos = place.pos
        first = Line(place, sems, a, lambda j: self._ref(j, pos[b], pos[c]))
        second = Line(place, sems, b, lambda j: self._ref(None, j, pos[c]))
        third, cross = [], []
        for jb in [pos[b]] + second.others:
            line = Line(place, sems, c, lambda j, jb=jb: self._ref(None, jb, j))
            third.append(line)
            if twin is not None:
                cross.append([self._cross(place, sems, jb, jc) for jc in [pos[c]] + line.others])
        self.all = first.all + second.all + sum((line.all for line in third), []) + sum(cross, [])

        def spread(m):
            third[m].start()
            if cross:
                cross[m][0].start()

        def finish_first():
            first.arrivals(lambda k: None)
            second.start()
            spread(0)

        def finish_third():
            for m, line in enumerate(third):
                line.arrivals(lambda k, m=m: cross[m][k + 1].start() if cross else None)

        self.rounds = [first.start]
        if first.slow:
            self.rounds.append(first.relay)
        self.rounds.append(finish_first)
        if second.slow:
            self.rounds.append(second.relay)
        self.rounds.append(lambda: second.arrivals(lambda k: spread(k + 1)))
        if third[0].slow:
            self.rounds.append(lambda: [line.relay() for line in third])
        self.rounds.append(finish_third)
        if cross:
            self.rounds.append(lambda: [c.came() for some in cross for c in some])

    def _ref(self, ia, ib, ic, twin=False):
        idx = [None] * 3
        for axis, i in zip(self.order, (ia, ib, ic)):
            idx[axis] = slice(None) if i is None else i
        return (self.twin if twin else self.view)(*idx)

    def _cross(self, place, sems, jb, jc):
        here = lambda: self._ref(None, jb, jc)
        return Copy(sems, here, here, place.peer(), lambda: self._ref(None, jb, jc, True))

    def sent(self):
        for c in self.all:
            c.sent()


class BackLine:
    def __init__(self, place, sems, axis, unit, land):
        self.size, p = place.sizes[axis], place.pos[axis]
        self.hands_on, self.slow = place.hands_on and axis == 0, axis == 0
        self.unit, self.land, self.p = unit, land, p
        at = functools.partial(place.at, axis)

        def copy(block, to, slot, send_if=None, recv_if=None):
            spot = lambda: land(slot)
            return Copy(sems, lambda: unit(block), spot, at(to), spot, send_if, recv_if)

        if self.size == 2:
            self.near = copy(1 - p, 1 - p, 0)
            self.all = [self.near]
            return
        near, far, last = place.near(axis), place.far(axis), self.size - 1 - p
        mid, outer = place.middle(axis), place.outer(axis)
        self.where_far, self.mid = far, mid
        self.near = copy(near, near, 0)
        self.far = copy(far, far, 1)
        if not self.hands_on:
            self.across = copy(last, last, 2)
            self.all = [self.near, self.far, self.across]
            return
        self.across = copy(last, last, 2, mid, mid)
        self.relayed = copy(last, near, 3, outer, mid)
        self.all = [self.near, self.far, self.across, self.relayed]

    def _add(self, block, slots):
        ref = self.unit(block)
        total = ref[...].astype(jnp.float32)
        for slot in slots:
            total = total + self.land(slot)[...].astype(jnp.float32)
        return total

    def start(self):
        if self.hands_on:
            self.relayed.start()
            self.near.start()
        else:
            for cp in self.all:
                cp.start()

    def relay(self):
        if not self.hands_on:
            return
        self.across.start()
        self.relayed.came()

        def body():
            ref = self.unit(self.where_far)
            ref[...] = self._add(self.where_far, (3,)).astype(ref.dtype)

        pl.when(self.mid)(body)
        self.far.start()

    def came(self):
        self.near.came()
        if self.size > 2:
            self.far.came()
            self.across.came()
        if self.hands_on:

            def body():
                ref = self.unit(self.p)
                ref[...] = self._add(self.p, (2,)).astype(ref.dtype)

            pl.when(self.mid)(body)

    def total(self):
        return self._add(self.p, range(2 if self.hands_on else self.size - 1))

    def collect(self):
        self.came()
        ref = self.unit(self.p)
        ref[...] = self.total().astype(ref.dtype)


class Scatter:
    def __init__(self, place, sems, view, order, lands):
        self.view, self.order = view, order
        a, b, c = order
        pos = place.pos
        land_c, land_b, land_a = lands if lands is not None else (None,) * 3
        spots = place.back_order(b)
        first = [
            BackLine(
                place, sems, c,
                lambda j, jb=jb: self._ref(None, jb, j),
                lambda slot, m=m: land_c.at[m, slot],
            )
            for m, jb in enumerate(spots)
        ]
        second = BackLine(
            place, sems, b, lambda j: self._ref(None, j, pos[c]), lambda slot: land_b.at[slot]
        )
        third = BackLine(
            place, sems, a, lambda j: self._ref(j, pos[b], pos[c]), lambda slot: land_a.at[slot]
        )
        self.third = third
        self.all = sum((line.all for line in first), []) + second.all + third.all

        def finish_first():
            for line in first:
                line.collect()
            second.start()

        def finish_second():
            second.collect()
            third.start()

        self.rounds = [lambda: [line.start() for line in first]]
        if first[0].slow:
            self.rounds.append(lambda: [line.relay() for line in first])
        self.rounds.append(finish_first)
        if second.slow:
            self.rounds.append(second.relay)
        self.rounds.append(finish_second)
        if third.slow:
            self.rounds.append(third.relay)
        self.rounds.append(third.came)

    def _ref(self, ia, ib, ic):
        idx = [None] * 3
        for axis, i in zip(self.order, (ia, ib, ic)):
            idx[axis] = slice(None) if i is None else i
        return self.view(*idx)

    def sent(self):
        for cp in self.all:
            cp.sent()

    def total(self):
        return self.third.total()


def land_shapes(grid, order, rows, cols):
    a, b, c = (grid[axis] for axis in order)
    slots_a, slots_b, slots_c = (
        4 if axis == 0 and hands_on(grid) else grid[axis] - 1 for axis in order
    )
    return [
        pltpu.VMEM((b, slots_c, a, rows, cols), jnp.bfloat16),
        pltpu.VMEM((slots_b, a, rows, cols), jnp.bfloat16),
        pltpu.VMEM((slots_a, rows, cols), jnp.bfloat16),
    ]


def tiles(total, **shares):
    out, at = [], 0
    names = list(shares)
    for name in names:
        span = shares[name] if name != names[-1] else total // LANES - at
        out.append((name, at * LANES, span * LANES))
        at += span
    return out


def weight_flows(sz):
    out = []
    for tensor, total, shares in (
        ("g", sz.ffn_half, dict(E=5, D=5)),
        ("u", sz.ffn_half, dict(F=5, C=5)),
        ("o", sz.full - sz.pack, dict(D=3)),
        ("d", sz.half, dict(C=2, D=2)),
    ):
        at = sz.pack if tensor == "o" else 0
        out += [(tensor + x, tensor, at + first, span) for x, first, span in tiles(total, **shares)]
    return out


def pack_flows(sz):
    return [("q" + n, "q", f, s) for n, f, s in tiles(sz.pack, C=4, D=3)]


def kv_flows(sz):
    half = sz.tokens // 2
    return [("kC", 0, half, 0, sz.kv_wide), ("kD", half, half, 0, sz.kv_wide)]


ORDER = (
    "qD0", "others", "gE0", "qC0", "qD1", "oD0", "qD2", "qC1", "gD0", "qC2", "uC0", "oD1", "uF0",
    "qD3", "qC3", "oD2", "dD0", "uF1", "qD4", "qD5", "qC4", "gD1", "prep", "gD2", "qC5", "dD1",
    "qkv", "uC1", "kD0", "dD2", "kC0", "uF2", "gD3", "uC2", "dC0", "kC1", "heads", "gE1", "kC2",
    "mask", "kD1", "kD2", "gD4", "uF3", "kC3", "dC1", "kD3", "gD5", "gE2", "uF4", "dC2", "kC4",
    "oD3", "uC3", "dD3", "kD4", "atta", "attb", "attc", "gE3", "dC3", "attd", "oD4", "uC4",
    "atte", "oD5", "gE4", "out", "dD4", "uF5", "dC4", "gE5", "uC5", "gu", "dD5", "dC5", "down",
    "bwd", "pd", "DC0", "DD0", "bwdb", "pg", "pu", "UF0", "UC0", "bwdc", "po", "UF1", "GD0",
    "batta", "battb", "battc", "battd", "GE0", "batte", "KD0", "KC0", "qs", "EC0", "GE1", "GD1",
    "KC1", "KD1", "GE2", "DC1", "DD1", "GD2", "OD0", "KC2", "KD2", "KC3", "KD3", "UC1", "DC2",
    "DD2", "GD3", "KD4", "OD1", "KC4", "DC3", "kq", "EC1", "EC2", "QD0", "QC0", "DC4", "DD3",
    "OD2", "OD3", "UF2", "GE3", "gi", "EC3", "UC2", "QD1", "QC1", "UC3", "QD2", "QD3", "DD4",
    "GE4", "QC2", "QC3", "UF3", "QD4", "UF4", "UC4", "OD4", "GD4", "QC4", "EC4", "fin",
)


class Order:
    def __init__(self, flows, words):
        self.flows, self.words, self.at = flows, words, 0

    def until(self, mark):
        while self.words[self.at] != mark:
            word = self.words[self.at]
            if word[-1] in "0123456":
                self.flows[word[:-1]].rounds[int(word[-1])]()
            self.at += 1
        self.at += 1


class Link:
    def __init__(self, sz, words, send, recv, local):
        self.place, self.sems, self.local = Place(sz.chips), Sems(send, recv), local
        self.flows, self.used = {}, 0
        self.order = Order(self.flows, words)

    def slot(self, count=1):
        self.used += count
        return self.used - count

    def bring(self, src, dst):
        return pltpu.make_async_copy(src, dst, self.local.at[self.slot()])

    def to_peer(self, src, dst):
        return Copy(self.sems, lambda: src, lambda: dst, self.place.peer(), lambda: dst)


def dot(left, right):
    return jnp.dot(left, right, preferred_element_type=jnp.float32)


def dot_nt(left, right):
    return lax.dot_general(
        left, right, (((1,), (1,)), ((), ())), preferred_element_type=jnp.float32
    )


def dot_tn(left, right):
    return lax.dot_general(
        left, right, (((0,), (0,)), ((), ())), preferred_element_type=jnp.float32
    )


def blocks_padded(value, block, block_p):
    if block == block_p:
        return value
    zero = jnp.zeros((value.shape[0], block_p - block), value.dtype)
    pieces = []
    for j in range(value.shape[1] // block):
        pieces += [value[:, j * block : (j + 1) * block], zero]
    return jnp.concatenate(pieces, axis=1)


def blocks_cut(value, block, block_p):
    if block == block_p:
        return value
    return jnp.concatenate(
        [value[:, j * block_p : j * block_p + block] for j in range(value.shape[1] // block_p)],
        axis=1,
    )


def lanes_of(ref, which, first, span):
    value = ref[which, :, :, :, :, pl.ds(first, span)]
    return value.reshape(-1, span)


def beside(*pieces):
    return jnp.concatenate([p for p in pieces if p.shape[1] > 0], axis=1)


def spread(sz, value):
    return blocks_padded(value, sz.rows, sz.rows_p)


def narrow(sz, value):
    return blocks_cut(value, sz.rows, sz.rows_p)


def tokens_in(sz, ref):
    value = ref[...].astype(jnp.float32)
    zero = jnp.zeros((sz.rows_p - sz.rows, sz.tokens), jnp.float32)
    pieces = []
    for j in range(sz.chips):
        pieces += [value[j * sz.rows : (j + 1) * sz.rows], zero]
    return jnp.concatenate(pieces, axis=0).T


def tokens_out(sz, value):
    value = value.T
    pieces = [value[j * sz.rows_p : j * sz.rows_p + sz.rows] for j in range(sz.chips)]
    return jnp.concatenate(pieces, axis=0).astype(jnp.bfloat16)


def rows_padded(value, rows):
    if value.shape[0] < rows:
        zero = jnp.zeros((rows - value.shape[0], value.shape[1]), value.dtype)
        value = jnp.concatenate([value, zero], axis=0)
    return value.astype(jnp.bfloat16)


def lane_index(shape):
    return lax.broadcasted_iota(jnp.int32, shape, len(shape) - 1)


def swap_halves(value):
    span = value.shape[1]
    first = lax.rem(lane_index(value.shape), HEAD_DIM) < HEAD_DIM // 2
    return jnp.where(
        first,
        pltpu.roll(value, span - HEAD_DIM // 2, 1),
        pltpu.roll(value, HEAD_DIM // 2, 1),
    )


def repeat_lanes(table, span):
    return jnp.concatenate([table] * (span // LANES), axis=1)


def chips_of(sz):
    return [(i, j, k) for i in range(sz.grid[0]) for j in range(sz.side) for k in range(sz.side)]


def gain_row(sz, wq, which):
    first = sz.gain_lane + which * sz.rows
    zero = jnp.zeros((1, sz.rows_p - sz.rows), jnp.float32)
    pieces = []
    for i, j, k in chips_of(sz):
        line = wq[0, i, j, k, sz.rows : sz.rows + 1, : sz.win].astype(jnp.float32)
        pieces += [line[:, first : first + sz.rows], zero]
    return jnp.concatenate(pieces, axis=1)


def rotary_tables(sz, place):
    lane = lane_index((sz.tokens, LANES))
    row = lax.broadcasted_iota(jnp.int32, (sz.tokens, LANES), 0)
    half = HEAD_DIM // 2
    place_of = (place.chip * sz.tokens + row).astype(jnp.float32)
    inv_freq = jnp.exp(lax.rem(lane, half).astype(jnp.float32) * (-math.log(10000.0) / half))
    angles = place_of * inv_freq
    sine = jnp.sin(angles)
    return jnp.cos(angles), jnp.where(lax.rem(lane, HEAD_DIM) < half, -sine, sine)


def forward_flows(sz, place, sems, full, kv):
    flows = {}
    for name, tensor, first, span in pack_flows(sz) + weight_flows(sz):

        def view(half, ref=full[tensor], first=first, span=span):
            return lambda i, j, k: ref.at[half, i, j, k, :, pl.ds(first, span)]

        core = place.core
        flows[name] = Gather(place, sems, view(core), ORDERS[name[1].upper()], view(1 - core))
    for name, r0, rn, first, span in kv_flows(sz):

        def view(i, j, k, r0=r0, rn=rn, first=first, span=span):
            return kv.at[i, j, k, pl.ds(r0, rn), pl.ds(first, span)]

        flows[name] = Gather(place, sems, view, ORDERS[name[1].upper()])
    return flows


def backward_flows(sz, place, sems, partial, kv, err, lands):
    flows, at = {}, 0
    for name, tensor, first, span in pack_flows(sz) + weight_flows(sz):

        def view(i, j, k, ref=partial[tensor], first=first, span=span):
            return ref.at[i, j, k, :, pl.ds(first, span)]

        land = None if lands is None else lands[at : at + 3]
        flows[name[0].upper() + name[1:]] = Scatter(place, sems, view, ORDERS[name[1].upper()], land)
        at += 3
    for name, r0, rn, first, span in kv_flows(sz):

        def view(i, j, k, r0=r0, rn=rn, first=first, span=span):
            return kv.at[i, j, k, pl.ds(r0, rn), pl.ds(first, span)]

        land = None if lands is None else lands[at : at + 3]
        flows[name[0].upper() + name[1:]] = Scatter(place, sems, view, ORDERS[name[1].upper()], land)
        at += 3
    flows["EC"] = Gather(place, sems, lambda i, j, k: err.at[i, j, k], ORDERS["C"])
    return flows


def forward_part(
    sz, link,
    q_in, k_in, v_in, out_in, gate_in, up_in, down_in, gains_in, seg_in, route_in, valid_in,
    hid_in, teach_in,
    state_out, dhid_out, small_out, prob_out, heads_out, dctx_out, cos_out, sin_out,
    po6,
    wq, wg, wu, wd, kv, bias, prob, hid, normed2, act, gate_s, up_s, ctx2, datt2, dffn2,
    dgate2, dup2, stage_d, stage_o, stage_h, col_in, keep, fused,
):
    place, sems, order, local = link.place, link.sems, link.order, link.local
    core = place.core
    t, n, wide = sz.tokens, sz.chips, sz.wide
    ctx_h = dctx_out
    full = {"q": wq, "o": wq, "g": wg, "u": wu, "d": wd}
    flows = forward_flows(sz, place, sems, full, kv)
    link.flows.update(flows)
    own, other = pl.ds(0, t), pl.ds(t, t)
    x_n2 = link.to_peer(normed2.at[own], normed2.at[other])
    x_act = link.to_peer(act.at[:, own], act.at[:, other])
    x_ctx = link.to_peer(ctx2.at[own], ctx2.at[other])
    x_dffn = link.to_peer(stage_d, dffn2.at[other])
    x_datt = link.to_peer(stage_o, datt2.at[other])
    x_dgate = link.to_peer(stage_h.at[0], dgate2.at[other])
    x_dup = link.to_peer(stage_h.at[1], dup2.at[other])

    f32 = jnp.float32
    spot = (core,) + place.pos
    marks = [ref[...].astype(f32) for ref in (seg_in, route_in, valid_in)]
    rest = sz.full - sz.gain_lane - 3 * sz.rows
    line = jnp.concatenate(marks + [gains_in[...].astype(f32), jnp.zeros((1, rest), f32)], axis=1)
    block = beside(
        *(ref[...].astype(f32) for ref in (q_in, k_in, v_in, out_in)),
        jnp.zeros((sz.rows, sz.full - sz.cols - sz.out_cols), f32),
    )
    wq[spot] = rows_padded(jnp.concatenate([block, line], axis=0), sz.rows_p)
    place.greet()
    order.until("others")
    for ref, own_in in ((wg, gate_in), (wu, up_in)):
        block = blocks_padded(own_in[...].astype(f32), sz.ffn_rows, sz.ffn_rows_p)
        ref[spot] = rows_padded(block, sz.rows_p)
    wd[spot] = rows_padded(spread(sz, down_in[...].astype(f32)), sz.ffn_rows_p)

    order.until("prep")
    hid[...] = tokens_in(sz, hid_in)
    hidden = hid[...]
    inv_first = lax.rsqrt(jnp.sum(hidden * hidden, axis=-1, keepdims=True) / sz.width + norm_eps)
    cos_out[...], sin_out[...] = rotary_tables(sz, place)
    col_in[...] = jnp.concatenate(marks + [jnp.zeros((5, t), f32)], axis=0).T
    cosine, sine = repeat_lanes(cos_out[...], 8 * LANES), repeat_lanes(sin_out[...], 8 * LANES)

    order.until("qkv")
    wq_full = [lanes_of(wq, h, 0, sz.pack) for h in (0, 1)]
    gain_one = gain_row(sz, wq, 0)
    normed = (hidden * inv_first * gain_one).astype(jnp.bfloat16)
    halves = [dot(normed, w) for w in wq_full]
    qc, kc = sz.q_cols, sz.k_cols
    q_pre = jnp.concatenate(
        [halves[0][:, :qc], halves[1][:, :qc], jnp.zeros((t, 8 * LANES - 2 * qc), jnp.float32)],
        axis=1,
    )
    pad_k = jnp.zeros((t, 3 * LANES - 2 * kc), jnp.float32)
    k_pre = jnp.concatenate(
        [halves[0][:, qc : qc + kc], halves[1][:, qc : qc + kc], pad_k], axis=1
    )
    v_pre = jnp.concatenate(
        [halves[0][:, qc + kc : qc + 2 * kc], halves[1][:, qc + kc : qc + 2 * kc]], axis=1
    )
    k_rot = k_pre * cosine[:, : 3 * LANES] + swap_halves(k_pre) * sine[:, : 3 * LANES]
    kv_own = jnp.concatenate(
        [
            piece[:, g * HEAD_DIM : (g + 1) * HEAD_DIM]
            for g in range(KV_HEADS)
            for piece in (k_rot, v_pre)
        ],
        axis=1,
    )
    kv[place.pos[0], place.pos[1], place.pos[2]] = kv_own.astype(jnp.bfloat16)
    order.until("heads")
    q_rot = q_pre * cosine + swap_halves(q_pre) * sine
    q_low = q_rot.astype(jnp.bfloat16).astype(jnp.float32) * HEAD_DIM ** (-0.5)
    blank = jnp.zeros((t, HEAD_DIM), jnp.float32)
    for h in range(HEADS):
        st, sub = h // sz.step_heads, h % sz.step_heads
        heads_out[st, pl.ds(sub * t, t)] = jnp.concatenate(
            [q_low[:, h * HEAD_DIM : (h + 1) * HEAD_DIM], blank], axis=1
        ).astype(jnp.bfloat16)
    order.until("mask")

    row_at = sz.rows
    seg_col, route_col, valid_col = col_in[:, 0:1], col_in[:, 1:2], col_in[:, 2:3]
    q_pos = place.chip * t + lax.broadcasted_iota(jnp.int32, (t, LANES), 0)
    count = jnp.zeros((1, LANES), jnp.float32)
    for m, (i, j, k) in enumerate(chips_of(sz)):
        line = wq[core, i, j, k, row_at : row_at + 1, : 2 * LANES].astype(jnp.float32)
        seg_row, route_row = line[:, :LANES], line[:, LANES:]
        k_pos = m * t + lane_index((t, LANES))
        allowed = (
            (seg_col == seg_row)
            & (k_pos <= q_pos)
            & ((route_row > 0.5) | (k_pos == q_pos))
        )
        bias[:, m * t : (m + 1) * t] = jnp.where(allowed, 0.0, masked_score).astype(bias.dtype)
        for h in (0, 1):
            count = count + wq[
                h, i, j, k, row_at : row_at + 1, 2 * LANES : 3 * LANES
            ].astype(jnp.float32)
    tok_count = jnp.sum(count, axis=-1, keepdims=True)
    small_out[...] = jnp.zeros(small_out.shape, f32)
    small_out[3:4] = jnp.broadcast_to(tok_count, (1, wide))
    small_out[4:5] = gain_one
    kept = []
    prob_sem = link.slot(sz.slots)

    def attend(st):
        g = st // sz.steps_per_kv
        slot = lax.rem(st, sz.slots)
        lanes = pl.ds(pl.multiple_of(g * LANES, LANES), LANES)
        tile = kv[:, :, :, :, lanes].reshape(sz.keys, LANES)
        s = dot_nt(heads_out[st], tile).reshape(sz.step_heads, t, sz.keys) + bias[...].astype(jnp.float32)[None]
        s = s.reshape(sz.step_rows, sz.keys)
        e = jnp.exp(s - jnp.max(s, axis=-1, keepdims=True))
        p = (e * (1.0 / jnp.sum(e, axis=-1, keepdims=True))).astype(jnp.bfloat16)
        save = pltpu.make_async_copy(prob.at[slot], prob_out.at[st], local.at[prob_sem + slot])

        @pl.when(st >= sz.slots)
        def _():
            save.wait()

        prob[slot] = p
        save.start()
        ctx_h[st] = dot(p, tile).astype(jnp.bfloat16)

    for g in range(KV_HEADS):
        order.until("att%s" % "abcde"[g])
        if g == 0:
            kept += [link.bring(ref, keep[x]) for x, ref in (("q", wq), ("k", kv)) if x in keep]
            for cp in kept:
                cp.start()
        pl.loop(g * sz.steps // KV_HEADS, (g + 1) * sz.steps // KV_HEADS)(attend)
    for slot in range(sz.slots):
        pltpu.make_async_copy(prob.at[slot], prob_out.at[slot], local.at[prob_sem + slot]).wait()

    ctx = jnp.concatenate(
        [
            ctx_h[h // sz.step_heads, pl.ds(h % sz.step_heads * t, t), HEAD_DIM:].astype(jnp.float32)
            for h in range(HEADS)
        ],
        axis=1,
    )
    ctx2[own] = spread(sz, ctx).astype(jnp.bfloat16)
    x_ctx.start()
    order.until("out")
    attn = [dot(ctx2[own], lanes_of(wq, q, sz.win, sz.window)) for q in (0, 1)]
    attn = [value[:, sz.skip : sz.skip + sz.out_cols] for value in attn]
    attn = spread(sz, jnp.concatenate(attn, axis=1))
    hidden = hid[...]
    gain_two, router = gain_row(sz, wq, 1), gain_row(sz, wq, 2)
    residual = hidden + attn
    inv_second = lax.rsqrt(
        jnp.sum(residual * residual, axis=-1, keepdims=True) / sz.width + norm_eps
    )
    normed2[own] = (residual * inv_second * gain_two).astype(jnp.bfloat16)
    x_n2.start()
    order.until("gu")
    for h in (0, 1):
        gate_pre = dot(normed2[own], wg[h].reshape(wide, sz.ffn_half))
        up_pre = dot(normed2[own], wu[h].reshape(wide, sz.ffn_half))
        gate_s[h], up_s[h] = gate_pre, up_pre
        act[h, own] = (gate_pre * jax.nn.sigmoid(gate_pre) * up_pre).astype(jnp.bfloat16)
    x_act.start()
    order.until("down")
    two = sz.grid[0] // 2

    def down(q, h):
        return wd[q, pl.ds(h * two, two)].reshape(sz.ffn_half, sz.half)

    ffn = jnp.concatenate(
        [dot(act[0, own], down(q, 0)) + dot(act[1, own], down(q, 1)) for q in (0, 1)], axis=1
    )

    router_sig = jax.nn.sigmoid(jnp.sum(hidden * router, axis=-1, keepdims=True))
    mix = route_col * router_sig
    branch = attn + ffn
    state = hidden + mix * branch
    state_out[...] = tokens_out(sz, state)
    misfit = state - tokens_in(sz, teach_in)
    small_out[2:3] = jnp.sum(valid_col * misfit * misfit, axis=0, keepdims=True)
    d_state = 2.0 / (sz.width * tok_count) * valid_col * misfit
    d_branch = mix * d_state
    d_logit = (
        route_col
        * jnp.sum(d_state * branch, axis=-1, keepdims=True)
        * router_sig
        * (1.0 - router_sig)
    )
    small_out[1:2] = jnp.sum(d_logit * hidden, axis=0, keepdims=True)
    d_ffn = d_branch.astype(jnp.bfloat16)
    low, high = d_ffn[:, : sz.half], d_ffn[:, sz.half :]
    stage_d[...] = jnp.where(core == 0, high, low)
    x_dffn.start()
    dffn2[own] = jnp.where(core == 0, low, high)
    order.until("bwd")
    for turn in (1, 0):
        h = core if turn == 0 else 1 - core
        d_act = dot_nt(low, down(0, h)) + dot_nt(high, down(1, h))
        gate_pre, up_pre = gate_s[h], up_s[h]
        sig = jax.nn.sigmoid(gate_pre)
        d_gate = (d_act * up_pre * sig * (1.0 + gate_pre * (1.0 - sig))).astype(jnp.bfloat16)
        d_up = (d_act * (gate_pre * sig)).astype(jnp.bfloat16)
        if turn == 1:
            stage_h[0], stage_h[1] = d_gate, d_up
            x_dgate.start()
            x_dup.start()
        else:
            dgate2[own], dup2[own] = d_gate, d_up

    def until(mark):
        if fused:
            order.until(mark)

    def copied(tensor):
        for name in flows:
            if name[0] == tensor:
                flows[name].sent()

    shape, pd = (sz.side, sz.side), wd.at[0]
    until("pd")
    x_act.came()
    x_dffn.came()
    copied("d")
    for h in (0, 1):
        for i in range(two):
            part = sz.ffn_half // two
            pd[h * two + i] = (
                dot_tn(act[h, :, pl.ds(i * part, part)], dffn2[...])
                .astype(jnp.bfloat16)
                .reshape(shape + (sz.ffn_rows_p, sz.half))
            )
    until("bwdb")
    d_normed2 = jnp.zeros((t, wide), jnp.float32)
    for h, d_gate, d_up in (
        (1 - core, stage_h[0], stage_h[1]),
        (core, dgate2[own], dup2[own]),
    ):
        d_normed2 = (
            d_normed2
            + dot_nt(d_gate, wg[h].reshape(wide, sz.ffn_half))
            + dot_nt(d_up, wu[h].reshape(wide, sz.ffn_half))
        )
    x_n2.came()
    part = wide // sz.grid[0]
    for name, came, right, ref in (
        ("g", x_dgate, dgate2, wg.at[0]),
        ("u", x_dup, dup2, wu.at[0]),
    ):
        until("p" + name)
        came.came()
        copied(name)
        for i in range(sz.grid[0]):
            ref[i] = (
                dot_tn(normed2[:, pl.ds(i * part, part)], right[...])
                .astype(jnp.bfloat16)
                .reshape(shape + (sz.rows_p, sz.ffn_half))
            )
    until("bwdc")
    small_out[0:1] = jnp.sum(d_normed2 * residual * inv_second, axis=0, keepdims=True)
    scaled = gain_two * d_normed2
    d_mid = inv_second * scaled - residual * (
        inv_second**3 * (jnp.sum(scaled * residual, axis=-1, keepdims=True) / sz.width)
    )
    dhid_out[...] = d_state + d_logit * router + d_mid
    d_attn = narrow(sz, d_branch + d_mid)
    left = jnp.zeros((t, sz.skip), f32)
    right = jnp.zeros((t, sz.window - sz.skip - sz.out_cols), f32)
    low, high = (
        beside(left, value, right).astype(jnp.bfloat16)
        for value in (d_attn[:, : sz.out_cols], d_attn[:, sz.out_cols :])
    )
    stage_o[...] = jnp.where(core == 0, high, low)
    x_datt.start()
    datt2[own] = jnp.where(core == 0, low, high)
    d_ctx = dot_nt(low, lanes_of(wq, 0, sz.win, sz.window))
    d_ctx = narrow(sz, d_ctx + dot_nt(high, lanes_of(wq, 1, sz.win, sz.window)))
    for h in range(HEADS):
        st, sub = h // sz.step_heads, h % sz.step_heads
        dctx_out[st, pl.ds(sub * t, t)] = jnp.concatenate(
            [blank, d_ctx[:, h * HEAD_DIM : (h + 1) * HEAD_DIM]], axis=1
        ).astype(jnp.bfloat16)
    until("po")
    x_ctx.came()
    x_datt.came()
    for tensor in "oqk":
        copied(tensor)
    for cp in kept:
        cp.wait()
    kept = []
    out_lanes = pl.ds(sz.pack, sz.full - sz.pack)
    edge = sz.pack - sz.win
    for i in range(sz.grid[0]):
        grad = dot_tn(ctx2[:, pl.ds(i * part, part)], datt2[...]).astype(jnp.bfloat16)
        po6[i] = grad[:, :edge].reshape(shape + (sz.rows_p, edge))
        wq[0, i, :, :, :, out_lanes] = grad[:, edge:].reshape(
            shape + (sz.rows_p, sz.full - sz.pack)
        )
    for name, ref in (
        ("d", wd.at[0]),
        ("g", wg.at[0]),
        ("u", wu.at[0]),
        ("o", wq.at[0, :, :, :, :, out_lanes]),
    ):
        if name in keep:
            kept.append(link.bring(ref, keep[name]))
            kept[-1].start()
    for cp in kept:
        cp.wait()
    for cp in (x_n2, x_act, x_ctx, x_dffn, x_datt, x_dgate, x_dup):
        cp.sent()


def backward_part(
    sz, link,
    prob_in, heads, dctx, hid_in, dhid, small_in, cos_in, sin_in,
    po6,
    ghid_out, gq_out, gk_out, gv_out, go_out, gg_out, gu_out, gd_out, gain1_out, gain2_out,
    router_out, loss_out,
    wq, kv, prob, dq_h, normed2, dpack2, stage, small2, fused,
):
    place, order, local = link.place, link.order, link.local
    core = place.core
    t, wide = sz.tokens, sz.wide
    flows = link.back_flows
    own, other = pl.ds(0, t), pl.ds(t, t)
    x_n = link.to_peer(normed2.at[own], normed2.at[other])
    x_pack = link.to_peer(stage, dpack2.at[other])
    x_small = link.to_peer(small2.at[0], small2.at[1])
    x_err = link.to_peer(small2.at[2], small2.at[3])
    prob_sem = link.slot(2)
    part_rows = sz.step_rows // sz.row_parts

    def fetch(st, slot):
        rows = pl.ds(st % sz.row_parts * part_rows, part_rows)
        return pltpu.make_async_copy(
            prob_in.at[st // sz.row_parts, rows], prob.at[slot], local.at[prob_sem + slot]
        )

    fetch(0, 0).start()
    small2[2] = small_in[...]
    if not fused:
        place.greet()
    x_err.start()
    if not fused:
        for name in "dgu":
            order.until("p" + name)
            link.gets[name].wait()
        link.gets["k"].wait()
        link.gets["q"].wait()
        order.until("po")
        link.gets["o"].start()
        link.gets["o"].wait()

    def attend(i, total):
        st = i // sz.row_parts
        slot = i % 2
        fetch(i, slot).wait()

        if isinstance(i, int):
            if i + 1 < sz.steps:
                fetch(i + 1, 1 - slot).start()
        else:

            @pl.when(i + 1 < sz.steps * sz.row_parts)
            def _():
                fetch(i + 1, 1 - slot).start()

        first, row = st // sz.steps_per_kv * LANES, i % sz.row_parts * part_rows
        if not isinstance(i, int):
            first, row = pl.multiple_of(first, LANES), pl.multiple_of(row, part_rows)
        tile = kv[:, :, :, :, pl.ds(first, LANES)].reshape(sz.keys, LANES)
        rows = pl.ds(row, part_rows)
        p_low = prob[slot]
        p = p_low.astype(jnp.float32)
        d_w = dot_nt(dctx[st, rows], tile)
        terms = p * d_w
        delta = jnp.sum(terms, axis=-1, keepdims=True)
        d_s = (terms - p * delta).astype(jnp.bfloat16)
        dq_h[0](st, rows, dot(d_s, tile))
        more = dot_tn(heads[st, rows], d_s) + dot_tn(dctx[st, rows], p_low)
        return more if total is None else total + more

    for g in range(KV_HEADS):
        order.until("batt%s" % "abcde"[g])
        each = sz.steps_per_kv * sz.row_parts
        if each == 1:
            total = attend(g, None)
        else:
            total = jnp.zeros((LANES, sz.keys), jnp.float32)
            total = lax.fori_loop(g * each, (g + 1) * each, attend, total)
        kv[:, :, :, :, pl.ds(g * LANES, LANES)] = (
            total.astype(jnp.bfloat16).T.reshape(sz.grid + (t, LANES))
        )
    order.until("qs")

    wq_full = [lanes_of(wq, h, 0, sz.pack) for h in (0, 1)]
    gain_one = small_in[4:5]
    hidden = tokens_in(sz, hid_in)
    inv_first = lax.rsqrt(jnp.sum(hidden * hidden, axis=-1, keepdims=True) / sz.width + norm_eps)
    normed2[own] = (hidden * inv_first * gain_one).astype(jnp.bfloat16)
    x_n.start()
    cosine, sine = cos_in[...], sin_in[...]
    scale = HEAD_DIM ** (-0.5)
    dq = jnp.concatenate(
        [
            dq_h[1](h)
            for h in range(HEADS)
        ]
        + [jnp.zeros((t, HEAD_DIM), jnp.float32)],
        axis=1,
    ) * scale
    dq = dq * repeat_lanes(cosine, 8 * LANES) - swap_halves(dq) * repeat_lanes(sine, 8 * LANES)
    d_q = dq.astype(jnp.bfloat16).astype(jnp.float32)

    x_err.came()
    both_err = jnp.sum(small2[2][2:3] + small2[3][2:3], axis=-1, keepdims=True)
    link.err[place.pos[0], place.pos[1], place.pos[2]] = jnp.broadcast_to(both_err, (8, LANES))
    order.until("kq")
    d_kv = jnp.concatenate([flows["KC"].total(), flows["KD"].total()], axis=0)
    in_key = lax.rem(lane_index(d_kv.shape), LANES) < HEAD_DIM
    cos_kv = jnp.where(in_key, repeat_lanes(cosine, sz.kv_wide), 1.0)
    sin_kv = jnp.where(in_key, repeat_lanes(sine, sz.kv_wide), 0.0)
    d_kv = d_kv * cos_kv - swap_halves(d_kv) * sin_kv
    d_kv = d_kv.astype(jnp.bfloat16).astype(jnp.float32)
    d_k = jnp.concatenate(
        [d_kv[:, g * LANES : g * LANES + HEAD_DIM] for g in range(KV_HEADS)], axis=1
    )
    d_v = jnp.concatenate(
        [d_kv[:, g * LANES + HEAD_DIM : (g + 1) * LANES] for g in range(KV_HEADS)], axis=1
    )
    qc, kc = sz.q_cols, sz.k_cols
    blank = jnp.zeros((t, sz.pack - sz.cols), jnp.float32)
    d_pack = [
        jnp.concatenate(
            [
                d_q[:, h * qc : (h + 1) * qc],
                d_k[:, h * kc : (h + 1) * kc],
                d_v[:, h * kc : (h + 1) * kc],
                blank,
            ],
            axis=1,
        ).astype(jnp.bfloat16)
        for h in (0, 1)
    ]
    stage[...] = jnp.where(core == 0, d_pack[1], d_pack[0])
    x_pack.start()
    dpack2[own] = jnp.where(core == 0, d_pack[0], d_pack[1])
    d_normed = dot_nt(d_pack[0], wq_full[0]) + dot_nt(d_pack[1], wq_full[1])
    small2[0] = small_in[...]
    small2[0, 2:3] = jnp.sum(d_normed * hidden * inv_first, axis=0, keepdims=True)
    x_small.start()
    x_n.came()
    x_pack.came()
    x_small.came()
    rows = small2[0] + small2[1]
    part = wide // sz.grid[0]
    shape = (sz.side, sz.side)
    for i in range(sz.grid[0]):
        grad = dot_tn(normed2[:, pl.ds(i * part, part)], dpack2[...])
        for b in range(part // sz.rows_p):
            first = i * part + b * sz.rows_p
            line = jnp.concatenate(
                [jnp.zeros((1, sz.gain_lane), jnp.float32)]
                + [rows[r : r + 1, first : first + sz.rows] for r in (2, 0, 1)]
                + [jnp.zeros((1, sz.pack - sz.gain_lane - 3 * sz.rows), jnp.float32)],
                axis=1,
            )
            block = grad[b * sz.rows_p : (b + 1) * sz.rows_p]
            is_line = lax.broadcasted_iota(jnp.int32, block.shape, 0) == sz.rows
            block = jnp.where(is_line, line, block)
            spot = (i, b // sz.side, b % sz.side)
            edge = block[:, sz.win :] + po6[spot].astype(jnp.float32)
            block = jnp.concatenate([block[:, : sz.win], edge], axis=1).astype(jnp.bfloat16)
            wq[(0,) + spot + (slice(None), pl.ds(0, sz.pack))] = block
    order.until("gi")
    scaled = gain_one * d_normed
    d_hid = (
        dhid[...]
        + inv_first * scaled
        - hidden * (inv_first**3 * (jnp.sum(scaled * hidden, axis=-1, keepdims=True) / sz.width))
    )
    ghid_out[...] = tokens_out(sz, d_hid)
    order.until("fin")

    def whole(tensor):
        return jnp.concatenate(
            [flows[name].total() for name in flows if name[0] == tensor], axis=1
        )

    gd_out[...] = narrow(sz, whole("D"))[: sz.ffn_rows]
    gg_out[...] = blocks_cut(whole("G"), sz.ffn_rows, sz.ffn_rows_p)[: sz.rows]
    gu_out[...] = blocks_cut(whole("U"), sz.ffn_rows, sz.ffn_rows_p)[: sz.rows]
    grad = whole("Q")
    grad_out = jnp.concatenate([grad[:, sz.cols :], whole("O")], axis=1)
    go_out[...] = grad_out[: sz.rows, : sz.out_cols]
    gq_out[...] = grad[: sz.rows, :qc]
    gk_out[...] = grad[: sz.rows, qc : qc + kc]
    gv_out[...] = grad[: sz.rows, qc + kc : qc + 2 * kc]
    for r, ref in enumerate((gain1_out, gain2_out, router_out)):
        first = sz.gain_lane + r * sz.rows
        ref[...] = grad[sz.rows : sz.rows + 1, first : first + sz.rows]
    total = jnp.zeros((8, LANES), jnp.float32)
    for i, j, k in chips_of(sz):
        total = total + link.err[i, j, k]
    loss_out[...] = total / (sz.width * small_in[3:4, :LANES])
    for flow in flows.values():
        flow.sent()
    for cp in (x_n, x_pack, x_small, x_err):
        cp.sent()


FORWARD_INS = 13


def set_back_flows(sz, link, partial, kv, err, lands):
    link.err = err
    link.back_flows = backward_flows(sz, link.place, link.sems, partial, kv, err, lands)
    link.flows.update(link.back_flows)


def whole_kernel(sz, *refs):
    at = FORWARD_INS
    ins = refs[:at]
    state, ghid, gq, gk, gv, go, gg, gu, gd, gain1, gain2, router, loss, prob_hbm = refs[at : at + 14]
    refs = refs[at + 14 :]
    small, heads, dctx, cosine, sine, po6 = refs[:6]
    first, refs = refs[6 : 6 + 21], refs[6 + 21 :]
    normed2, dpack2, stage, small2, err, lands, send, recv, local = refs
    wq, wg, wu, wd, kv, bias, prob = first[:7]
    dhid, gates = bias.at[:, pl.ds(0, sz.wide)], first[10]
    per = sz.ffn_half // LANES

    def dq_put(st, rows, value):
        for sub in range(sz.step_heads):
            h = st * sz.step_heads + sub
            part = value[sub * sz.tokens : (sub + 1) * sz.tokens]
            gates[h // per, :, pl.ds(h % per * LANES, LANES)] = part

    def dq_get(h):
        return gates[h // per, :, pl.ds(h % per * LANES, LANES)][:, :HEAD_DIM]

    link = Link(sz, ORDER, send, recv, local)
    partial = {"q": wq, "o": wq, "g": wg, "u": wu, "d": wd}
    partial = {name: ref.at[0] for name, ref in partial.items()}
    set_back_flows(sz, link, partial, kv, err, lands)
    forward_part(
        sz, link, *ins, state, dhid, small, prob_hbm, heads, dctx, cosine, sine, po6, *first, {}, True
    )
    backward_part(
        sz, link, prob_hbm, heads, dctx, ins[11], dhid, small, cosine, sine, po6,
        ghid, gq, gk, gv, go, gg, gu, gd, gain1, gain2, router, loss,
        wq, kv, prob, (dq_put, dq_get), normed2, dpack2, stage, small2, True,
    )


def forward_kernel(sz, *refs):
    at = FORWARD_INS
    ins, refs = refs[:at], refs[at:]
    state, dhid, small, wq_out, kv_out, prob, heads, dctx, cosine, sine, po6 = refs[:11]
    keep = dict(zip("qkguod", (wq_out, kv_out) + refs[11:15]))
    first, (send, recv, local) = refs[15 : 15 + 21], refs[15 + 21 :]
    link = Link(sz, ORDER, send, recv, local)
    forward_part(
        sz, link, *ins, state, dhid, small, prob, heads, dctx, cosine, sine, po6, *first, keep, False
    )


def backward_kernel(sz, *refs):
    wq_in, kv_in, prob_in, heads, dctx, pg_in, pu_in, po_in, pd_in, *more = refs[:15]
    outs, refs = refs[15 : 15 + 12], refs[15 + 12 :]
    wq, kv, prob, dq_h, normed2, dpack2, stage, pg, pu, pd, small2, err, lands = refs[:13]
    send, recv, local = refs[13:]
    link = Link(sz, ORDER[ORDER.index("bwd") + 1 :], send, recv, local)

    def dq_put(st, rows, value):
        dq_h[st, rows] = value

    def dq_get(h):
        return dq_h[h // sz.step_heads, pl.ds(h % sz.step_heads * sz.tokens, sz.tokens), :HEAD_DIM]

    partial = {"q": wq.at[0], "o": wq.at[0], "g": pg, "u": pu, "d": pd}
    set_back_flows(sz, link, partial, kv, err, lands)
    po = wq.at[0, :, :, :, :, pl.ds(sz.pack, sz.full - sz.pack)]
    pairs = ((pd_in, pd), (pg_in, pg), (pu_in, pu), (po_in, po), (kv_in, kv), (wq_in, wq))
    link.gets = {name: link.bring(src, dst) for name, (src, dst) in zip("dguokq", pairs)}
    for name, cp in link.gets.items():
        if name != "o":
            cp.start()
    backward_part(
        sz, link, prob_in, heads, dctx, *more, *outs,
        wq, kv, prob, (dq_put, dq_get), normed2, dpack2, stage, small2, False,
    )


def count_copies(sz, flows_of, more):
    sems = Sems()
    tensors = dict.fromkeys("qogud")
    flows_of(sz, Place(sz.chips, True), sems, tensors)
    return sems.used + more


def deliver_kernel(*refs):
    half = len(refs) // 2
    for source, target in zip(refs[: half - 1], refs[half:-1]):
        target[...] = source[...]
    refs[-1][0, 0] = refs[half - 1][0, 0]


def body(chips, hidden_in, segment_ids, route_mask, valid_mask, teacher, norm_gain, w_query, w_key,
         w_value, w_out, ffn_gain, w_gate, w_up, w_down, router_weight):
    sz = Sizes(chips, hidden_in.shape, w_gate.shape, w_down.shape)
    t = sz.tokens
    gains = jnp.concatenate([norm_gain, ffn_gain, router_weight])[None]
    low, f32 = jnp.bfloat16, jnp.float32
    grid = sz.grid
    any_spec, vmem_spec = pl.BlockSpec(memory_space=pl.ANY), pl.BlockSpec(memory_space=pltpu.VMEM)
    shape = jax.ShapeDtypeStruct
    gate_shape = grid + (sz.rows_p, sz.ffn_half)
    out_shape = grid + (sz.rows_p, sz.full - sz.pack)
    edge_shape = grid + (sz.rows_p, sz.pack - sz.win)
    down_shape = grid + (sz.ffn_rows_p, sz.half)
    pack_shape = grid + (sz.rows_p, sz.full)
    kv_shape = grid + (t, sz.kv_wide)
    head_shape = (sz.steps, sz.step_rows, LANES)
    prob_shape = (sz.steps, sz.step_rows, sz.keys)
    copies_f = count_copies(sz, lambda *a: forward_flows(*a, None), 7)
    copies_b = count_copies(sz, lambda *a: backward_flows(*a, None, None, None), 4)
    first_scratch = [
        pltpu.VMEM((2,) + pack_shape, low),
        pltpu.VMEM((2,) + gate_shape, low),
        pltpu.VMEM((2,) + gate_shape, low),
        pltpu.VMEM((2,) + down_shape, low),
        pltpu.VMEM(kv_shape, low),
        pltpu.VMEM((t, sz.keys), sz.bias_type),
        pltpu.VMEM((sz.slots, sz.step_rows, sz.keys), low),
        pltpu.VMEM((t, sz.wide), f32),
        pltpu.VMEM((2 * t, sz.wide), low),
        pltpu.VMEM((2, 2 * t, sz.ffn_half), low),
        pltpu.VMEM((2, t, sz.ffn_half), f32),
        pltpu.VMEM((2, t, sz.ffn_half), f32),
        pltpu.VMEM((2 * t, sz.wide), low),
        pltpu.VMEM((2 * t, sz.window), low),
        pltpu.VMEM((2 * t, sz.half), low),
        pltpu.VMEM((2 * t, sz.ffn_half), low),
        pltpu.VMEM((2 * t, sz.ffn_half), low),
        pltpu.VMEM((t, sz.half), low),
        pltpu.VMEM((t, sz.window), low),
        pltpu.VMEM((2, t, sz.ffn_half), low),
        pltpu.VMEM((t, 8), f32),
    ]
    lands = []
    for name, tensor, first, span in pack_flows(sz) + weight_flows(sz):
        rows = sz.ffn_rows_p if tensor == "d" else sz.rows_p
        lands += land_shapes(grid, ORDERS[name[1].upper()], rows, span)
    for name, r0, rn, first, span in kv_flows(sz):
        lands += land_shapes(grid, ORDERS[name[1].upper()], rn, span)
    second_scratch = [
        pltpu.VMEM(head_shape, f32),
        pltpu.VMEM((2 * t, sz.wide), low),
        pltpu.VMEM((2 * t, sz.pack), low),
        pltpu.VMEM((t, sz.pack), low),
    ]
    last_scratch = [pltpu.VMEM((4, 8, sz.wide), f32), pltpu.VMEM(grid + (8, LANES), f32), lands]
    results = [
        shape((sz.width, t), low),
        shape((sz.rows, sz.q_cols), f32),
        shape((sz.rows, sz.k_cols), f32),
        shape((sz.rows, sz.k_cols), f32),
        shape((sz.rows, sz.width // 2), f32),
        shape((sz.rows, sz.ffn_cols), f32),
        shape((sz.rows, sz.ffn_cols), f32),
        shape((sz.ffn_rows, sz.width // 2), f32),
        shape((1, sz.rows), f32),
        shape((1, sz.rows), f32),
        shape((1, sz.rows), f32),
        shape((8, LANES), f32),
    ]
    ins = (
        w_query, w_key, w_value, w_out, w_gate, w_up, w_down, gains,
        segment_ids, route_mask, valid_mask, hidden_in[0].T, teacher[0].T,
    )
    state_shape, dhid_shape = shape((sz.width, t), low), shape((t, sz.wide), f32)
    small_shape, table_shape = shape((8, sz.wide), f32), shape((t, LANES), f32)

    def sem_scratch(copies):
        return [pltpu.SemaphoreType.DMA((count,)) for count in (copies, copies, 16)]

    def params(number):
        return pltpu.CompilerParams(
            collective_id=number, has_side_effects=True, vmem_limit_bytes=VMEM_LIMIT
        )

    if sz.keys <= 4096:
        outs = pl.pallas_call(
            functools.partial(whole_kernel, sz),
            out_shape=[state_shape] + results + [shape(prob_shape, low)],
            in_specs=[vmem_spec] * FORWARD_INS,
            out_specs=[vmem_spec] * 13 + [any_spec],
            scratch_shapes=[
                pltpu.VMEM(small_shape.shape, f32),
                pltpu.VMEM(head_shape, low),
                pltpu.VMEM(head_shape, low),
                pltpu.VMEM(table_shape.shape, f32),
                pltpu.VMEM(table_shape.shape, f32),
                pltpu.VMEM(edge_shape, low),
            ]
            + first_scratch
            + second_scratch[1:]
            + last_scratch
            + sem_scratch(copies_f + copies_b),
            compiler_params=params(0),
            name="whole",
        )(*ins)
        outs = outs[:-1]
    else:
        outs = pl.pallas_call(
            functools.partial(forward_kernel, sz),
            out_shape=[
                state_shape,
                dhid_shape,
                small_shape,
                shape((2,) + pack_shape, low),
                shape(kv_shape, low),
                shape(prob_shape, low),
                shape(head_shape, low),
                shape(head_shape, low),
                table_shape,
                table_shape,
                shape(edge_shape, low),
                shape(gate_shape, low),
                shape(gate_shape, low),
                shape(out_shape, low),
                shape(down_shape, low),
            ],
            in_specs=[vmem_spec] * FORWARD_INS,
            out_specs=[vmem_spec] * 3 + [any_spec] * 3 + [vmem_spec] * 5 + [any_spec] * 4,
            scratch_shapes=first_scratch + sem_scratch(copies_f),
            compiler_params=params(1),
            name="forward",
        )(*ins)
        state, dhid, small, wq_all, kv_all, prob, heads, dctx, cosine, sine, edge, pg, pu, po, pd = outs
        outs = pl.pallas_call(
            functools.partial(backward_kernel, sz),
            out_shape=results,
            in_specs=[any_spec] * 3 + [vmem_spec] * 2 + [any_spec] * 4 + [vmem_spec] * 6,
            out_specs=[vmem_spec] * 12,
            scratch_shapes=[
                pltpu.VMEM((2,) + pack_shape, low),
                pltpu.VMEM(kv_shape, low),
                pltpu.VMEM((2, sz.step_rows // sz.row_parts, sz.keys), low),
            ]
            + second_scratch
            + [
                pltpu.VMEM(gate_shape, low),
                pltpu.VMEM(gate_shape, low),
                pltpu.VMEM(down_shape, low),
            ]
            + last_scratch
            + sem_scratch(copies_b),
            compiler_params=params(2),
            name="backward",
        )(
            wq_all, kv_all, prob, heads, dctx, pg, pu, po, pd,
            ins[11], dhid, small, cosine, sine, edge,
        )
        outs = [state] + list(outs)
    last = len(outs) - 1
    state, ghid, gq, gk, gv, go, gg, gu, gd, gain1, gain2, router, loss = pl.pallas_call(
        deliver_kernel,
        out_shape=[shape(o.shape, o.dtype) for o in outs[:-1]] + [shape((1, 1), f32)],
        in_specs=[vmem_spec] * (last + 1),
        out_specs=[vmem_spec] * last + [pl.BlockSpec(memory_space=pltpu.SMEM)],
        name="deliver",
    )(*outs)
    return (
        state.T[None],
        loss.reshape(()),
        ghid.T[None],
        gain1.reshape(-1),
        gq,
        gk,
        gv,
        go,
        gain2.reshape(-1),
        gg,
        gu,
        gd,
        router.reshape(-1),
    )


def solution(mesh):
    tokens, rows, blocks = P("dp", "seq", None), P("dp", "seq"), P("seq", "dp")
    vector = P("seq")
    return jax.shard_map(
        functools.partial(body, mesh.shape["seq"]),
        mesh=mesh,
        in_specs=(
            tokens, rows, rows, rows, tokens, vector, blocks, blocks, blocks, blocks, vector,
            blocks, blocks, blocks, vector,
        ),
        out_specs=(
            tokens, P(), tokens, vector, blocks, blocks, blocks, blocks, vector, blocks, blocks,
            blocks, vector,
        ),
        check_vma=False,
    )
```

```python
import functools
import math

import jax
import jax.numpy as jnp
from jax import lax
from jax.experimental import pallas as pl
from jax.experimental.pallas import tpu as pltpu
from jax.sharding import PartitionSpec as P

HEADS = 15
KV_HEADS = 5
HEAD_DIM = 64
GROUPS = HEADS // KV_HEADS
LANES = 128

norm_eps = 1e-05
masked_score = -1e30

MESH = pl.DeviceIdType.MESH
VMEM_LIMIT = 62 * 2**20

ORDERS = {"C": (0, 2, 1), "D": (0, 1, 2), "E": (2, 1, 0), "F": (1, 2, 0)}


def round_up(value, unit):
    return (value + unit - 1) // unit * unit


class Sizes:
    def __init__(self, chips, hidden_block, gate_block, down_block):
        self.chips = chips
        _, self.tokens, self.width = hidden_block
        self.side = math.isqrt(chips // 4)
        self.grid = (4, self.side, self.side)
        self.keys = self.tokens * chips
        self.rows, _ = gate_block
        self.rows_p = round_up(self.rows, 16)
        self.wide = chips * self.rows_p
        self.half = self.wide // 2
        self.ffn_rows = down_block[0]
        self.ffn_rows_p = round_up(self.ffn_rows, 16)
        self.ffn_half = chips * self.ffn_rows_p // 2
        self.q_cols = HEADS * HEAD_DIM // 2
        self.k_cols = KV_HEADS * HEAD_DIM // 2
        self.cols = self.q_cols + 2 * self.k_cols
        self.pack = round_up(self.cols, LANES)
        self.out_cols = self.width // 2
        self.full = round_up(self.cols + self.out_cols, LANES)
        self.win = self.cols // LANES * LANES
        self.skip = self.cols - self.win
        self.window = self.full - self.win
        self.ffn_cols = gate_block[1]
        self.gain_lane = 3 * self.tokens
        assert self.rows < self.rows_p and self.gain_lane + 3 * self.rows <= self.win
        self.step_heads = GROUPS if self.keys <= 4096 else 1
        self.steps = HEADS // self.step_heads
        self.steps_per_kv = GROUPS // self.step_heads
        self.step_rows = self.step_heads * self.tokens
        self.kv_wide = KV_HEADS * LANES
        self.slots = 2 if self.keys <= 4096 else 1
        self.row_parts = 1 if self.keys <= 4096 else 4
        self.bias_type = jnp.float32 if self.keys <= 4096 else jnp.bfloat16


def hands_on(grid):
    return grid[1] == 2


class Place:
    def __init__(self, chips, count_only=False):
        side = math.isqrt(chips // 4)
        self.sizes = (4, side, side)
        self.strides = (side * side, side, 1)
        self.count_only, self.hands_on = count_only, hands_on(self.sizes)
        if count_only:
            self.core, self.chip, self.pos = 0, 0, (0, 0, 0)
            return
        self.core = lax.axis_index("dp")
        self.chip = lax.axis_index("seq")
        self.pos = (
            self.chip // (side * side),
            lax.rem(self.chip // side, side),
            lax.rem(self.chip, side),
        )

    def near(self, axis):
        p = self.pos[axis]
        return p + 1 - 2 * lax.rem(p, 2) if not self.count_only else 1

    def far(self, axis):
        p = self.pos[axis]
        return lax.rem(p + 2, 4) if not self.count_only else 2

    def middle(self, axis):
        p = self.pos[axis]
        return jnp.logical_or(p == 1, p == 2) if not self.count_only else False

    def outer(self, axis):
        p = self.pos[axis]
        return jnp.logical_or(p == 0, p == 3) if not self.count_only else True

    def others(self, axis):
        p = self.pos[axis]
        return [1 - p] if self.sizes[axis] == 2 else [self.near(axis), self.far(axis), 3 - p]

    def back_order(self, axis):
        return self.others(axis)[::-1] + [self.pos[axis]]

    def at(self, axis, other):
        return (self.core, self.chip + (other - self.pos[axis]) * self.strides[axis])

    def peer(self):
        return (1 - self.core, self.chip)

    def greet(self):
        barrier = pltpu.get_barrier_semaphore()
        devices = [self.peer()]
        for axis, size in enumerate(self.sizes):
            devices += [self.at(axis, other) for other in self.others(axis)]
        for dev in devices:
            pl.semaphore_signal(barrier, inc=1, device_id=dev, device_id_type=MESH)
        pl.semaphore_wait(barrier, len(devices))


class Sems:
    def __init__(self, send=None, recv=None):
        self.send, self.recv, self.used = send, recv, 0

    def take(self):
        self.used += 1
        return self.used - 1


def when(cond, body):
    if cond is None:
        body()
    else:
        pl.when(cond)(body)


class Copy:
    def __init__(self, sems, src, dst, dev, come, send_if=None, recv_if=None):
        self.i, self.sems = sems.take(), sems
        self.src, self.dst, self.dev, self.come = src, dst, dev, come
        self.send_if, self.recv_if = send_if, recv_if

    def _make(self, src, dst):
        return pltpu.make_async_remote_copy(
            src_ref=src(),
            dst_ref=dst(),
            send_sem=self.sems.send.at[self.i],
            recv_sem=self.sems.recv.at[self.i],
            device_id=self.dev,
            device_id_type=MESH,
        )

    def start(self):
        when(self.send_if, lambda: self._make(self.src, self.dst).start())

    def sent(self):
        when(self.send_if, lambda: self._make(self.src, self.dst).wait_send())

    def came(self):
        when(self.recv_if, lambda: self._make(self.come, self.come).wait_recv())


class Line:
    def __init__(self, place, sems, axis, unit):
        self.size, p = place.sizes[axis], place.pos[axis]
        self.hands_on, self.slow = place.hands_on and axis == 0, axis == 0
        at = functools.partial(place.at, axis)

        def copy(block, to, come, send_if=None, recv_if=None):
            src = lambda: unit(block)
            return Copy(sems, src, src, at(to), lambda: unit(come), send_if, recv_if)

        if self.size == 2:
            self.near = copy(p, 1 - p, 1 - p)
            self.all = [self.near]
            self.others = [1 - p]
            return
        near, far, last = place.near(axis), place.far(axis), self.size - 1 - p
        self.near = copy(p, near, near)
        self.far = copy(p, far, far)
        self.others = [near, far, last]
        if self.hands_on:
            mid = place.middle(axis)
            self.across = copy(p, last, last, mid, mid)
            self.relayed = copy(far, near, last, mid, place.outer(axis))
            self.all = [self.near, self.far, self.across, self.relayed]
        else:
            self.across = copy(p, last, last)
            self.all = [self.near, self.far, self.across]

    def start(self):
        self.near.start()
        if self.size > 2:
            self.far.start()
            self.across.start()

    def relay(self):
        if not self.hands_on:
            return
        self.far.came()
        self.relayed.start()

    def arrivals(self, then):
        self.near.came()
        then(0)
        if self.size > 2:
            if not self.hands_on:
                self.far.came()
            then(1)
            self.across.came()
            if self.hands_on:
                self.relayed.came()
            then(2)


class Gather:
    def __init__(self, place, sems, view, order, twin=None):
        self.view, self.twin, self.order = view, twin, order
        a, b, c = order
        pos = place.pos
        first = Line(place, sems, a, lambda j: self._ref(j, pos[b], pos[c]))
        second = Line(place, sems, b, lambda j: self._ref(None, j, pos[c]))
        third, cross = [], []
        for jb in [pos[b]] + second.others:
            line = Line(place, sems, c, lambda j, jb=jb: self._ref(None, jb, j))
            third.append(line)
            if twin is not None:
                cross.append([self._cross(place, sems, jb, jc) for jc in [pos[c]] + line.others])
        self.all = first.all + second.all + sum((line.all for line in third), []) + sum(cross, [])

        def spread(m):
            third[m].start()
            if cross:
                cross[m][0].start()

        def finish_first():
            first.arrivals(lambda k: None)
            second.start()
            spread(0)

        def finish_third():
            for m, line in enumerate(third):
                line.arrivals(lambda k, m=m: cross[m][k + 1].start() if cross else None)

        self.rounds = [first.start]
        if first.slow:
            self.rounds.append(first.relay)
        self.rounds.append(finish_first)
        if second.slow:
            self.rounds.append(second.relay)
        self.rounds.append(lambda: second.arrivals(lambda k: spread(k + 1)))
        if third[0].slow:
            self.rounds.append(lambda: [line.relay() for line in third])
        self.rounds.append(finish_third)
        if cross:
            self.rounds.append(lambda: [c.came() for some in cross for c in some])

    def _ref(self, ia, ib, ic, twin=False):
        idx = [None] * 3
        for axis, i in zip(self.order, (ia, ib, ic)):
            idx[axis] = slice(None) if i is None else i
        return (self.twin if twin else self.view)(*idx)

    def _cross(self, place, sems, jb, jc):
        here = lambda: self._ref(None, jb, jc)
        return Copy(sems, here, here, place.peer(), lambda: self._ref(None, jb, jc, True))

    def sent(self):
        for c in self.all:
            c.sent()


class BackLine:
    def __init__(self, place, sems, axis, unit, land):
        self.size, p = place.sizes[axis], place.pos[axis]
        self.hands_on, self.slow = place.hands_on and axis == 0, axis == 0
        self.unit, self.land, self.p = unit, land, p
        at = functools.partial(place.at, axis)

        def copy(block, to, slot, send_if=None, recv_if=None):
            spot = lambda: land(slot)
            return Copy(sems, lambda: unit(block), spot, at(to), spot, send_if, recv_if)

        if self.size == 2:
            self.near = copy(1 - p, 1 - p, 0)
            self.all = [self.near]
            return
        near, far, last = place.near(axis), place.far(axis), self.size - 1 - p
        mid, outer = place.middle(axis), place.outer(axis)
        self.where_far, self.mid = far, mid
        self.near = copy(near, near, 0)
        self.far = copy(far, far, 1)
        if not self.hands_on:
            self.across = copy(last, last, 2)
            self.all = [self.near, self.far, self.across]
            return
        self.across = copy(last, last, 2, mid, mid)
        self.relayed = copy(last, near, 3, outer, mid)
        self.all = [self.near, self.far, self.across, self.relayed]

    def _add(self, block, slots):
        ref = self.unit(block)
        total = ref[...].astype(jnp.float32)
        for slot in slots:
            total = total + self.land(slot)[...].astype(jnp.float32)
        return total

    def start(self):
        if self.hands_on:
            self.relayed.start()
            self.near.start()
        else:
            for cp in self.all:
                cp.start()

    def relay(self):
        if not self.hands_on:
            return
        self.across.start()
        self.relayed.came()

        def body():
            ref = self.unit(self.where_far)
            ref[...] = self._add(self.where_far, (3,)).astype(ref.dtype)

        pl.when(self.mid)(body)
        self.far.start()

    def came(self):
        self.near.came()
        if self.size > 2:
            self.far.came()
            self.across.came()
        if self.hands_on:

            def body():
                ref = self.unit(self.p)
                ref[...] = self._add(self.p, (2,)).astype(ref.dtype)

            pl.when(self.mid)(body)

    def total(self):
        return self._add(self.p, range(2 if self.hands_on else self.size - 1))

    def collect(self):
        self.came()
        ref = self.unit(self.p)
        ref[...] = self.total().astype(ref.dtype)


class Scatter:
    def __init__(self, place, sems, view, order, lands):
        self.view, self.order = view, order
        a, b, c = order
        pos = place.pos
        land_c, land_b, land_a = lands if lands is not None else (None,) * 3
        spots = place.back_order(b)
        first = [
            BackLine(
                place, sems, c,
                lambda j, jb=jb: self._ref(None, jb, j),
                lambda slot, m=m: land_c.at[m, slot],
            )
            for m, jb in enumerate(spots)
        ]
        second = BackLine(
            place, sems, b, lambda j: self._ref(None, j, pos[c]), lambda slot: land_b.at[slot]
        )
        third = BackLine(
            place, sems, a, lambda j: self._ref(j, pos[b], pos[c]), lambda slot: land_a.at[slot]
        )
        self.third = third
        self.all = sum((line.all for line in first), []) + second.all + third.all

        def finish_first():
            for line in first:
                line.collect()
            second.start()

        def finish_second():
            second.collect()
            third.start()

        self.rounds = [lambda: [line.start() for line in first]]
        if first[0].slow:
            self.rounds.append(lambda: [line.relay() for line in first])
        self.rounds.append(finish_first)
        if second.slow:
            self.rounds.append(second.relay)
        self.rounds.append(finish_second)
        if third.slow:
            self.rounds.append(third.relay)
        self.rounds.append(third.came)

    def _ref(self, ia, ib, ic):
        idx = [None] * 3
        for axis, i in zip(self.order, (ia, ib, ic)):
            idx[axis] = slice(None) if i is None else i
        return self.view(*idx)

    def sent(self):
        for cp in self.all:
            cp.sent()

    def total(self):
        return self.third.total()


def land_shapes(grid, order, rows, cols):
    a, b, c = (grid[axis] for axis in order)
    slots_a, slots_b, slots_c = (
        4 if axis == 0 and hands_on(grid) else grid[axis] - 1 for axis in order
    )
    return [
        pltpu.VMEM((b, slots_c, a, rows, cols), jnp.bfloat16),
        pltpu.VMEM((slots_b, a, rows, cols), jnp.bfloat16),
        pltpu.VMEM((slots_a, rows, cols), jnp.bfloat16),
    ]


def tiles(total, **shares):
    out, at = [], 0
    names = list(shares)
    for name in names:
        span = shares[name] if name != names[-1] else total // LANES - at
        out.append((name, at * LANES, span * LANES))
        at += span
    return out


def weight_flows(sz):
    out = []
    for tensor, total, shares in (
        ("g", sz.ffn_half, dict(E=5, D=5)),
        ("u", sz.ffn_half, dict(F=5, C=5)),
        ("o", sz.full - sz.pack, dict(D=3)),
        ("d", sz.half, dict(C=2, D=2)),
    ):
        at = sz.pack if tensor == "o" else 0
        out += [(tensor + x, tensor, at + first, span) for x, first, span in tiles(total, **shares)]
    return out


def pack_flows(sz):
    return [("q" + n, "q", f, s) for n, f, s in tiles(sz.pack, E=1, C=3, D=3)]


def kv_flows(sz):
    half = sz.tokens // 2
    return [("kC", 0, half, 0, sz.kv_wide), ("kD", half, half, 0, sz.kv_wide)]


ORDER = (
    "qD0", "others", "uF0", "qE0", "qC0", "qE1", "gE0", "qD1", "qE2", "oD0", "qD2", "qC1", "uC0",
    "qC2", "qD3", "qE3", "gD0", "qE4", "qC3", "oD1", "oD2", "uC1", "dC0", "prep", "uC2", "qD4",
    "gD1", "dD0", "qD5", "qC4", "qC5", "oD3", "qE5", "qkv", "heads", "kC0", "uC3", "kD0", "uF1",
    "gD2", "kC1", "dC1", "kC2", "mask", "kD1", "kD2", "uF2", "dD1", "oD4", "kC3", "gD3", "kD3",
    "gE1", "uC4", "uF3", "uC5", "gD4", "dC2", "gE2", "dD2", "kC4", "oD5", "kD4", "atta", "attb",
    "uF4", "dC3", "attc", "dD3", "gE3", "gD5", "attd", "atte", "gE4", "dC4", "uF5", "out", "dD4",
    "gE5", "gu", "dD5", "dC5", "down", "bwd", "pd", "bwdb", "pg", "GE0", "DC0", "DD0", "pu",
    "bwdc", "po", "OD0", "GE1", "batta", "battb", "battc", "UF0", "battd", "batte", "KC0", "KD0",
    "DD1", "qs", "EC0", "UF1", "KC1", "DC1", "GD0", "KD1", "UC0", "DD2", "KC2", "DD3", "KD2",
    "DC2", "KC3", "OD1", "KD3", "GE2", "UC1", "GD1", "DC3", "OD2", "KC4", "KD4", "kq", "EC1",
    "EC2", "QE0", "gi", "EC3", "QE1", "QD0", "QC0", "UF2", "OD3", "GE3", "DD4", "UC2", "UC3",
    "QD1", "GD2", "GD3", "DC4", "QC1", "UF3", "OD4", "QD2", "QD3", "QC2", "GE4", "QE2", "QC3",
    "UC4", "QE3", "GD4", "QD4", "QE4", "QC4", "UF4", "EC4", "fin",
)


class Order:
    def __init__(self, flows, words):
        self.flows, self.words, self.at = flows, words, 0

    def until(self, mark):
        while self.words[self.at] != mark:
            word = self.words[self.at]
            if word[-1] in "0123456":
                self.flows[word[:-1]].rounds[int(word[-1])]()
            self.at += 1
        self.at += 1


class Link:
    def __init__(self, sz, words, send, recv, local):
        self.place, self.sems, self.local = Place(sz.chips), Sems(send, recv), local
        self.flows, self.used = {}, 0
        self.order = Order(self.flows, words)

    def slot(self, count=1):
        self.used += count
        return self.used - count

    def bring(self, src, dst):
        return pltpu.make_async_copy(src, dst, self.local.at[self.slot()])

    def to_peer(self, src, dst):
        return Copy(self.sems, lambda: src, lambda: dst, self.place.peer(), lambda: dst)


def dot(left, right):
    return jnp.dot(left, right, preferred_element_type=jnp.float32)


def dot_nt(left, right):
    return lax.dot_general(
        left, right, (((1,), (1,)), ((), ())), preferred_element_type=jnp.float32
    )


def dot_tn(left, right):
    return lax.dot_general(
        left, right, (((0,), (0,)), ((), ())), preferred_element_type=jnp.float32
    )


def blocks_padded(value, block, block_p):
    if block == block_p:
        return value
    zero = jnp.zeros((value.shape[0], block_p - block), value.dtype)
    pieces = []
    for j in range(value.shape[1] // block):
        pieces += [value[:, j * block : (j + 1) * block], zero]
    return jnp.concatenate(pieces, axis=1)


def blocks_cut(value, block, block_p):
    if block == block_p:
        return value
    return jnp.concatenate(
        [value[:, j * block_p : j * block_p + block] for j in range(value.shape[1] // block_p)],
        axis=1,
    )


def lanes_of(ref, which, first, span):
    value = ref[which, :, :, :, :, pl.ds(first, span)]
    return value.reshape(-1, span)


def beside(*pieces):
    return jnp.concatenate([p for p in pieces if p.shape[1] > 0], axis=1)


def spread(sz, value):
    return blocks_padded(value, sz.rows, sz.rows_p)


def narrow(sz, value):
    return blocks_cut(value, sz.rows, sz.rows_p)


def tokens_in(sz, ref):
    value = ref[...].astype(jnp.float32)
    zero = jnp.zeros((sz.rows_p - sz.rows, sz.tokens), jnp.float32)
    pieces = []
    for j in range(sz.chips):
        pieces += [value[j * sz.rows : (j + 1) * sz.rows], zero]
    return jnp.concatenate(pieces, axis=0).T


def tokens_out(sz, value):
    value = value.T
    pieces = [value[j * sz.rows_p : j * sz.rows_p + sz.rows] for j in range(sz.chips)]
    return jnp.concatenate(pieces, axis=0).astype(jnp.bfloat16)


def rows_padded(value, rows):
    if value.shape[0] < rows:
        zero = jnp.zeros((rows - value.shape[0], value.shape[1]), value.dtype)
        value = jnp.concatenate([value, zero], axis=0)
    return value.astype(jnp.bfloat16)


def lane_index(shape):
    return lax.broadcasted_iota(jnp.int32, shape, len(shape) - 1)


def swap_halves(value):
    span = value.shape[1]
    first = lax.rem(lane_index(value.shape), HEAD_DIM) < HEAD_DIM // 2
    return jnp.where(
        first,
        pltpu.roll(value, span - HEAD_DIM // 2, 1),
        pltpu.roll(value, HEAD_DIM // 2, 1),
    )


def repeat_lanes(table, span):
    return jnp.concatenate([table] * (span // LANES), axis=1)


def chips_of(sz):
    return [(i, j, k) for i in range(sz.grid[0]) for j in range(sz.side) for k in range(sz.side)]


def gain_row(sz, wq, which):
    first = sz.gain_lane + which * sz.rows
    zero = jnp.zeros((1, sz.rows_p - sz.rows), jnp.float32)
    pieces = []
    for i, j, k in chips_of(sz):
        line = wq[0, i, j, k, sz.rows : sz.rows + 1, : sz.win].astype(jnp.float32)
        pieces += [line[:, first : first + sz.rows], zero]
    return jnp.concatenate(pieces, axis=1)


def rotary_tables(sz, place):
    lane = lane_index((sz.tokens, LANES))
    row = lax.broadcasted_iota(jnp.int32, (sz.tokens, LANES), 0)
    half = HEAD_DIM // 2
    place_of = (place.chip * sz.tokens + row).astype(jnp.float32)
    inv_freq = jnp.exp(lax.rem(lane, half).astype(jnp.float32) * (-math.log(10000.0) / half))
    angles = place_of * inv_freq
    sine = jnp.sin(angles)
    return jnp.cos(angles), jnp.where(lax.rem(lane, HEAD_DIM) < half, -sine, sine)


def forward_flows(sz, place, sems, full, kv):
    flows = {}
    for name, tensor, first, span in pack_flows(sz) + weight_flows(sz):

        def view(half, ref=full[tensor], first=first, span=span):
            return lambda i, j, k: ref.at[half, i, j, k, :, pl.ds(first, span)]

        core = place.core
        flows[name] = Gather(place, sems, view(core), ORDERS[name[1].upper()], view(1 - core))
    for name, r0, rn, first, span in kv_flows(sz):

        def view(i, j, k, r0=r0, rn=rn, first=first, span=span):
            return kv.at[i, j, k, pl.ds(r0, rn), pl.ds(first, span)]

        flows[name] = Gather(place, sems, view, ORDERS[name[1].upper()])
    return flows


def backward_flows(sz, place, sems, partial, kv, err, lands):
    flows, at = {}, 0
    for name, tensor, first, span in pack_flows(sz) + weight_flows(sz):

        def view(i, j, k, ref=partial[tensor], first=first, span=span):
            return ref.at[i, j, k, :, pl.ds(first, span)]

        land = None if lands is None else lands[at : at + 3]
        flows[name[0].upper() + name[1:]] = Scatter(place, sems, view, ORDERS[name[1].upper()], land)
        at += 3
    for name, r0, rn, first, span in kv_flows(sz):

        def view(i, j, k, r0=r0, rn=rn, first=first, span=span):
            return kv.at[i, j, k, pl.ds(r0, rn), pl.ds(first, span)]

        land = None if lands is None else lands[at : at + 3]
        flows[name[0].upper() + name[1:]] = Scatter(place, sems, view, ORDERS[name[1].upper()], land)
        at += 3
    flows["EC"] = Gather(place, sems, lambda i, j, k: err.at[i, j, k], ORDERS["C"])
    return flows


def forward_part(
    sz, link,
    q_in, k_in, v_in, out_in, gate_in, up_in, down_in, gains_in, seg_in, route_in, valid_in,
    hid_in, teach_in,
    state_out, dhid_out, small_out, prob_out, heads_out, dctx_out, cos_out, sin_out,
    po6,
    wq, wg, wu, wd, kv, bias, prob, hid, normed2, act, gate_s, up_s, ctx2, datt2, dffn2,
    dgate2, dup2, stage_d, stage_o, stage_h, col_in, keep, fused,
):
    place, sems, order, local = link.place, link.sems, link.order, link.local
    core = place.core
    t, n, wide = sz.tokens, sz.chips, sz.wide
    ctx_h = dctx_out
    full = {"q": wq, "o": wq, "g": wg, "u": wu, "d": wd}
    flows = forward_flows(sz, place, sems, full, kv)
    link.flows.update(flows)
    own, other = pl.ds(0, t), pl.ds(t, t)
    x_n2 = link.to_peer(normed2.at[own], normed2.at[other])
    x_act = link.to_peer(act.at[:, own], act.at[:, other])
    x_ctx = link.to_peer(ctx2.at[own], ctx2.at[other])
    x_dffn = link.to_peer(stage_d, dffn2.at[other])
    x_datt = link.to_peer(stage_o, datt2.at[other])
    x_dgate = link.to_peer(stage_h.at[0], dgate2.at[other])
    x_dup = link.to_peer(stage_h.at[1], dup2.at[other])

    f32 = jnp.float32
    spot = (core,) + place.pos
    marks = [ref[...].astype(f32) for ref in (seg_in, route_in, valid_in)]
    rest = sz.full - sz.gain_lane - 3 * sz.rows
    line = jnp.concatenate(marks + [gains_in[...].astype(f32), jnp.zeros((1, rest), f32)], axis=1)
    block = beside(
        *(ref[...].astype(f32) for ref in (q_in, k_in, v_in, out_in)),
        jnp.zeros((sz.rows, sz.full - sz.cols - sz.out_cols), f32),
    )
    wq[spot] = rows_padded(jnp.concatenate([block, line], axis=0), sz.rows_p)
    place.greet()
    order.until("others")
    for ref, own_in in ((wg, gate_in), (wu, up_in)):
        block = blocks_padded(own_in[...].astype(f32), sz.ffn_rows, sz.ffn_rows_p)
        ref[spot] = rows_padded(block, sz.rows_p)
    wd[spot] = rows_padded(spread(sz, down_in[...].astype(f32)), sz.ffn_rows_p)

    order.until("prep")
    hid[...] = tokens_in(sz, hid_in)
    hidden = hid[...]
    inv_first = lax.rsqrt(jnp.sum(hidden * hidden, axis=-1, keepdims=True) / sz.width + norm_eps)
    cos_out[...], sin_out[...] = rotary_tables(sz, place)
    col_in[...] = jnp.concatenate(marks + [jnp.zeros((5, t), f32)], axis=0).T
    cosine, sine = repeat_lanes(cos_out[...], 8 * LANES), repeat_lanes(sin_out[...], 8 * LANES)

    order.until("qkv")
    wq_full = [lanes_of(wq, h, 0, sz.pack) for h in (0, 1)]
    gain_one = gain_row(sz, wq, 0)
    normed = (hidden * inv_first * gain_one).astype(jnp.bfloat16)
    halves = [dot(normed, w) for w in wq_full]
    qc, kc = sz.q_cols, sz.k_cols
    q_pre = jnp.concatenate(
        [halves[0][:, :qc], halves[1][:, :qc], jnp.zeros((t, 8 * LANES - 2 * qc), jnp.float32)],
        axis=1,
    )
    pad_k = jnp.zeros((t, 3 * LANES - 2 * kc), jnp.float32)
    k_pre = jnp.concatenate(
        [halves[0][:, qc : qc + kc], halves[1][:, qc : qc + kc], pad_k], axis=1
    )
    v_pre = jnp.concatenate(
        [halves[0][:, qc + kc : qc + 2 * kc], halves[1][:, qc + kc : qc + 2 * kc]], axis=1
    )
    k_rot = k_pre * cosine[:, : 3 * LANES] + swap_halves(k_pre) * sine[:, : 3 * LANES]
    kv_own = jnp.concatenate(
        [
            piece[:, g * HEAD_DIM : (g + 1) * HEAD_DIM]
            for g in range(KV_HEADS)
            for piece in (k_rot, v_pre)
        ],
        axis=1,
    )
    kv[place.pos[0], place.pos[1], place.pos[2]] = kv_own.astype(jnp.bfloat16)
    order.until("heads")
    q_rot = q_pre * cosine + swap_halves(q_pre) * sine
    q_low = q_rot.astype(jnp.bfloat16).astype(jnp.float32) * HEAD_DIM ** (-0.5)
    blank = jnp.zeros((t, HEAD_DIM), jnp.float32)
    for h in range(HEADS):
        st, sub = h // sz.step_heads, h % sz.step_heads
        heads_out[st, pl.ds(sub * t, t)] = jnp.concatenate(
            [q_low[:, h * HEAD_DIM : (h + 1) * HEAD_DIM], blank], axis=1
        ).astype(jnp.bfloat16)
    order.until("mask")

    row_at = sz.rows
    seg_col, route_col, valid_col = col_in[:, 0:1], col_in[:, 1:2], col_in[:, 2:3]
    q_pos = place.chip * t + lax.broadcasted_iota(jnp.int32, (t, LANES), 0)
    count = jnp.zeros((1, LANES), jnp.float32)
    for m, (i, j, k) in enumerate(chips_of(sz)):
        line = wq[core, i, j, k, row_at : row_at + 1, : 2 * LANES].astype(jnp.float32)
        seg_row, route_row = line[:, :LANES], line[:, LANES:]
        k_pos = m * t + lane_index((t, LANES))
        allowed = (
            (seg_col == seg_row)
            & (k_pos <= q_pos)
            & ((route_row > 0.5) | (k_pos == q_pos))
        )
        bias[:, m * t : (m + 1) * t] = jnp.where(allowed, 0.0, masked_score).astype(bias.dtype)
        for h in (0, 1):
            count = count + wq[
                h, i, j, k, row_at : row_at + 1, 2 * LANES : 3 * LANES
            ].astype(jnp.float32)
    tok_count = jnp.sum(count, axis=-1, keepdims=True)
    small_out[...] = jnp.zeros(small_out.shape, f32)
    small_out[3:4] = jnp.broadcast_to(tok_count, (1, wide))
    small_out[4:5] = gain_one
    kept = []
    prob_sem = link.slot(sz.slots)

    def attend(st):
        g = st // sz.steps_per_kv
        slot = lax.rem(st, sz.slots)
        lanes = pl.ds(pl.multiple_of(g * LANES, LANES), LANES)
        tile = kv[:, :, :, :, lanes].reshape(sz.keys, LANES)
        s = dot_nt(heads_out[st], tile).reshape(sz.step_heads, t, sz.keys) + bias[...].astype(jnp.float32)[None]
        s = s.reshape(sz.step_rows, sz.keys)
        e = jnp.exp(s - jnp.max(s, axis=-1, keepdims=True))
        p = (e * (1.0 / jnp.sum(e, axis=-1, keepdims=True))).astype(jnp.bfloat16)
        save = pltpu.make_async_copy(prob.at[slot], prob_out.at[st], local.at[prob_sem + slot])

        @pl.when(st >= sz.slots)
        def _():
            save.wait()

        prob[slot] = p
        save.start()
        ctx_h[st] = dot(p, tile).astype(jnp.bfloat16)

    for g in range(KV_HEADS):
        order.until("att%s" % "abcde"[g])
        if g == 0:
            kept += [link.bring(ref, keep[x]) for x, ref in (("q", wq), ("k", kv)) if x in keep]
            for cp in kept:
                cp.start()
        pl.loop(g * sz.steps // KV_HEADS, (g + 1) * sz.steps // KV_HEADS)(attend)
    for slot in range(sz.slots):
        pltpu.make_async_copy(prob.at[slot], prob_out.at[slot], local.at[prob_sem + slot]).wait()

    ctx = jnp.concatenate(
        [
            ctx_h[h // sz.step_heads, pl.ds(h % sz.step_heads * t, t), HEAD_DIM:].astype(jnp.float32)
            for h in range(HEADS)
        ],
        axis=1,
    )
    ctx2[own] = spread(sz, ctx).astype(jnp.bfloat16)
    x_ctx.start()
    order.until("out")
    attn = [dot(ctx2[own], lanes_of(wq, q, sz.win, sz.window)) for q in (0, 1)]
    attn = [value[:, sz.skip : sz.skip + sz.out_cols] for value in attn]
    attn = spread(sz, jnp.concatenate(attn, axis=1))
    hidden = hid[...]
    gain_two, router = gain_row(sz, wq, 1), gain_row(sz, wq, 2)
    residual = hidden + attn
    inv_second = lax.rsqrt(
        jnp.sum(residual * residual, axis=-1, keepdims=True) / sz.width + norm_eps
    )
    normed2[own] = (residual * inv_second * gain_two).astype(jnp.bfloat16)
    x_n2.start()
    order.until("gu")
    for h in (0, 1):
        gate_pre = dot(normed2[own], wg[h].reshape(wide, sz.ffn_half))
        up_pre = dot(normed2[own], wu[h].reshape(wide, sz.ffn_half))
        gate_s[h], up_s[h] = gate_pre, up_pre
        act[h, own] = (gate_pre * jax.nn.sigmoid(gate_pre) * up_pre).astype(jnp.bfloat16)
    x_act.start()
    order.until("down")
    two = sz.grid[0] // 2

    def down(q, h):
        return wd[q, pl.ds(h * two, two)].reshape(sz.ffn_half, sz.half)

    ffn = jnp.concatenate(
        [dot(act[0, own], down(q, 0)) + dot(act[1, own], down(q, 1)) for q in (0, 1)], axis=1
    )

    router_sig = jax.nn.sigmoid(jnp.sum(hidden * router, axis=-1, keepdims=True))
    mix = route_col * router_sig
    branch = attn + ffn
    state = hidden + mix * branch
    state_out[...] = tokens_out(sz, state)
    misfit = state - tokens_in(sz, teach_in)
    small_out[2:3] = jnp.sum(valid_col * misfit * misfit, axis=0, keepdims=True)
    d_state = 2.0 / (sz.width * tok_count) * valid_col * misfit
    d_branch = mix * d_state
    d_logit = (
        route_col
        * jnp.sum(d_state * branch, axis=-1, keepdims=True)
        * router_sig
        * (1.0 - router_sig)
    )
    small_out[1:2] = jnp.sum(d_logit * hidden, axis=0, keepdims=True)
    d_ffn = d_branch.astype(jnp.bfloat16)
    low, high = d_ffn[:, : sz.half], d_ffn[:, sz.half :]
    stage_d[...] = jnp.where(core == 0, high, low)
    x_dffn.start()
    dffn2[own] = jnp.where(core == 0, low, high)
    order.until("bwd")
    for turn in (1, 0):
        h = core if turn == 0 else 1 - core
        d_act = dot_nt(low, down(0, h)) + dot_nt(high, down(1, h))
        gate_pre, up_pre = gate_s[h], up_s[h]
        sig = jax.nn.sigmoid(gate_pre)
        d_gate = (d_act * up_pre * sig * (1.0 + gate_pre * (1.0 - sig))).astype(jnp.bfloat16)
        d_up = (d_act * (gate_pre * sig)).astype(jnp.bfloat16)
        if turn == 1:
            stage_h[0], stage_h[1] = d_gate, d_up
            x_dgate.start()
            x_dup.start()
        else:
            dgate2[own], dup2[own] = d_gate, d_up

    def until(mark):
        if fused:
            order.until(mark)

    def copied(tensor):
        for name in flows:
            if name[0] == tensor:
                flows[name].sent()

    shape, pd = (sz.side, sz.side), wd.at[0]
    until("pd")
    x_act.came()
    x_dffn.came()
    copied("d")
    for h in (0, 1):
        for i in range(two):
            part = sz.ffn_half // two
            pd[h * two + i] = (
                dot_tn(act[h, :, pl.ds(i * part, part)], dffn2[...])
                .astype(jnp.bfloat16)
                .reshape(shape + (sz.ffn_rows_p, sz.half))
            )
    until("bwdb")
    d_normed2 = jnp.zeros((t, wide), jnp.float32)
    for h, d_gate, d_up in (
        (1 - core, stage_h[0], stage_h[1]),
        (core, dgate2[own], dup2[own]),
    ):
        d_normed2 = (
            d_normed2
            + dot_nt(d_gate, wg[h].reshape(wide, sz.ffn_half))
            + dot_nt(d_up, wu[h].reshape(wide, sz.ffn_half))
        )
    x_n2.came()
    part = wide // sz.grid[0]
    for name, came, right, ref in (
        ("g", x_dgate, dgate2, wg.at[0]),
        ("u", x_dup, dup2, wu.at[0]),
    ):
        until("p" + name)
        came.came()
        copied(name)
        for i in range(sz.grid[0]):
            ref[i] = (
                dot_tn(normed2[:, pl.ds(i * part, part)], right[...])
                .astype(jnp.bfloat16)
                .reshape(shape + (sz.rows_p, sz.ffn_half))
            )
    until("bwdc")
    small_out[0:1] = jnp.sum(d_normed2 * residual * inv_second, axis=0, keepdims=True)
    scaled = gain_two * d_normed2
    d_mid = inv_second * scaled - residual * (
        inv_second**3 * (jnp.sum(scaled * residual, axis=-1, keepdims=True) / sz.width)
    )
    dhid_out[...] = d_state + d_logit * router + d_mid
    d_attn = narrow(sz, d_branch + d_mid)
    left = jnp.zeros((t, sz.skip), f32)
    right = jnp.zeros((t, sz.window - sz.skip - sz.out_cols), f32)
    low, high = (
        beside(left, value, right).astype(jnp.bfloat16)
        for value in (d_attn[:, : sz.out_cols], d_attn[:, sz.out_cols :])
    )
    stage_o[...] = jnp.where(core == 0, high, low)
    x_datt.start()
    datt2[own] = jnp.where(core == 0, low, high)
    d_ctx = dot_nt(low, lanes_of(wq, 0, sz.win, sz.window))
    d_ctx = narrow(sz, d_ctx + dot_nt(high, lanes_of(wq, 1, sz.win, sz.window)))
    for h in range(HEADS):
        st, sub = h // sz.step_heads, h % sz.step_heads
        dctx_out[st, pl.ds(sub * t, t)] = jnp.concatenate(
            [blank, d_ctx[:, h * HEAD_DIM : (h + 1) * HEAD_DIM]], axis=1
        ).astype(jnp.bfloat16)
    until("po")
    x_ctx.came()
    x_datt.came()
    for tensor in "oqk":
        copied(tensor)
    for cp in kept:
        cp.wait()
    kept = []
    out_lanes = pl.ds(sz.pack, sz.full - sz.pack)
    edge = sz.pack - sz.win
    for i in range(sz.grid[0]):
        grad = dot_tn(ctx2[:, pl.ds(i * part, part)], datt2[...]).astype(jnp.bfloat16)
        po6[i] = grad[:, :edge].reshape(shape + (sz.rows_p, edge))
        wq[0, i, :, :, :, out_lanes] = grad[:, edge:].reshape(
            shape + (sz.rows_p, sz.full - sz.pack)
        )
    for name, ref in (
        ("d", wd.at[0]),
        ("g", wg.at[0]),
        ("u", wu.at[0]),
        ("o", wq.at[0, :, :, :, :, out_lanes]),
    ):
        if name in keep:
            kept.append(link.bring(ref, keep[name]))
            kept[-1].start()
    for cp in kept:
        cp.wait()
    for cp in (x_n2, x_act, x_ctx, x_dffn, x_datt, x_dgate, x_dup):
        cp.sent()


def backward_part(
    sz, link,
    prob_in, heads, dctx, hid_in, dhid, small_in, cos_in, sin_in,
    po6,
    ghid_out, gq_out, gk_out, gv_out, go_out, gg_out, gu_out, gd_out, gain1_out, gain2_out,
    router_out, loss_out,
    wq, kv, prob, dq_h, normed2, dpack2, stage, small2, fused,
):
    place, order, local = link.place, link.order, link.local
    core = place.core
    t, wide = sz.tokens, sz.wide
    flows = link.back_flows
    own, other = pl.ds(0, t), pl.ds(t, t)
    x_n = link.to_peer(normed2.at[own], normed2.at[other])
    x_pack = link.to_peer(stage, dpack2.at[other])
    x_small = link.to_peer(small2.at[0], small2.at[1])
    x_err = link.to_peer(small2.at[2], small2.at[3])
    prob_sem = link.slot(2)
    part_rows = sz.step_rows // sz.row_parts

    def fetch(st, slot):
        rows = pl.ds(st % sz.row_parts * part_rows, part_rows)
        return pltpu.make_async_copy(
            prob_in.at[st // sz.row_parts, rows], prob.at[slot], local.at[prob_sem + slot]
        )

    fetch(0, 0).start()
    small2[2] = small_in[...]
    if not fused:
        place.greet()
    x_err.start()
    if not fused:
        for name in "dgu":
            order.until("p" + name)
            link.gets[name].wait()
        link.gets["k"].wait()
        link.gets["q"].wait()
        order.until("po")
        link.gets["o"].start()
        link.gets["o"].wait()

    def attend(i, total):
        st = i // sz.row_parts
        slot = i % 2
        fetch(i, slot).wait()

        if isinstance(i, int):
            if i + 1 < sz.steps:
                fetch(i + 1, 1 - slot).start()
        else:

            @pl.when(i + 1 < sz.steps * sz.row_parts)
            def _():
                fetch(i + 1, 1 - slot).start()

        first, row = st // sz.steps_per_kv * LANES, i % sz.row_parts * part_rows
        if not isinstance(i, int):
            first, row = pl.multiple_of(first, LANES), pl.multiple_of(row, part_rows)
        tile = kv[:, :, :, :, pl.ds(first, LANES)].reshape(sz.keys, LANES)
        rows = pl.ds(row, part_rows)
        p_low = prob[slot]
        p = p_low.astype(jnp.float32)
        d_w = dot_nt(dctx[st, rows], tile)
        terms = p * d_w
        delta = jnp.sum(terms, axis=-1, keepdims=True)
        d_s = (terms - p * delta).astype(jnp.bfloat16)
        dq_h[0](st, rows, dot(d_s, tile))
        more = dot_tn(heads[st, rows], d_s) + dot_tn(dctx[st, rows], p_low)
        return more if total is None else total + more

    for g in range(KV_HEADS):
        order.until("batt%s" % "abcde"[g])
        each = sz.steps_per_kv * sz.row_parts
        if each == 1:
            total = attend(g, None)
        else:
            total = jnp.zeros((LANES, sz.keys), jnp.float32)
            total = lax.fori_loop(g * each, (g + 1) * each, attend, total)
        kv[:, :, :, :, pl.ds(g * LANES, LANES)] = (
            total.astype(jnp.bfloat16).T.reshape(sz.grid + (t, LANES))
        )
    order.until("qs")

    wq_full = [lanes_of(wq, h, 0, sz.pack) for h in (0, 1)]
    gain_one = small_in[4:5]
    hidden = tokens_in(sz, hid_in)
    inv_first = lax.rsqrt(jnp.sum(hidden * hidden, axis=-1, keepdims=True) / sz.width + norm_eps)
    normed2[own] = (hidden * inv_first * gain_one).astype(jnp.bfloat16)
    x_n.start()
    cosine, sine = cos_in[...], sin_in[...]
    scale = HEAD_DIM ** (-0.5)
    dq = jnp.concatenate(
        [
            dq_h[1](h)
            for h in range(HEADS)
        ]
        + [jnp.zeros((t, HEAD_DIM), jnp.float32)],
        axis=1,
    ) * scale
    dq = dq * repeat_lanes(cosine, 8 * LANES) - swap_halves(dq) * repeat_lanes(sine, 8 * LANES)
    d_q = dq.astype(jnp.bfloat16).astype(jnp.float32)

    x_err.came()
    both_err = jnp.sum(small2[2][2:3] + small2[3][2:3], axis=-1, keepdims=True)
    link.err[place.pos[0], place.pos[1], place.pos[2]] = jnp.broadcast_to(both_err, (8, LANES))
    order.until("kq")
    d_kv = jnp.concatenate([flows["KC"].total(), flows["KD"].total()], axis=0)
    in_key = lax.rem(lane_index(d_kv.shape), LANES) < HEAD_DIM
    cos_kv = jnp.where(in_key, repeat_lanes(cosine, sz.kv_wide), 1.0)
    sin_kv = jnp.where(in_key, repeat_lanes(sine, sz.kv_wide), 0.0)
    d_kv = d_kv * cos_kv - swap_halves(d_kv) * sin_kv
    d_kv = d_kv.astype(jnp.bfloat16).astype(jnp.float32)
    d_k = jnp.concatenate(
        [d_kv[:, g * LANES : g * LANES + HEAD_DIM] for g in range(KV_HEADS)], axis=1
    )
    d_v = jnp.concatenate(
        [d_kv[:, g * LANES + HEAD_DIM : (g + 1) * LANES] for g in range(KV_HEADS)], axis=1
    )
    qc, kc = sz.q_cols, sz.k_cols
    blank = jnp.zeros((t, sz.pack - sz.cols), jnp.float32)
    d_pack = [
        jnp.concatenate(
            [
                d_q[:, h * qc : (h + 1) * qc],
                d_k[:, h * kc : (h + 1) * kc],
                d_v[:, h * kc : (h + 1) * kc],
                blank,
            ],
            axis=1,
        ).astype(jnp.bfloat16)
        for h in (0, 1)
    ]
    stage[...] = jnp.where(core == 0, d_pack[1], d_pack[0])
    x_pack.start()
    dpack2[own] = jnp.where(core == 0, d_pack[0], d_pack[1])
    d_normed = dot_nt(d_pack[0], wq_full[0]) + dot_nt(d_pack[1], wq_full[1])
    small2[0] = small_in[...]
    small2[0, 2:3] = jnp.sum(d_normed * hidden * inv_first, axis=0, keepdims=True)
    x_small.start()
    x_n.came()
    x_pack.came()
    x_small.came()
    rows = small2[0] + small2[1]
    part = wide // sz.grid[0]
    shape = (sz.side, sz.side)
    for i in range(sz.grid[0]):
        grad = dot_tn(normed2[:, pl.ds(i * part, part)], dpack2[...])
        for b in range(part // sz.rows_p):
            first = i * part + b * sz.rows_p
            line = jnp.concatenate(
                [jnp.zeros((1, sz.gain_lane), jnp.float32)]
                + [rows[r : r + 1, first : first + sz.rows] for r in (2, 0, 1)]
                + [jnp.zeros((1, sz.pack - sz.gain_lane - 3 * sz.rows), jnp.float32)],
                axis=1,
            )
            block = grad[b * sz.rows_p : (b + 1) * sz.rows_p]
            is_line = lax.broadcasted_iota(jnp.int32, block.shape, 0) == sz.rows
            block = jnp.where(is_line, line, block)
            spot = (i, b // sz.side, b % sz.side)
            edge = block[:, sz.win :] + po6[spot].astype(jnp.float32)
            block = jnp.concatenate([block[:, : sz.win], edge], axis=1).astype(jnp.bfloat16)
            wq[(0,) + spot + (slice(None), pl.ds(0, sz.pack))] = block
    order.until("gi")
    scaled = gain_one * d_normed
    d_hid = (
        dhid[...]
        + inv_first * scaled
        - hidden * (inv_first**3 * (jnp.sum(scaled * hidden, axis=-1, keepdims=True) / sz.width))
    )
    ghid_out[...] = tokens_out(sz, d_hid)
    order.until("fin")

    def whole(tensor):
        return jnp.concatenate(
            [flows[name].total() for name in flows if name[0] == tensor], axis=1
        )

    gd_out[...] = narrow(sz, whole("D"))[: sz.ffn_rows]
    gg_out[...] = blocks_cut(whole("G"), sz.ffn_rows, sz.ffn_rows_p)[: sz.rows]
    gu_out[...] = blocks_cut(whole("U"), sz.ffn_rows, sz.ffn_rows_p)[: sz.rows]
    grad = whole("Q")
    grad_out = jnp.concatenate([grad[:, sz.cols :], whole("O")], axis=1)
    go_out[...] = grad_out[: sz.rows, : sz.out_cols]
    gq_out[...] = grad[: sz.rows, :qc]
    gk_out[...] = grad[: sz.rows, qc : qc + kc]
    gv_out[...] = grad[: sz.rows, qc + kc : qc + 2 * kc]
    for r, ref in enumerate((gain1_out, gain2_out, router_out)):
        first = sz.gain_lane + r * sz.rows
        ref[...] = grad[sz.rows : sz.rows + 1, first : first + sz.rows]
    total = jnp.zeros((8, LANES), jnp.float32)
    for i, j, k in chips_of(sz):
        total = total + link.err[i, j, k]
    loss_out[...] = total / (sz.width * small_in[3:4, :LANES])
    for flow in flows.values():
        flow.sent()
    for cp in (x_n, x_pack, x_small, x_err):
        cp.sent()


FORWARD_INS = 13


def set_back_flows(sz, link, partial, kv, err, lands):
    link.err = err
    link.back_flows = backward_flows(sz, link.place, link.sems, partial, kv, err, lands)
    link.flows.update(link.back_flows)


def whole_kernel(sz, *refs):
    at = FORWARD_INS
    ins = refs[:at]
    state, ghid, gq, gk, gv, go, gg, gu, gd, gain1, gain2, router, loss, prob_hbm = refs[at : at + 14]
    refs = refs[at + 14 :]
    small, heads, dctx, cosine, sine, po6 = refs[:6]
    first, refs = refs[6 : 6 + 21], refs[6 + 21 :]
    normed2, dpack2, stage, small2, err, lands, send, recv, local = refs
    wq, wg, wu, wd, kv, bias, prob = first[:7]
    dhid, gates = bias.at[:, pl.ds(0, sz.wide)], first[10]
    per = sz.ffn_half // LANES

    def dq_put(st, rows, value):
        for sub in range(sz.step_heads):
            h = st * sz.step_heads + sub
            part = value[sub * sz.tokens : (sub + 1) * sz.tokens]
            gates[h // per, :, pl.ds(h % per * LANES, LANES)] = part

    def dq_get(h):
        return gates[h // per, :, pl.ds(h % per * LANES, LANES)][:, :HEAD_DIM]

    link = Link(sz, ORDER, send, recv, local)
    partial = {"q": wq, "o": wq, "g": wg, "u": wu, "d": wd}
    partial = {name: ref.at[0] for name, ref in partial.items()}
    set_back_flows(sz, link, partial, kv, err, lands)
    forward_part(
        sz, link, *ins, state, dhid, small, prob_hbm, heads, dctx, cosine, sine, po6, *first, {}, True
    )
    backward_part(
        sz, link, prob_hbm, heads, dctx, ins[11], dhid, small, cosine, sine, po6,
        ghid, gq, gk, gv, go, gg, gu, gd, gain1, gain2, router, loss,
        wq, kv, prob, (dq_put, dq_get), normed2, dpack2, stage, small2, True,
    )


def forward_kernel(sz, *refs):
    at = FORWARD_INS
    ins, refs = refs[:at], refs[at:]
    state, dhid, small, wq_out, kv_out, prob, heads, dctx, cosine, sine, po6 = refs[:11]
    keep = dict(zip("qkguod", (wq_out, kv_out) + refs[11:15]))
    first, (send, recv, local) = refs[15 : 15 + 21], refs[15 + 21 :]
    link = Link(sz, ORDER, send, recv, local)
    forward_part(
        sz, link, *ins, state, dhid, small, prob, heads, dctx, cosine, sine, po6, *first, keep, False
    )


def backward_kernel(sz, *refs):
    wq_in, kv_in, prob_in, heads, dctx, pg_in, pu_in, po_in, pd_in, *more = refs[:15]
    outs, refs = refs[15 : 15 + 12], refs[15 + 12 :]
    wq, kv, prob, dq_h, normed2, dpack2, stage, pg, pu, pd, small2, err, lands = refs[:13]
    send, recv, local = refs[13:]
    link = Link(sz, ORDER[ORDER.index("bwd") + 1 :], send, recv, local)

    def dq_put(st, rows, value):
        dq_h[st, rows] = value

    def dq_get(h):
        return dq_h[h // sz.step_heads, pl.ds(h % sz.step_heads * sz.tokens, sz.tokens), :HEAD_DIM]

    partial = {"q": wq.at[0], "o": wq.at[0], "g": pg, "u": pu, "d": pd}
    set_back_flows(sz, link, partial, kv, err, lands)
    po = wq.at[0, :, :, :, :, pl.ds(sz.pack, sz.full - sz.pack)]
    pairs = ((pd_in, pd), (pg_in, pg), (pu_in, pu), (po_in, po), (kv_in, kv), (wq_in, wq))
    link.gets = {name: link.bring(src, dst) for name, (src, dst) in zip("dguokq", pairs)}
    for name, cp in link.gets.items():
        if name != "o":
            cp.start()
    backward_part(
        sz, link, prob_in, heads, dctx, *more, *outs,
        wq, kv, prob, (dq_put, dq_get), normed2, dpack2, stage, small2, False,
    )


def count_copies(sz, flows_of, more):
    sems = Sems()
    tensors = dict.fromkeys("qogud")
    flows_of(sz, Place(sz.chips, True), sems, tensors)
    return sems.used + more


def deliver_kernel(*refs):
    half = len(refs) // 2
    for source, target in zip(refs[: half - 1], refs[half:-1]):
        target[...] = source[...]
    refs[-1][0, 0] = refs[half - 1][0, 0]


def body(chips, hidden_in, segment_ids, route_mask, valid_mask, teacher, norm_gain, w_query, w_key,
         w_value, w_out, ffn_gain, w_gate, w_up, w_down, router_weight):
    sz = Sizes(chips, hidden_in.shape, w_gate.shape, w_down.shape)
    t = sz.tokens
    gains = jnp.concatenate([norm_gain, ffn_gain, router_weight])[None]
    low, f32 = jnp.bfloat16, jnp.float32
    grid = sz.grid
    any_spec, vmem_spec = pl.BlockSpec(memory_space=pl.ANY), pl.BlockSpec(memory_space=pltpu.VMEM)
    shape = jax.ShapeDtypeStruct
    gate_shape = grid + (sz.rows_p, sz.ffn_half)
    out_shape = grid + (sz.rows_p, sz.full - sz.pack)
    edge_shape = grid + (sz.rows_p, sz.pack - sz.win)
    down_shape = grid + (sz.ffn_rows_p, sz.half)
    pack_shape = grid + (sz.rows_p, sz.full)
    kv_shape = grid + (t, sz.kv_wide)
    head_shape = (sz.steps, sz.step_rows, LANES)
    prob_shape = (sz.steps, sz.step_rows, sz.keys)
    copies_f = count_copies(sz, lambda *a: forward_flows(*a, None), 7)
    copies_b = count_copies(sz, lambda *a: backward_flows(*a, None, None, None), 4)
    first_scratch = [
        pltpu.VMEM((2,) + pack_shape, low),
        pltpu.VMEM((2,) + gate_shape, low),
        pltpu.VMEM((2,) + gate_shape, low),
        pltpu.VMEM((2,) + down_shape, low),
        pltpu.VMEM(kv_shape, low),
        pltpu.VMEM((t, sz.keys), sz.bias_type),
        pltpu.VMEM((sz.slots, sz.step_rows, sz.keys), low),
        pltpu.VMEM((t, sz.wide), f32),
        pltpu.VMEM((2 * t, sz.wide), low),
        pltpu.VMEM((2, 2 * t, sz.ffn_half), low),
        pltpu.VMEM((2, t, sz.ffn_half), f32),
        pltpu.VMEM((2, t, sz.ffn_half), f32),
        pltpu.VMEM((2 * t, sz.wide), low),
        pltpu.VMEM((2 * t, sz.window), low),
        pltpu.VMEM((2 * t, sz.half), low),
        pltpu.VMEM((2 * t, sz.ffn_half), low),
        pltpu.VMEM((2 * t, sz.ffn_half), low),
        pltpu.VMEM((t, sz.half), low),
        pltpu.VMEM((t, sz.window), low),
        pltpu.VMEM((2, t, sz.ffn_half), low),
        pltpu.VMEM((t, 8), f32),
    ]
    lands = []
    for name, tensor, first, span in pack_flows(sz) + weight_flows(sz):
        rows = sz.ffn_rows_p if tensor == "d" else sz.rows_p
        lands += land_shapes(grid, ORDERS[name[1].upper()], rows, span)
    for name, r0, rn, first, span in kv_flows(sz):
        lands += land_shapes(grid, ORDERS[name[1].upper()], rn, span)
    second_scratch = [
        pltpu.VMEM(head_shape, f32),
        pltpu.VMEM((2 * t, sz.wide), low),
        pltpu.VMEM((2 * t, sz.pack), low),
        pltpu.VMEM((t, sz.pack), low),
    ]
    last_scratch = [pltpu.VMEM((4, 8, sz.wide), f32), pltpu.VMEM(grid + (8, LANES), f32), lands]
    results = [
        shape((sz.width, t), low),
        shape((sz.rows, sz.q_cols), f32),
        shape((sz.rows, sz.k_cols), f32),
        shape((sz.rows, sz.k_cols), f32),
        shape((sz.rows, sz.width // 2), f32),
        shape((sz.rows, sz.ffn_cols), f32),
        shape((sz.rows, sz.ffn_cols), f32),
        shape((sz.ffn_rows, sz.width // 2), f32),
        shape((1, sz.rows), f32),
        shape((1, sz.rows), f32),
        shape((1, sz.rows), f32),
        shape((8, LANES), f32),
    ]
    ins = (
        w_query, w_key, w_value, w_out, w_gate, w_up, w_down, gains,
        segment_ids, route_mask, valid_mask, hidden_in[0].T, teacher[0].T,
    )
    state_shape, dhid_shape = shape((sz.width, t), low), shape((t, sz.wide), f32)
    small_shape, table_shape = shape((8, sz.wide), f32), shape((t, LANES), f32)

    def sem_scratch(copies):
        return [pltpu.SemaphoreType.DMA((count,)) for count in (copies, copies, 16)]

    def params(number):
        return pltpu.CompilerParams(
            collective_id=number, has_side_effects=True, vmem_limit_bytes=VMEM_LIMIT
        )

    if sz.keys <= 4096:
        outs = pl.pallas_call(
            functools.partial(whole_kernel, sz),
            out_shape=[state_shape] + results + [shape(prob_shape, low)],
            in_specs=[vmem_spec] * FORWARD_INS,
            out_specs=[vmem_spec] * 13 + [any_spec],
            scratch_shapes=[
                pltpu.VMEM(small_shape.shape, f32),
                pltpu.VMEM(head_shape, low),
                pltpu.VMEM(head_shape, low),
                pltpu.VMEM(table_shape.shape, f32),
                pltpu.VMEM(table_shape.shape, f32),
                pltpu.VMEM(edge_shape, low),
            ]
            + first_scratch
            + second_scratch[1:]
            + last_scratch
            + sem_scratch(copies_f + copies_b),
            compiler_params=params(0),
            name="whole",
        )(*ins)
        outs = outs[:-1]
    else:
        outs = pl.pallas_call(
            functools.partial(forward_kernel, sz),
            out_shape=[
                state_shape,
                dhid_shape,
                small_shape,
                shape((2,) + pack_shape, low),
                shape(kv_shape, low),
                shape(prob_shape, low),
                shape(head_shape, low),
                shape(head_shape, low),
                table_shape,
                table_shape,
                shape(edge_shape, low),
                shape(gate_shape, low),
                shape(gate_shape, low),
                shape(out_shape, low),
                shape(down_shape, low),
            ],
            in_specs=[vmem_spec] * FORWARD_INS,
            out_specs=[vmem_spec] * 3 + [any_spec] * 3 + [vmem_spec] * 5 + [any_spec] * 4,
            scratch_shapes=first_scratch + sem_scratch(copies_f),
            compiler_params=params(1),
            name="forward",
        )(*ins)
        state, dhid, small, wq_all, kv_all, prob, heads, dctx, cosine, sine, edge, pg, pu, po, pd = outs
        outs = pl.pallas_call(
            functools.partial(backward_kernel, sz),
            out_shape=results,
            in_specs=[any_spec] * 3 + [vmem_spec] * 2 + [any_spec] * 4 + [vmem_spec] * 6,
            out_specs=[vmem_spec] * 12,
            scratch_shapes=[
                pltpu.VMEM((2,) + pack_shape, low),
                pltpu.VMEM(kv_shape, low),
                pltpu.VMEM((2, sz.step_rows // sz.row_parts, sz.keys), low),
            ]
            + second_scratch
            + [
                pltpu.VMEM(gate_shape, low),
                pltpu.VMEM(gate_shape, low),
                pltpu.VMEM(down_shape, low),
            ]
            + last_scratch
            + sem_scratch(copies_b),
            compiler_params=params(2),
            name="backward",
        )(
            wq_all, kv_all, prob, heads, dctx, pg, pu, po, pd,
            ins[11], dhid, small, cosine, sine, edge,
        )
        outs = [state] + list(outs)
    last = len(outs) - 1
    state, ghid, gq, gk, gv, go, gg, gu, gd, gain1, gain2, router, loss = pl.pallas_call(
        deliver_kernel,
        out_shape=[shape(o.shape, o.dtype) for o in outs[:-1]] + [shape((1, 1), f32)],
        in_specs=[vmem_spec] * (last + 1),
        out_specs=[vmem_spec] * last + [pl.BlockSpec(memory_space=pltpu.SMEM)],
        name="deliver",
    )(*outs)
    return (
        state.T[None],
        loss.reshape(()),
        ghid.T[None],
        gain1.reshape(-1),
        gq,
        gk,
        gv,
        go,
        gain2.reshape(-1),
        gg,
        gu,
        gd,
        router.reshape(-1),
    )


def solution(mesh):
    tokens, rows, blocks = P("dp", "seq", None), P("dp", "seq"), P("seq", "dp")
    vector = P("seq")
    return jax.shard_map(
        functools.partial(body, mesh.shape["seq"]),
        mesh=mesh,
        in_specs=(
            tokens, rows, rows, rows, tokens, vector, blocks, blocks, blocks, blocks, vector,
            blocks, blocks, blocks, vector,
        ),
        out_specs=(
            tokens, P(), tokens, vector, blocks, blocks, blocks, blocks, vector, blocks, blocks,
            blocks, vector,
        ),
        check_vma=False,
    )
```
